32 devices in a mesh: batch: 4 (over y, x), head: 8 (over z, core).
Axes of the slice: x: 2, y: 2, z: 4, core: 2. Of those that a mesh axis runs over, the one named last changes fastest.
Arguments:
- tokens: bfloat16 [8, 1024, 2048], P('batch', 'head'), may hold values from -6 to 6
- segment_ids: int32 [8, 1024], P('batch'), may hold values from 0 to 3, as said below
- position_ids: int32 [8, 1024], P('batch'), may hold values from 0 to 1023, as said below
- w_query: bfloat16 [2048, 2048], P('batch', 'head'), may hold values from -0.125 to 0.125
- w_key: bfloat16 [2048, 2048], P('batch', 'head'), may hold values from -0.125 to 0.125
- w_value: bfloat16 [2048, 2048], P('batch', 'head'), may hold values from -0.125 to 0.125
- w_output: bfloat16 [2048, 2048], P('batch', 'head'), may hold values from -0.75 to 0.75
- w_gate: bfloat16 [2048, 8192], P('batch', 'head'), may hold values from -0.125 to 0.125
- w_up: bfloat16 [2048, 8192], P('batch', 'head'), may hold values from -0.125 to 0.125
- w_down: bfloat16 [2048, 8192], P('batch', 'head'), may hold values from -0.0625 to 0.0625
- attn_gain: bfloat16 [2048], P('batch'), may hold values from 0.099609375 to 1.8984375
- mlp_gain: bfloat16 [2048], P('batch'), may hold values from 0.099609375 to 1.8984375
- cotangent: bfloat16 [8, 1024, 2048], P('batch', 'head'), may hold values from -6 to 6
Outputs:
- layer_out: bfloat16 [8, 1024, 2048], P('batch', 'head')
- grad_input: float32 [8, 1024, 2048], P('batch', 'head')
- grad_query: float32 [2048, 2048], P('batch', 'head')
- grad_key: float32 [2048, 2048], P('batch', 'head')
- grad_value: float32 [2048, 2048], P('batch', 'head')
- grad_output: float32 [2048, 2048], P('batch', 'head')
- grad_gate: float32 [2048, 8192], P('batch', 'head')
- grad_up: float32 [2048, 8192], P('batch', 'head')
- grad_down: float32 [2048, 8192], P('batch', 'head')
- grad_attn_gain: float32 [2048], P('batch')
- grad_mlp_gain: float32 [2048], P('batch')
The draws below stay inside these ranges and needn't reach their ends.
Inputs may be any that keep to these rules, and one draw needn't show every extreme that they name: `segment_ids`: within a row the ids start at 0, rise by one at each document's first token and never fall. In every aligned block of 2 rows, one row (which one is drawn from the seed) is a single document of all 1024 tokens, and the next row in the block (cyclically) is cut into documents of exactly 256 tokens; in all other rows documents have 256 to 512 tokens except the last of a row, which may be shorter. `position_ids`: the token's index counted from its document's first token.
All inputs are finite; a program needn't handle non-finite values.
Results may differ from the reference program's by a relative error of at most 0.02.
Values may be sent and summed in bfloat16 or wider, within the bound.
A program may use at most 184 MiB of HBM per device.

```python
import jax
import jax.numpy as jnp
from jax import lax

D = 2048
HEADS = 32
HEAD_DIM = 64
FF = 8192
ROW_LEN = 1024
DOC_MIN = 256
DOC_MAX = 512
ROWS_DEV = 2
ROWS = 8


def documents(key):
    slot_count = ROW_LEN // DOC_MIN + 1
    groups = ROWS // ROWS_DEV
    whole_row = jax.random.randint(jax.random.fold_in(key, 12), (groups,), 0, ROWS_DEV).astype(jnp.int32)
    row_in_group = (jnp.arange(ROWS).astype(jnp.int32) % ROWS_DEV).astype(jnp.int32)
    chosen = row_in_group == jnp.repeat(whole_row, ROWS_DEV)
    shortest = row_in_group == jnp.repeat((whole_row + 1) % ROWS_DEV, ROWS_DEV)
    lengths = jax.random.randint(jax.random.fold_in(key, 11), (ROWS, slot_count), DOC_MIN, DOC_MAX + 1).astype(jnp.int32)
    lengths = jnp.where(shortest[:, None], DOC_MIN, lengths).astype(jnp.int32)
    bounds = jnp.cumsum(lengths, axis=1).astype(jnp.int32)
    token_index = jnp.arange(ROW_LEN).astype(jnp.int32)
    past_bound = token_index[None, :, None] >= bounds[:, None, :]
    segments = jnp.sum(past_bound.astype(jnp.int32), axis=2).astype(jnp.int32)
    starts = jnp.max(jnp.where(past_bound, bounds[:, None, :], 0), axis=2).astype(jnp.int32)
    positions = token_index[None, :] - starts
    segments = jnp.where(chosen[:, None], 0, segments).astype(jnp.int32)
    positions = jnp.where(chosen[:, None], token_index[None, :], positions).astype(jnp.int32)
    return (segments, positions)


def draw_segment_ids(key, part):
    shared = documents(key)
    return shared[0]


def draw_position_ids(key, part):
    shared = documents(key)
    return shared[1]


def block_levels(stream_key, dims, pieces, smallest, high):
    def one(dim, blocks):
        steps = jax.random.uniform(jax.random.fold_in(jax.random.fold_in(stream_key, 6), dim), (blocks,), jnp.float32, smallest / len(pieces), high / len(pieces))
        return jnp.repeat(jnp.exp(steps), dims[dim] // blocks).reshape((-1,) + (1,) * (len(dims) - dim - 1))

    factor_of = one(*pieces[0])
    for cut in pieces[1:]:
        factor_of = factor_of * one(*cut)
    return factor_of


def noise(rng, shape, deviation, reach, shards=(), dtype=jnp.bfloat16):
    loudness = block_levels(rng, shape, shards, -0.22, 0.18) if shards else 1.0
    values = jax.random.normal(rng, shape, jnp.float32) * deviation * loudness
    return jnp.minimum(jnp.maximum(values, -reach), reach).astype(dtype)


def setup_inputs(seed: int = 0) -> dict:
    keys = jax.random.split(jax.random.key(seed), 14)
    return {
        "tokens": noise(keys[0], (ROWS, ROW_LEN, D), 1.0, 6.0, ((0, 4), (1, 8))),
        "segment_ids": draw_segment_ids(jax.random.fold_in(keys[13], 71), 0),
        "position_ids": draw_position_ids(jax.random.fold_in(keys[13], 71), 0),
        "w_query": noise(keys[3], (D, D), D ** -0.5, 0.125, ((0, 4), (1, 8))),
        "w_key": noise(keys[4], (D, D), D ** -0.5, 0.125, ((0, 4), (1, 8))),
        "w_value": noise(keys[5], (D, D), D ** -0.5, 0.125, ((0, 4), (1, 8))),
        "w_output": noise(keys[6], (D, D), (D // 32) ** -0.5, 0.75, ((0, 4), (1, 8))),
        "w_gate": noise(keys[7], (D, FF), D ** -0.5, 0.125, ((0, 4), (1, 8))),
        "w_up": noise(keys[8], (D, FF), D ** -0.5, 0.125, ((0, 4), (1, 8))),
        "w_down": noise(keys[9], (D, FF), FF ** -0.5, 0.0625, ((0, 4), (1, 8))),
        "attn_gain": jnp.clip(1.0 + 0.18 * jax.random.normal(keys[10], (D,), jnp.float32), 0.099609375, 1.8984375).astype(jnp.bfloat16),
        "mlp_gain": jnp.clip(1.0 + 0.18 * jax.random.normal(keys[11], (D,), jnp.float32), 0.099609375, 1.8984375).astype(jnp.bfloat16),
        "cotangent": noise(keys[12], (ROWS, ROW_LEN, D), 1.0, 6.0, ((0, 4), (1, 8))),
    }


@jax.custom_vjp
def low(v):
    return lax.optimization_barrier(v.astype(jnp.bfloat16)).astype(jnp.float32)

@jax.custom_vjp
def low_back(v):
    return v

def low_keep(v):
    return (low(v), None)

def low_pass(kept, grad):
    return (grad,)

def back_keep(v):
    return (v, None)

def back_low(kept, grad):
    return (low(grad),)
low.defvjp(low_keep, low_pass)
low_back.defvjp(back_keep, back_low)
epsilon = 1e-05
rope_base = 130000.0
masked_value = -1000000000.0

def normed(values, gain):
    inv_root = lax.rsqrt(lax.optimization_barrier(jnp.mean(values * values, axis=-1, keepdims=True)) + epsilon)
    return values * inv_root * gain

def rope_tables(positions):
    half_dim = HEAD_DIM // 2
    frequency = rope_base ** (-(jnp.arange(half_dim).astype(jnp.float32) * 2.0) / HEAD_DIM)
    angles = positions.astype(jnp.float32)[:, None] * frequency[None, :]
    return (jnp.cos(angles)[:, None, :], jnp.sin(angles)[:, None, :])

def rotate(values, cosine, sine):
    half_dim = values.shape[-1] // 2
    first_half = values[..., :half_dim]
    second = values[..., half_dim:]
    return jnp.concatenate([first_half * cosine - second * sine, second * cosine + first_half * sine], axis=-1)

def product(left, right):
    return jnp.dot(left, right, precision=lax.Precision.HIGHEST)

def attend(query, key_rot, values, segments):
    length = query.shape[0]
    scores = jnp.einsum('qhd,khd->hqk', query, key_rot, precision=lax.Precision.HIGHEST) * HEAD_DIM ** (-0.5)
    scores = low_back(scores)
    token_index = jnp.arange(length)
    allowed = (segments[:, None] == segments[None, :]) & (token_index[None, :] <= token_index[:, None])
    masked = jnp.where(allowed[None, :, :], scores, masked_value)
    row_max = lax.optimization_barrier(jnp.max(masked, axis=-1, keepdims=True))
    weights_exp = jnp.exp(masked - row_max)
    probabilities = low(weights_exp / lax.optimization_barrier(jnp.sum(weights_exp, axis=-1, keepdims=True)))
    return jnp.einsum('hqk,khd->qhd', probabilities, values, precision=lax.Precision.HIGHEST)

def layer(inputs, params, segments, positions):
    w_query, w_key, w_value, w_output, w_gate, w_up, w_down, attn_gain, mlp_gain = params
    length = inputs.shape[0]
    head_shape = (length, HEADS, HEAD_DIM)
    cosine, sine = rope_tables(positions)
    attn_in = low(normed(inputs, attn_gain))
    query = low(rotate(low_back(product(attn_in, w_query)).reshape(head_shape), cosine, sine))
    key_rot = low(rotate(low_back(product(attn_in, w_key)).reshape(head_shape), cosine, sine))
    values = low(low_back(product(attn_in, w_value))).reshape(head_shape)
    attended = jax.checkpoint(attend)(query, key_rot, values, segments).reshape(length, D)
    attended = low(low_back(attended))
    mixed = inputs + low_back(product(attended, w_output.T))
    mlp_in = low(normed(mixed, mlp_gain))
    gate_act = low_back(product(mlp_in, w_gate))
    up_act = low_back(product(mlp_in, w_up))
    hidden = low(jax.nn.silu(gate_act) * up_act)
    return mixed + low_back(product(hidden, w_down.T))

def reference(tokens, segment_ids, position_ids, w_query, w_key, w_value, w_output, w_gate, w_up, w_down, attn_gain, mlp_gain, cotangent):
    params = tuple((weight.astype(jnp.float32) for weight in (w_query, w_key, w_value, w_output, w_gate, w_up, w_down, attn_gain, mlp_gain)))

    def one_row(totals, row_data):
        inputs, segments, positions, grad_row = row_data

        def forward(values, weights):
            return layer(values, weights, segments, positions)
        result, pull_back = jax.vjp(forward, inputs.astype(jnp.float32), params)
        input_grad, param_grads = pull_back(grad_row.astype(jnp.float32))
        totals = jax.tree.map(jnp.add, totals, param_grads)
        return (totals, (result.astype(jnp.bfloat16), input_grad))
    zeros = tuple((jnp.zeros_like(weight) for weight in params))
    totals, (layer_out, grad_input) = lax.scan(one_row, zeros, (tokens, segment_ids, position_ids, cotangent))
    return (layer_out, grad_input, totals[0], totals[1], totals[2], totals[3], totals[4], totals[5], totals[6], totals[7], totals[8])
```

```python
import functools

import jax
import jax.numpy as jnp
from jax import lax
from jax.experimental import pallas as pl
from jax.experimental.pallas import tpu as pltpu
from jax.sharding import PartitionSpec as P

HEAD_DIM = 64
epsilon = 1e-05
rope_base = 130000.0
masked_value = -1000000000.0
MESH = pl.DeviceIdType.MESH
F32 = jnp.float32
BF16 = jnp.bfloat16
DMA = pltpu.SemaphoreType.DMA
ANY = pl.BlockSpec(memory_space=pl.ANY)
VMEM = pl.BlockSpec(memory_space=pltpu.VMEM)
VMEM_LIMIT = 60 * 2**20


class Place:
    def __init__(self, batch, head):
        self.n, self.H = batch, head
        self.L = head // 2
        self.b = lax.axis_index("batch")
        self.h = lax.axis_index("head")
        self.z = self.h // 2
        self.c = self.h % 2
        self.sib = self.z * 2 + (1 - self.c)
        self.up = self.h + 2
        self.down = self.h - 2
        self.x, self.y = self.b % 2, self.b // 2
        self.xn = self.y * 2 + (1 - self.x)
        self.yn = (1 - self.y) * 2 + self.x
        self.dg = (1 - self.y) * 2 + (1 - self.x)
        self.square = batch == 4

    def greet(self, line=True, batch=True, all_heads=False):
        barrier = pltpu.get_barrier_semaphore()
        me, L = self, self.L

        def hello(device):
            pl.semaphore_signal(barrier, inc=1, device_id=device, device_id_type=MESH)

        count = 0
        if all_heads:
            for off in range(1, self.H):
                hello({"head": (me.h + off) % self.H})
                count += 1
        elif line:
            hello({"head": me.sib})
            count += 1

            @pl.when(me.z > 0)
            def _():
                hello({"head": me.down})

            @pl.when(me.z < L - 1)
            def _():
                hello({"head": me.up})

        if batch:
            if self.square and not all_heads:
                hello({"batch": me.xn})
                hello({"batch": me.yn})
                count += 2
            else:
                for off in range(1, self.n):
                    hello({"batch": (me.b + off) % self.n})
                    count += 1
        if line and not all_heads:
            count = count + jnp.minimum(me.z, 1) + jnp.minimum(L - 1 - me.z, 1)
        pl.semaphore_wait(barrier, count)


def remote(src, dst, ssem, rsem, device):
    return pltpu.make_async_remote_copy(
        src_ref=src, dst_ref=dst, send_sem=ssem, recv_sem=rsem, device_id=device, device_id_type=MESH
    )


class Gather:
    def __init__(self, at, own, out, sems):
        self.at, self.own, self.out = at, own, out
        self.line_recv, self.sib_recv, self.up_send, self.down_send, self.sib_send, self.local = sems

    @staticmethod
    def sems(at_L):
        return [DMA((at_L,))] * 5 + [DMA]

    def _up(self, zb, src):
        at = self.at
        return remote(src, self.out.at[zb * 2 + at.c], self.up_send.at[zb], self.line_recv.at[zb], {"head": at.up})

    def _down(self, zb, src):
        at = self.at
        return remote(src, self.out.at[zb * 2 + at.c], self.down_send.at[zb], self.line_recv.at[zb], {"head": at.down})

    def _sib(self, zb, src):
        at = self.at
        return remote(src, self.out.at[zb * 2 + at.c], self.sib_send.at[zb], self.sib_recv.at[zb], {"head": at.sib})

    def _mine(self):
        return pltpu.make_async_copy(self.own, self.out.at[self.at.h], self.local)

    def start(self):
        at = self.at

        @pl.when(at.z < at.L - 1)
        def _():
            self._up(at.z, self.own).start()

        @pl.when(at.z > 0)
        def _():
            self._down(at.z, self.own).start()

        self._sib(at.z, self.own).start()
        self._mine().start()

    def step(self, k):
        at = self.at
        below, above = at.z - k, at.z + k

        @pl.when(below >= 0)
        def _():
            block = self.out.at[below * 2 + at.c]
            self._up(below, block).wait_recv()

            @pl.when(at.z < at.L - 1)
            def _():
                self._up(below, block).start()

            self._sib(below, block).start()

        @pl.when(above <= at.L - 1)
        def _():
            block = self.out.at[above * 2 + at.c]
            self._down(above, block).wait_recv()

            @pl.when(at.z > 0)
            def _():
                self._down(above, block).start()

            self._sib(above, block).start()

    def finish(self):
        at = self.at
        self._mine().wait()
        for zb in range(at.L):
            block = self.out.at[zb * 2 + at.c]
            self._sib(zb, block).wait_send()
            other = self.out.at[zb * 2 + 1 - at.c]
            remote(other, other, self.sib_send.at[zb], self.sib_recv.at[zb], {"head": at.sib}).wait_recv()

            @pl.when((zb <= at.z) & (at.z < at.L - 1))
            def _():
                self._up(zb, block).wait_send()

            @pl.when((zb >= at.z) & (at.z > 0))
            def _():
                self._down(zb, block).wait_send()


class Reduce:
    def __init__(self, at, src, own, sib, recv, sems):
        self.at, self.src, self.own, self.sib, self.recv = at, src, own, sib, recv
        self.load, self.sib_send, self.sib_recv, self.fwd_send, self.recv_sem = sems

    @staticmethod
    def sems(L):
        return [DMA((L,)), DMA((L,)), DMA((L,)), DMA((L,)), DMA((L + 1,))]

    @staticmethod
    def bufs(L, T, D):
        return [pltpu.VMEM((L, T, D), BF16), pltpu.VMEM((L, T, D), BF16), pltpu.VMEM((L + 1, T, D), BF16)]

    def _load(self, zd):
        return pltpu.make_async_copy(self.src.at[zd * 2 + self.at.c], self.own.at[zd], self.load.at[zd])

    def _sib(self, zd):
        at = self.at
        return remote(
            self.src.at[zd * 2 + 1 - at.c], self.sib.at[zd], self.sib_send.at[zd], self.sib_recv.at[zd], {"head": at.sib}
        )

    def _fwd(self, zd, slot, device):
        return remote(self.recv.at[zd], self.recv.at[slot], self.fwd_send.at[zd], self.recv_sem.at[slot], {"head": device})

    def start(self):
        at, L = self.at, self.at.L
        order = []
        for k in range((L + 1) // 2):
            order += [L - 1 - k] + ([k] if k != L - 1 - k else [])
        for zd in order:
            self._sib(zd).start()
            self._load(zd).start()

    def _chunks(self, fn):
        T = self.own.shape[1]
        step = 32 if T % 32 == 0 else T

        @pl.loop(0, T // step)
        def _(i):
            fn(pl.ds(pl.multiple_of(i * step, step), step))

    def _hop(self, zd, first, slot, device, which):
        @pl.when(first)
        def _():
            if which in ("first", "both"):
                self._load(zd).wait()
                self._sib(zd).wait_recv()

                def add(rows):
                    self.recv[zd, rows, :] = (self.own[zd, rows, :].astype(F32) + self.sib[zd, rows, :].astype(F32)).astype(
                        BF16
                    )

                self._chunks(add)
                self._fwd(zd, slot, device).start()

        @pl.when(jnp.logical_not(first))
        def _():
            if which in ("mid", "both"):
                self._load(zd).wait()
                self._sib(zd).wait_recv()
                self._fwd(zd, zd, device).wait_recv()

                def add(rows):
                    self.recv[zd, rows, :] = (
                        self.own[zd, rows, :].astype(F32)
                        + self.sib[zd, rows, :].astype(F32)
                        + self.recv[zd, rows, :].astype(F32)
                    ).astype(BF16)

                self._chunks(add)
                self._fwd(zd, slot, device).start()

    def hops(self, k, which="both"):
        at, L = self.at, self.at.L
        far, near = L - 1 - k, k

        @pl.when(far > at.z)
        def _():
            self._hop(far, at.z == 0, far, at.up, which)

        @pl.when(near < at.z)
        def _():
            self._hop(near, at.z == L - 1, jnp.where(at.z - 1 == near, L, near), at.down, which)

    def final(self, add):
        at, L = self.at, self.at.L
        z = at.z
        self._load(z).wait()
        self._sib(z).wait_recv()

        @pl.when(z > 0)
        def _():
            self._fwd(z, z, at.up).wait_recv()

        @pl.when(z < L - 1)
        def _():
            self._fwd(z, L, at.down).wait_recv()

        def base(rows):
            return self.own[z, rows, :].astype(F32) + self.sib[z, rows, :].astype(F32)

        @pl.when(z == 0)
        def _():
            self._chunks(lambda rows: add(rows, base(rows) + self.recv[L, rows, :].astype(F32)))

        @pl.when(z == L - 1)
        def _():
            self._chunks(lambda rows: add(rows, base(rows) + self.recv[z, rows, :].astype(F32)))

        @pl.when((z > 0) & (z < L - 1))
        def _():
            self._chunks(
                lambda rows: add(
                    rows, base(rows) + self.recv[z, rows, :].astype(F32) + self.recv[L, rows, :].astype(F32)
                )
            )

    def finish(self):
        at = self.at
        for zd in range(at.L):
            self._sib(zd).wait_send()

            @pl.when(zd != at.z)
            def _():
                self._fwd(zd, zd, at.up).wait_send()


class BatchGather:
    def __init__(self, at, own, out, sems):
        self.at, self.own, self.out = at, own, out
        self.send, self.recv, self.local = sems

    @staticmethod
    def sems(n):
        m = 4 if n == 4 else n
        return [DMA((m,)), DMA((m,)), DMA]

    def _half(self, b, i):
        half = self.own.shape[0] // 2
        return self.out(b, pl.ds(i * half, half))

    def _all(self, b):
        return self.out(b, pl.ds(0, self.own.shape[0]))

    def _direct(self, i, device):
        at = self.at
        return remote(self.own, self._all(at.b), self.send.at[i], self.recv.at[i], {"batch": device})

    def start(self):
        at = self.at
        pltpu.make_async_copy(self.own, self._all(at.b), self.local).start()
        if at.square:
            self._direct(0, at.xn).start()
            self._direct(1, at.yn).start()
        else:
            for off in range(1, at.n):
                remote(
                    self.own, self._all(at.b), self.send.at[off], self.recv.at[off], {"batch": (at.b + off) % at.n}
                ).start()

    def forward(self):
        at = self.at
        if at.square:
            block = self._all(at.xn)
            remote(block, block, self.send.at[0], self.recv.at[0], {"batch": at.xn}).wait_recv()
            half = self._half(at.xn, 0)
            remote(half, half, self.send.at[2], self.recv.at[2], {"batch": at.yn}).start()
            block = self._all(at.yn)
            remote(block, block, self.send.at[1], self.recv.at[1], {"batch": at.yn}).wait_recv()
            half = self._half(at.yn, 1)
            remote(half, half, self.send.at[3], self.recv.at[3], {"batch": at.xn}).start()

    def finish(self):
        at = self.at
        pltpu.make_async_copy(self.own, self._all(at.b), self.local).wait()
        if at.square:
            self._direct(0, at.xn).wait_send()
            self._direct(1, at.yn).wait_send()
            half = self._half(at.dg, 0)
            remote(half, half, self.send.at[2], self.recv.at[2], {"batch": at.yn}).wait()
            half = self._half(at.dg, 1)
            remote(half, half, self.send.at[3], self.recv.at[3], {"batch": at.xn}).wait()
        else:
            for off in range(1, at.n):
                block = self._all((at.b + at.n - off) % at.n)
                remote(block, block, self.send.at[off], self.recv.at[off], {"batch": (at.b + off) % at.n}).wait()


class BatchReduce:
    def __init__(self, at, src, bufs, sems, before=None):
        self.at, self.src, self.before = at, src, before
        if at.square:
            self.first, self.mine, self.second = bufs
        else:
            (self.slots,) = bufs
        self.send, self.recv, self.load = sems

    @staticmethod
    def sems(n):
        m = 6 if n == 4 else n
        return [DMA((m,)), DMA((m,)), DMA((4,))]

    @staticmethod
    def bufs(n, R, K):
        if n == 4:
            return [
                pltpu.VMEM((4, R // 2, K), BF16),
                pltpu.VMEM((4, R // 2, K), BF16),
                pltpu.VMEM((2, R // 2, K), BF16),
            ]
        return [pltpu.VMEM((n, R, K), BF16)]

    def _first(self, i):
        at, half = self.at, self.src.shape[1] // 2
        if i < 2:
            src = self.src.at[i * 2 + 1 - at.x, pl.ds(0, half), :]
            device = {"batch": at.xn}
        else:
            src = self.src.at[(1 - at.y) * 2 + i - 2, pl.ds(half, half), :]
            device = {"batch": at.yn}
        return remote(src, self.first.at[i], self.send.at[i], self.recv.at[i], device)

    def _taken(self, i):
        if self.before is None:
            return self._first(i)
        return pltpu.make_async_copy(self.before.at[i], self.first.at[i], self.recv.at[i])

    def _load(self, i):
        at, half = self.at, self.src.shape[1] // 2
        if i < 2:
            src = self.src.at[i * 2 + at.x, pl.ds(0, half), :]
        else:
            src = self.src.at[at.y * 2 + i - 2, pl.ds(half, half), :]
        return pltpu.make_async_copy(src, self.mine.at[i], self.load.at[i])

    def _second(self, j):
        at = self.at
        if j == 0:
            return remote(
                self.mine.at[1 - at.y], self.second.at[0], self.send.at[4], self.recv.at[4], {"batch": at.yn}
            )
        return remote(self.mine.at[3 - at.x], self.second.at[1], self.send.at[5], self.recv.at[5], {"batch": at.xn})

    def _direct(self, off):
        at = self.at
        to = (at.b + off) % at.n
        return remote(self.src.at[to], self.slots.at[off], self.send.at[off], self.recv.at[off], {"batch": to})

    def start(self):
        at = self.at
        if at.square:
            for i in (0, 2, 1, 3):
                self._taken(i).start()
                self._load(i).start()
        else:
            for off in range(1, at.n):
                self._direct(off).start()
            pltpu.make_async_copy(self.src.at[at.b], self.slots.at[0], self.load.at[0]).start()

    def _chunks(self, R, fn):
        step = 16

        @pl.loop(0, R // step)
        def _(i):
            fn(pl.multiple_of(i * step, step), step)

    def second_step(self):
        at = self.at
        if at.square:
            for i in range(4):
                self._load(i).wait()
                if self.before is None:
                    self._first(i).wait_recv()
                else:
                    self._taken(i).wait()
            for j, i in ((0, 1 - at.y), (1, 3 - at.x)):

                def add(r, step, i=i):
                    rows = pl.ds(r, step)
                    self.mine[i, rows, :] = (
                        self.mine[i, rows, :].astype(F32) + self.first[i, rows, :].astype(F32)
                    ).astype(BF16)

                self._chunks(self.mine.shape[1], add)
                self._second(j).start()

    def final(self, put):
        at = self.at
        if at.square:
            half = self.src.shape[1] // 2
            for j, i in ((0, at.y), (1, 2 + at.x)):
                self._second(j).wait_recv()

                def add(r, step, i=i, j=j):
                    rows = pl.ds(r, step)
                    put(
                        pl.ds(r + j * half, step),
                        self.mine[i, rows, :].astype(F32)
                        + self.first[i, rows, :].astype(F32)
                        + self.second[j, rows, :].astype(F32),
                    )

                self._chunks(half, add)
        else:
            pltpu.make_async_copy(self.src.at[at.b], self.slots.at[0], self.load.at[0]).wait()
            for off in range(1, at.n):
                self._direct(off).wait_recv()

            def add(r, step):
                rows = pl.ds(r, step)
                total = self.slots[0, rows, :].astype(F32)
                for off in range(1, at.n):
                    total = total + self.slots[off, rows, :].astype(F32)
                put(rows, total)

            self._chunks(self.src.shape[1], add)

    def finish(self):
        at = self.at
        if at.square:
            for i in range(4 if self.before is None else 0):
                self._first(i).wait_send()
            self._second(0).wait_send()
            self._second(1).wait_send()
        else:
            for off in range(1, at.n):
                self._direct(off).wait_send()


class Names:
    def __init__(self):
        self.shapes = []

    def add(self, shapes):
        start = len(self.shapes)
        self.shapes += list(shapes)
        return slice(start, len(self.shapes))


def chunk_loop(rows, step, fn):
    step = min(step, rows)

    @pl.loop(0, rows // step)
    def _(i):
        fn(pl.ds(pl.multiple_of(i * step, step), step))


def inv_root_of(values):
    return lax.rsqrt(jnp.mean(values * values, axis=-1, keepdims=True) + epsilon)


def gather_all(n, H, tokens, cotangent, gains, weights):
    rows, T, D = tokens.shape
    R = weights[0].shape[0]
    hw, ff = weights[0].shape[1], weights[4].shape[1]
    L = H // 2
    names = Names()
    normed_at = names.add([pltpu.VMEM((rows, T, D), BF16)])
    z_at = [names.add(Gather.sems(L)) for _ in range(2 * rows)]
    w_at = [names.add(BatchGather.sems(n)) for _ in range(7)]
    g_at = names.add([DMA((n,)), DMA((n,)), DMA])

    def kernel(tok, ct, gain, wq, wk, wv, wo, wg, wu, wd, attn_in, ct_full, w_qkv, w_o, w_gu, w_d, gains_full, *scratch):
        at = Place(n, H)
        (normed,) = scratch[normed_at]
        at.greet()
        gsend, grecv, glocal = scratch[g_at]

        def gain_dst(b):
            return gains_full.at[:, pl.ds(pl.multiple_of(b * R, R), R)]

        gain_jobs = []
        if at.square:
            first = remote(gain, gain_dst(at.b), gsend.at[0], grecv.at[0], {"batch": at.xn})
            own_y = remote(gain, gain_dst(at.b), gsend.at[1], grecv.at[1], {"batch": at.yn})
            first.start()
            own_y.start()
        else:
            for o in range(1, n):
                job = remote(gain, gain_dst(at.b), gsend.at[o], grecv.at[o], {"batch": (at.b + o) % n})
                job.start()
                gain_jobs.append(job)
        mine = pltpu.make_async_copy(gain, gain_dst(at.b), glocal)
        mine.start()

        ct_jobs = [Gather(at, ct.at[r], ct_full.at[r], scratch[z_at[rows + r]]) for r in range(rows)]
        in_jobs = [Gather(at, normed.at[r], attn_in.at[r], scratch[z_at[r]]) for r in range(rows)]
        outs = []
        for src, dst, col, width in (
            (wq, w_qkv, 0, hw),
            (wk, w_qkv, hw, hw),
            (wv, w_qkv, 2 * hw, hw),
            (wo, w_o, 0, hw),
            (wg, w_gu, 0, ff),
            (wu, w_gu, ff, ff),
            (wd, w_d, 0, ff),
        ):
            outs.append((src, lambda b, rr, dst=dst, col=col, width=width: dst.at[b, rr, pl.ds(col, width)]))
        w_jobs = [BatchGather(at, src, out, scratch[w_at[i]]) for i, (src, out) in enumerate(outs)]
        ct_jobs[0].start()
        mine.wait()
        if at.square:
            got = gain_dst(at.xn)
            remote(got, got, gsend.at[0], grecv.at[0], {"batch": at.xn}).wait_recv()
            fwd = remote(got, got, gsend.at[2], grecv.at[2], {"batch": at.yn})
            fwd.start()
            got = gain_dst(at.yn)
            remote(got, got, gsend.at[1], grecv.at[1], {"batch": at.yn}).wait_recv()
            got = gain_dst(at.dg)
            remote(got, got, gsend.at[2], grecv.at[2], {"batch": at.yn}).wait_recv()
            first.wait_send()
            own_y.wait_send()
            fwd.wait_send()
        else:
            for o in range(1, n):
                got = gain_dst((at.b + n - o) % n)
                remote(got, got, gsend.at[o], grecv.at[o], {"batch": (at.b + o) % n}).wait_recv()
                gain_jobs[o - 1].wait_send()

        for job in w_jobs:
            job.start()
        for r in range(rows):

            def norm(part, r=r):
                values = tok[r, part, :].astype(F32)
                normed[r, part, :] = (values * inv_root_of(values) * gains_full[0:1, :]).astype(BF16)

            chunk_loop(T, 32, norm)
            in_jobs[r].start()
        for job in ct_jobs[1:]:
            job.start()
        order = [ct_jobs[0]] + in_jobs + ct_jobs[1:]
        for k in range(1, L):
            for job in order:
                job.step(k)
            for job in {1: w_jobs[:4], 2: w_jobs[4:]}.get(k, ()):
                job.forward()
        for job in order + w_jobs:
            job.finish()

    return pl.pallas_call(
        kernel,
        out_shape=(
            jax.ShapeDtypeStruct((rows, H, T, D), BF16),
            jax.ShapeDtypeStruct((rows, H, T, D), BF16),
            jax.ShapeDtypeStruct((n, R, 3 * hw), BF16),
            jax.ShapeDtypeStruct((n, R, hw), BF16),
            jax.ShapeDtypeStruct((n, R, 2 * ff), BF16),
            jax.ShapeDtypeStruct((n, R, ff), BF16),
            jax.ShapeDtypeStruct((8, D), F32),
        ),
        in_specs=[VMEM, ANY, VMEM] + [ANY] * 7,
        out_specs=(ANY,) * 6 + (VMEM,),
        scratch_shapes=names.shapes,
        compiler_params=pltpu.CompilerParams(collective_id=1, has_side_effects=True, vmem_limit_bytes=VMEM_LIMIT),
        name="gather_all",
    )(tokens, cotangent, gains, *weights)


def far_first(L, z):
    return sorted(range(L), key=lambda zd: (-abs(zd - z), -zd))


class Plan:
    def __init__(self, L, rank, reduces, early, follow, begin, tasks):
        self.L = L
        order = [far_first(L, z) for z in range(L)]
        never = 10**6
        jobs = list(rank)
        ready = {j: [[never] * L for _ in range(L)] for j in reduces}
        own = {j: begin.get(j, never) for j in jobs if j not in reduces}
        arrive = {j: {} for j in jobs}
        sent = {j: set() for j in jobs}
        for j, when in early.items():
            for z in range(L):
                for i in range(L):
                    ready[j][z][order[z][i]] = when[i]
        self.final, self.complete, self.tasks, self.sends = {}, {}, {}, []
        todo = list(tasks)
        total = L * (L - 1) * 2
        last = {j: -1 for j in jobs}
        s = free = 0

        def close():
            for j in jobs:
                if len(sent[j]) == total:
                    if j in reduces and j not in self.final:
                        self.final[j] = max(last[j] + 1, max(ready[j][z][z] for z in range(L)) - 1, s - 1)
                        if j in follow:
                            own[follow[j]] = self.final[j] + 1
                    if j in own and j not in self.complete:
                        self.complete[j] = last[j] + 2

        while any(len(sent[j]) < total for j in jobs) or todo:
            close()
            now = {}
            for z in range(L):
                for way in (1, -1):
                    if not 0 <= z + way < L:
                        continue
                    for j in jobs:
                        best = []
                        for block in range(L):
                            for half in (0, 1):
                                if (z, way, block, half) in sent[j]:
                                    continue
                                came = arrive[j].get((z, way, block, half), never)
                                if j in reduces:
                                    first = not 0 <= z - way < L
                                    if (block - z) * way > 0 and ready[j][z][block] <= s and (first or came + 2 <= s):
                                        best.append((-abs(block - z), half, block))
                                elif (z - block) * way >= 0 and (own[j] <= s if block == z else came + 2 <= s):
                                    best.append((abs(block - z), half, block))
                        if best:
                            _, half, block = min(best)
                            now[(z, way)] = (j, block, half)
                            break
            for (z, way), (j, block, half) in now.items():
                sent[j].add((z, way, block, half))
                arrive[j][(z + way, way, block, half)] = s
                last[j] = s
            self.sends.append(now)
            if todo and s >= free:
                name, needs, makes, i, length = todo[0]
                if needs is None or self.complete.get(needs, never) <= s:
                    self.tasks[s] = todo.pop(0)
                    free = s + length
                    for j in makes:
                        for z in range(L):
                            ready[j][z][order[z][i]] = s + 2
            s += 1
        close()
        self.jobs, self.reduces, self.order = jobs, reduces, order
        self.ready, self.arrive, self.own = ready, arrive, own
        self.slots = 1 + max(list(self.final.values()) + list(self.complete.values()))

    def block(self, z, i):
        return pick(z, [self.order[q][i] for q in range(self.L)])


def run_plan(plan, at, jobs, task, after, finish):
    z, L = at.z, at.L
    for s in range(plan.slots):
        now = plan.sends[s] if s < len(plan.sends) else {}
        for q in range(L):
            mine = [(way, now[(q, way)]) for way in (1, -1) if (q, way) in now]
            if mine:

                @pl.when(z == q)
                def _():
                    for way, (j, block, half) in mine:
                        jobs[j].copy(q, way, block, half).start()

        if s in plan.tasks:
            task(plan.tasks[s][0])
        after(s)
        past = plan.sends[s - 1] if 0 <= s - 1 < len(plan.sends) else {}
        for q in range(L):
            came = [(way, past[(q - way, way)]) for way in (1, -1) if (q - way, way) in past]
            adds = []
            for j in plan.reduces:
                for (zq, way, block, half), when in plan.arrive[j].items():
                    if zq == q and block != q and max(when + 1, plan.ready[j][q][block] - 1) == s:
                        adds.append((j, block, half))
            if came or adds:

                @pl.when(z == q)
                def _():
                    for way, (j, block, half) in came:
                        jobs[j].landed(q, way, block, half).wait_recv()
                        if j not in plan.reduces:
                            jobs[j].share(block, half).start()
                    for j, block, half in adds:
                        jobs[j].add(block, half)

        for j, when in plan.final.items():
            if when == s:
                finish(j)


def pick(z, values):
    if len(set(values)) == 1:
        return values[0]
    out = jnp.int32(values[0])
    for i, v in enumerate(values[1:], 1):
        out = jnp.where(z == i, v, out)
    return out


class SlotReduce:
    def __init__(self, at, sib, recv, sems):
        self.at, self.sib, self.recv = at, sib, recv
        self.sib_send, self.sib_recv, self.fwd_send, self.recv_sem = sems
        self.half = sib.shape[1] // 2

    @staticmethod
    def sems(L):
        return [DMA((L,)), DMA((L,)), DMA((L, 2)), DMA((L + 1, 2))]

    @staticmethod
    def bufs(L, T, D):
        return [pltpu.VMEM((L, T, D), BF16), pltpu.VMEM((L + 1, T, D), BF16)]

    def part(self, half):
        return pl.ds(half * self.half, self.half)

    def slot(self, z, way, zd):
        return self.at.L if way < 0 and z == zd else zd

    def copy(self, z, way, zd, half):
        at, part = self.at, self.part(half)
        first = not 0 <= z - way < at.L
        src = (self.sib if first else self.recv).at[zd, part, :]
        slot = self.slot(z + way, way, zd)
        device = {"head": at.up if way > 0 else at.down}
        return remote(src, self.recv.at[slot, part, :], self.fwd_send.at[zd, half], self.recv_sem.at[slot, half], device)

    def landed(self, z, way, zd, half):
        at, part = self.at, self.part(half)
        slot = self.slot(z, way, zd)
        block = self.recv.at[slot, part, :]
        device = {"head": at.down if way > 0 else at.up}
        return remote(block, block, self.fwd_send.at[zd, half], self.recv_sem.at[slot, half], device)

    def exchange(self, zd, src):
        return remote(src, self.sib.at[zd], self.sib_send.at[zd], self.sib_recv.at[zd], {"head": self.at.sib})

    def combine(self, zd, mine):
        def add(rows):
            self.sib[zd, rows, :] = (self.sib[zd, rows, :].astype(F32) + mine[rows, :].astype(F32)).astype(BF16)

        chunk_loop(self.sib.shape[1], 32, add)

    def add(self, zd, half):
        def one(rows):
            self.recv[zd, rows, :] = (self.recv[zd, rows, :].astype(F32) + self.sib[zd, rows, :].astype(F32)).astype(BF16)

        step = min(32, self.half)

        @pl.loop(0, self.half // step)
        def _(i):
            one(pl.ds(pl.multiple_of(half * self.half + i * step, step), step))

    def final(self, put):
        at, z = self.at, self.at.z

        def run(extra):
            def part(rows):
                value = self.sib[z, rows, :].astype(F32)
                for slot in extra:
                    value = value + self.recv[slot, rows, :].astype(F32)
                put(rows, value)

            chunk_loop(self.sib.shape[1], 32, part)

        @pl.when(z == 0)
        def _():
            run((at.L,))

        @pl.when(z == at.L - 1)
        def _():
            run((z,))

        @pl.when((z > 0) & (z < at.L - 1))
        def _():
            run((z, at.L))

    def sent(self):
        at = self.at
        for zd in range(at.L):

            @pl.when(zd != at.z)
            def _():
                for half in (0, 1):
                    block = self.recv.at[zd, self.part(half), :]
                    remote(block, block, self.fwd_send.at[zd, half], self.recv_sem.at[zd, half], {"head": at.up}).wait_send()


class SlotGather:
    def __init__(self, at, own, out, sems):
        self.at, self.own, self.out = at, own, out
        self.line_recv, self.up_send, self.down_send, self.sib_send, self.sib_recv, self.local = sems
        self.half = own.shape[0] // 2

    @staticmethod
    def sems(L):
        return [DMA((L, 2))] * 5 + [DMA]

    def block(self, index, half):
        return self.out.at[index, pl.ds(half * self.half, self.half), :]

    def mine(self, half):
        return self.own.at[pl.ds(half * self.half, self.half), :]

    def copy(self, z, way, zb, half):
        at = self.at
        dst = self.block(zb * 2 + at.c, half)
        src = self.mine(half) if zb == z else dst
        send = (self.up_send if way > 0 else self.down_send).at[zb, half]
        return remote(src, dst, send, self.line_recv.at[zb, half], {"head": at.up if way > 0 else at.down})

    def landed(self, z, way, zb, half):
        at = self.at
        dst = self.block(zb * 2 + at.c, half)
        return remote(dst, dst, self.up_send.at[zb, half], self.line_recv.at[zb, half], {"head": at.down if way > 0 else at.up})

    def share(self, zb, half, src=None):
        at = self.at
        dst = self.block(zb * 2 + at.c, half)
        return remote(dst if src is None else src, dst, self.sib_send.at[zb, half], self.sib_recv.at[zb, half], {"head": at.sib})

    def keep(self):
        return pltpu.make_async_copy(self.own, self.out.at[self.at.h], self.local)

    def begin(self):
        for half in (0, 1):
            self.share(self.at.z, half, self.mine(half)).start()
        self.keep().start()

    def finish(self):
        at = self.at
        self.keep().wait()
        for zb in range(at.L):
            for half in (0, 1):
                self.share(zb, half).wait_send()
                other = self.block(zb * 2 + 1 - at.c, half)
                remote(other, other, self.sib_send.at[zb, half], self.sib_recv.at[zb, half], {"head": at.sib}).wait_recv()

            @pl.when((zb <= at.z) & (at.z < at.L - 1))
            def _():
                for half in (0, 1):
                    self.copy(-1, 1, zb, half).wait_send()

            @pl.when((zb >= at.z) & (at.z > 0))
            def _():
                for half in (0, 1):
                    self.copy(-1, -1, zb, half).wait_send()


def norm_back_part(values, gain, grad):
    inv_root = inv_root_of(values)
    unit = values * inv_root
    weighted = grad * gain
    back = inv_root * (weighted - unit * jnp.mean(weighted * unit, axis=-1, keepdims=True))
    return back, jnp.sum(grad * unit, axis=0, keepdims=True)


def feed_forward(n, H, terms, ct_full, tokens, cotangent, gains, w_gu, w_d):
    rows, T, D = tokens.shape
    L = H // 2
    ff = w_d.shape[1]
    S = H * T
    U = w_d.shape[0] // n // 2
    square = n == 4
    rank = []
    for kinds in (("mix", "in"), ("sum", "att"), ("out",)):
        rank += [(kind, r) for r in range(rows) for kind in kinds]
    tasks = []
    for r in range(rows):
        for i in range(L):
            tasks.append((("first", r, i), ("in", r), (), i, 1))
            tasks.append((("second", r, i), None, (("sum", r), ("out", r)), i, 1))
    tasks += [(("grad", k, 0), None, (), 0, 1) for k in range(2 * n)]
    plan = Plan(
        L,
        rank,
        [j for j in rank if j[0] in ("mix", "sum", "out")],
        {("mix", r): [r * L + i for i in range(L)] for r in range(rows)},
        {(a, r): (b, r) for a, b in (("mix", "in"), ("sum", "att")) for r in range(rows)},
        {},
        tasks,
    )
    names = Names()
    n_bufs = [names.add(SlotReduce.bufs(L, T, D)) for _ in range(2 * rows)]
    n_sems = [names.add(SlotReduce.sems(L)) for _ in range(2 * rows)]
    n_gsem = [names.add(SlotGather.sems(L)) for _ in range(rows)]
    rest = names.add(
        [
            pltpu.VMEM((rows, T, D), BF16),
            pltpu.VMEM((rows, T, D), BF16),
            pltpu.VMEM((rows, T, D), F32),
            pltpu.VMEM((2, 2, T, D), BF16),
            pltpu.VMEM((2, 2, T, D), BF16),
            pltpu.VMEM((max(D, rows * S), 2 * ff), BF16),
            pltpu.VMEM((max(D, rows * S), ff), BF16),
            pltpu.VMEM((2, 2, T, D), BF16),
            pltpu.VMEM((2, 2, T, D), BF16),
            pltpu.VMEM((2, max(2 * T, U), ff), BF16),
            pltpu.VMEM((2, max(2 * T, U), 2 * ff), BF16),
            pltpu.VMEM((2, rows, H, T, U), BF16),
            pltpu.VMEM((2, rows, H, T, U), BF16),
            DMA((4,)),
            DMA((2, 4)),
            DMA((2, 4)),
            DMA((2,)),
            DMA((rows, L)),
            DMA((2,)),
            DMA((2,)),
            DMA((2,)),
            DMA((2,)),
        ]
    )
    tile = min(256, ff)
    wide = min(512, D)

    def kernel(
        src,
        ctf,
        tok,
        ct,
        gain,
        wgu_hbm,
        wd_hbm,
        mlp_in,
        g_att,
        hid_hbm,
        ggu_hbm,
        grad_gu,
        grad_d,
        first_gu,
        first_d,
        g_mixed,
        layer_out,
        gain_sum,
        *scratch,
    ):
        at = Place(n, H)
        z = at.z
        (
            normed,
            att,
            mixed,
            stage_g,
            stage_o,
            wgu,
            wd,
            xb,
            cb,
            hb,
            gb,
            xt,
            ct_t,
            t_sem,
            gsend,
            grecv,
            w_sem,
            own_sem,
            x_sem,
            c_sem,
            h_sem,
            g_sem,
        ) = scratch[rest]
        loads = [
            pltpu.make_async_copy(wgu_hbm, wgu.at[pl.ds(0, D), :], w_sem.at[0]),
            pltpu.make_async_copy(wd_hbm, wd.at[pl.ds(0, D), :], w_sem.at[1]),
        ]
        red, gat = {}, {}
        for r in range(rows):
            for kind in ("mix", "sum"):
                red[(kind, r)] = SlotReduce(at, *scratch[n_bufs[r]], scratch[n_sems[r]])
            red[("out", r)] = SlotReduce(at, *scratch[n_bufs[rows + r]], scratch[n_sems[rows + r]])
            gat[("in", r)] = SlotGather(at, normed.at[r], mlp_in.at[r], scratch[n_gsem[r]])
            gat[("att", r)] = SlotGather(at, att.at[r], g_att.at[r], scratch[n_gsem[r]])
        both = {**red, **gat}
        at.greet(batch=square)

        def mine_of(r, zd):
            return red[("out", r)].recv.at[zd]

        def own_load(r, zd):
            return pltpu.make_async_copy(src.at[r, zd * 2 + at.c], mine_of(r, zd), own_sem.at[r, zd])

        def exchange(r, zd):
            return red[("mix", r)].exchange(zd, src.at[r, zd * 2 + 1 - at.c])

        for r in range(rows):
            for i in range(L):
                zd = plan.block(z, i)
                exchange(r, zd).start()
                own_load(r, zd).start()
        for job in loads:
            job.start()
        gain_sum[...] = jnp.zeros_like(gain_sum)

        def combine_mix(r, i):
            zd = plan.block(z, i)
            own_load(r, zd).wait()
            exchange(r, zd).wait()
            red[("mix", r)].combine(zd, mine_of(r, zd))

        def combine_terms(r, i):
            zd = plan.block(z, i)
            for kind, stage in (("sum", stage_g), ("out", stage_o)):
                job = red[(kind, r)]
                job.exchange(zd, stage.at[i % 2, 1 - at.c]).wait()
                job.combine(zd, stage.at[i % 2, at.c])

        def x_load(r, i):
            blk = plan.block(z, i)
            return (
                pltpu.make_async_copy(mlp_in.at[r, pl.ds(2 * blk, 2)], xb.at[i % 2], x_sem.at[i % 2]),
                pltpu.make_async_copy(ctf.at[r, pl.ds(2 * blk, 2)], cb.at[i % 2], c_sem.at[i % 2]),
            )

        def act_store(r, i):
            blk = plan.block(z, i)
            at_row = pl.ds(pl.multiple_of(r * S + blk * 2 * T, 2 * T), 2 * T)
            return (
                pltpu.make_async_copy(hb.at[i % 2, pl.ds(0, 2 * T), :], hid_hbm.at[at_row, :], h_sem.at[i % 2]),
                pltpu.make_async_copy(gb.at[i % 2, pl.ds(0, 2 * T), :], ggu_hbm.at[at_row, :], g_sem.at[i % 2]),
            )

        def first_part(r, i):
            if i == 0:
                gat[("in", r)].finish()
                for job in x_load(r, 0):
                    job.start()
                if r == 0:
                    for job in loads:
                        job.wait()
            for job in x_load(r, i):
                job.wait()
            if i + 1 < L:
                for job in x_load(r, i + 1):
                    job.start()
            if r * L + i >= 2:
                before = (r, i - 2) if i >= 2 else (r - 1, L + i - 2)
                for job in act_store(*before):
                    job.wait()
            k = i % 2

            @pl.loop(0, ff // tile)
            def _(j):
                cols = pl.ds(pl.multiple_of(j * tile, tile), tile)
                up_cols = pl.ds(pl.multiple_of(ff + j * tile, tile), tile)
                x = xb[k].reshape(2 * T, D)
                gate = jnp.dot(x, wgu[0:D, cols], preferred_element_type=F32)
                up = jnp.dot(x, wgu[0:D, up_cols], preferred_element_type=F32)
                back = jnp.dot(cb[k].reshape(2 * T, D), wd[0:D, cols], preferred_element_type=F32)
                sig = 1.0 / (1.0 + jnp.exp(-gate))
                silu = gate * sig
                hb[k, 0 : 2 * T, cols] = (silu * up).astype(BF16)
                gb[k, 0 : 2 * T, cols] = (back * up * (sig * (1.0 + gate * (1.0 - sig)))).astype(BF16)
                gb[k, 0 : 2 * T, up_cols] = (back * silu).astype(BF16)

            for job in act_store(r, i):
                job.start()

        def second_part(r, i):
            k = i % 2

            @pl.loop(0, D // wide)
            def _(j):
                cols = pl.ds(pl.multiple_of(j * wide, wide), wide)
                back = cols_dot(gb[k, 0 : 2 * T, :], wgu[cols, :]).astype(BF16)
                stage_g[k, 0, :, cols] = back[:T]
                stage_g[k, 1, :, cols] = back[T:]
                out = cols_dot(hb[k, 0 : 2 * T, :], wd[cols, :]).astype(BF16)
                stage_o[k, 0, :, cols] = out[:T]
                stage_o[k, 1, :, cols] = out[T:]

            zd = plan.block(z, i)
            for kind, stage in (("sum", stage_g), ("out", stage_o)):
                red[(kind, r)].exchange(zd, stage.at[k, 1 - at.c]).start()

        def finish_mix(r):
            def put(part, value):
                value = value + tok[r, part, :].astype(F32)
                mixed[r, part, :] = value
                normed[r, part, :] = (value * inv_root_of(value) * gain[1:2, :]).astype(BF16)

            red[("mix", r)].final(put)
            red[("mix", r)].sent()
            gat[("in", r)].begin()

        def finish_sum(r):
            def put(part, value):
                back, gain_part = norm_back_part(mixed[r, part, :], gain[1:2, :], value)
                total = ct[r, part, :].astype(F32) + back
                g_mixed[r, part, :] = total
                att[r, part, :] = total.astype(BF16)
                gain_sum[1:2, :] += gain_part

            red[("sum", r)].final(put)
            red[("sum", r)].sent()
            gat[("att", r)].begin()

        def finish_out(r):
            def put(part, value):
                layer_out[r, part, :] = (mixed[r, part, :] + value).astype(BF16)

            red[("out", r)].final(put)
            red[("out", r)].sent()

        if square:
            units = [
                ((1 - at.y) * 2 + 1 - at.x, 0, 1 - at.y, at.xn),
                ((1 - at.y) * 2 + 1 - at.x, 1, 3 - at.x, at.yn),
                (at.y * 2 + 1 - at.x, 0, at.y, at.xn),
                ((1 - at.y) * 2 + at.x, 1, 2 + at.x, at.yn),
                ((1 - at.y) * 2 + at.x, 0, None, None),
                (at.y * 2 + 1 - at.x, 1, None, None),
                (at.b, 0, None, None),
                (at.b, 1, None, None),
            ]
        else:
            units = [(k // 2, k % 2, None, None) for k in range(2 * n)]
        again = [
            pltpu.make_async_copy(ggu_hbm, wgu.at[pl.ds(0, rows * S), :], w_sem.at[0]),
            pltpu.make_async_copy(hid_hbm, wd.at[pl.ds(0, rows * S), :], w_sem.at[1]),
        ]

        def columns(k):
            cols = pl.ds(pl.multiple_of((units[k][0] * 2 + units[k][1]) * U, U), U)
            return [
                pltpu.make_async_copy(mlp_in.at[:, :, :, cols], xt.at[k % 2], t_sem.at[k % 2]),
                pltpu.make_async_copy(ctf.at[:, :, :, cols], ct_t.at[k % 2], t_sem.at[2 + k % 2]),
            ]

        def grad_store(k):
            b, half = units[k][:2]
            part = pl.ds(half * U, U)
            return [
                pltpu.make_async_copy(hb.at[k % 2, pl.ds(0, U), :], grad_d.at[b, part, :], h_sem.at[k % 2]),
                pltpu.make_async_copy(gb.at[k % 2, pl.ds(0, U), :], grad_gu.at[b, part, :], g_sem.at[k % 2]),
            ]

        def grad_sends(k):
            b, half, slot, to = units[k]
            part = pl.ds(half * U, U)
            return [
                remote(src.at[b, part, :], dst.at[slot], gsend.at[a, k], grecv.at[a, slot], {"batch": to})
                for a, (src, dst) in enumerate(((grad_d, first_d), (grad_gu, first_gu)))
            ]

        def prepare_grads():
            for i in (L - 2, L - 1):
                for job in act_store(rows - 1, i):
                    job.wait()
            for job in again + columns(0):
                job.start()

        def grad(k):
            if k == 0:
                for job in again:
                    job.wait()
            for job in columns(k):
                job.wait()
            if k + 1 < 2 * n:
                for job in columns(k + 1):
                    job.start()
            ring = k % 2

            @pl.loop(0, 2 * ff // tile)
            def _(j):
                cols = pl.ds(pl.multiple_of(j * tile, tile), tile)
                x = xt[ring].reshape(rows * S, U)
                gb[ring, 0:U, cols] = rows_dot(x, wgu[0 : rows * S, cols]).astype(BF16)

            @pl.loop(0, ff // tile)
            def _(j):
                cols = pl.ds(pl.multiple_of(j * tile, tile), tile)
                x = ct_t[ring].reshape(rows * S, U)
                hb[ring, 0:U, cols] = rows_dot(x, wd[0 : rows * S, cols]).astype(BF16)

            for job in grad_store(k):
                job.start()

        def task(name):
            kind, r, i = name
            if kind == "first":
                first_part(r, i)
            elif kind == "second":
                second_part(r, i)
                if (r, i) == (rows - 1, L - 1):
                    prepare_grads()
            else:
                grad(r)

        def after(s):
            if s + 1 < rows * L:
                combine_mix((s + 1) // L, (s + 1) % L)
            name = plan.tasks[s - 1][0] if s - 1 in plan.tasks else None
            if name and name[0] == "second":
                combine_terms(*name[1:])
            if name and name[0] == "grad":
                for job in grad_store(name[1]):
                    job.wait()
                if units[name[1]][3] is not None:
                    for job in grad_sends(name[1]):
                        job.start()

        def finish(j):
            {"mix": finish_mix, "sum": finish_sum, "out": finish_out}[j[0]](j[1])

        combine_mix(0, 0)
        run_plan(plan, at, both, task, after, finish)
        if square:
            for k in range(4):
                for job in grad_sends(k):
                    job.wait()
        for r in range(rows):
            gat[("att", r)].finish()

    return pl.pallas_call(
        kernel,
        out_shape=(
            jax.ShapeDtypeStruct((rows, H, T, D), BF16),
            jax.ShapeDtypeStruct((rows, H, T, D), BF16),
            jax.ShapeDtypeStruct((rows * S, ff), BF16),
            jax.ShapeDtypeStruct((rows * S, 2 * ff), BF16),
            jax.ShapeDtypeStruct((n, 2 * U, 2 * ff), BF16),
            jax.ShapeDtypeStruct((n, 2 * U, ff), BF16),
            jax.ShapeDtypeStruct((4, U, 2 * ff), BF16),
            jax.ShapeDtypeStruct((4, U, ff), BF16),
            jax.ShapeDtypeStruct((rows, T, D), F32),
            jax.ShapeDtypeStruct((rows, T, D), BF16),
            jax.ShapeDtypeStruct((8, D), F32),
        ),
        in_specs=[ANY, ANY, VMEM, VMEM, VMEM, ANY, ANY],
        out_specs=(ANY,) * 8 + (VMEM, VMEM, VMEM),
        scratch_shapes=names.shapes,
        compiler_params=pltpu.CompilerParams(collective_id=2, has_side_effects=True, vmem_limit_bytes=VMEM_LIMIT),
        name="feed_forward",
    )(terms, ct_full, tokens, cotangent, gains, w_gu, w_d)


def last_sums(n, H, terms, tokens, g_mixed, gains, gain_sum, g_qkv, g_o, g_gu, g_d, first_gu, first_d):
    rows, T, D = tokens.shape
    L = H // 2
    R, hw = g_o.shape[1], g_o.shape[2]
    ff = g_d.shape[2]
    names = Names()
    r_bufs = [names.add(Reduce.bufs(L, T, D)) for _ in range(rows)]
    r_sems = [names.add(Reduce.sems(L)) for _ in range(rows)]
    b_bufs = [names.add(BatchReduce.bufs(n, R, w)) for w in (ff, 2 * ff, hw, 3 * hw)]
    b_sems = [names.add(BatchReduce.sems(n)) for _ in range(4)]
    s_at = names.add(
        [pltpu.VMEM((8, D), F32), pltpu.VMEM((n, 8, R), F32), pltpu.VMEM((H, 8, R), F32)]
        + [DMA((n,)), DMA((n,)), DMA((H,)), DMA((H,)), DMA]
    )

    def kernel(src, tok, gmix, gain, gain_in, gqkv, go, ggu, gd, fgu, fd, grad_in, gq, gk, gv, gout, ggate, gup, gdown, gain_out, *scratch):
        at = Place(n, H)
        at.greet(all_heads=True)
        small, over_batch, over_head, bsend, brecv, hsend, hrecv, local = scratch[s_at]
        sums = [Reduce(at, src.at[r], *scratch[r_bufs[r]], scratch[r_sems[r]]) for r in range(rows)]
        weights = [
            BatchReduce(at, s, scratch[b_bufs[i]], scratch[b_sems[i]], first if at.square else None)
            for i, (s, first) in enumerate(((gd, fd), (ggu, fgu), (go, None), (gqkv, None)))
        ]
        for job in sums[:1] + weights + sums[1:]:
            job.start()
        for job in weights[:2]:
            job.second_step()
        small[...] = gain_in[...]

        def finish_sum(r):
            def put(part, value):
                back, gain_part = norm_back_part(tok[r, part, :].astype(F32), gain[0:1, :], value)
                grad_in[r, part, :] = gmix[r, part, :] + back
                small[0:1, :] += gain_part

            sums[r].final(put)

        for k in range(L - 1):
            sums[0].hops(k)
        for r in range(rows):
            if r + 1 < rows:
                for k in range(L - 1):
                    sums[r + 1].hops(k, "first")
            finish_sum(r)
            if r + 1 < rows:
                for k in range(L - 1):
                    sums[r + 1].hops(k, "mid")
        for job in weights[2:]:
            job.second_step()

        def slice_of(b):
            return small.at[:, pl.ds(pl.multiple_of(b * R, R), R)]

        def batch_job(off):
            to = (at.b + off) % n
            return remote(slice_of(to), over_batch.at[off], bsend.at[off], brecv.at[off], {"batch": to})

        for off in range(1, n):
            batch_job(off).start()
        mine = pltpu.make_async_copy(slice_of(at.b), over_batch.at[0], local)
        mine.start()

        def put_o(part, value):
            gout[part, :] = value

        def put_d(part, value):
            gdown[part, :] = value

        def put_gu(part, value):
            ggate[part, :] = value[:, :ff]
            gup[part, :] = value[:, ff:]

        weights[0].final(put_d)
        weights[1].final(put_gu)
        weights[2].final(put_o)
        mine.wait()
        total = over_batch[0]
        for off in range(1, n):
            batch_job(off).wait_recv()
            total = total + over_batch[off]
        over_head[at.h] = total

        def head_job(off, block):
            to = (at.h + off) % H
            return remote(over_head.at[block], over_head.at[block], hsend.at[off], hrecv.at[off], {"head": to})

        for off in range(1, H):
            head_job(off, at.h).start()

        def put_qkv(part, value):
            gq[part, :] = value[:, :hw]
            gk[part, :] = value[:, hw : 2 * hw]
            gv[part, :] = value[:, 2 * hw :]

        weights[3].final(put_qkv)
        for off in range(1, H):
            head_job(off, (at.h + H - off) % H).wait_recv()
        total = over_head[0]
        for h in range(1, H):
            total = total + over_head[h]
        gain_out[...] = total
        for off in range(1, n):
            batch_job(off).wait_send()
        for off in range(1, H):
            head_job(off, at.h).wait_send()
        for job in sums + weights:
            job.finish()

    return pl.pallas_call(
        kernel,
        out_shape=(
            jax.ShapeDtypeStruct((rows, T, D), F32),
            jax.ShapeDtypeStruct((R, hw), F32),
            jax.ShapeDtypeStruct((R, hw), F32),
            jax.ShapeDtypeStruct((R, hw), F32),
            jax.ShapeDtypeStruct((R, hw), F32),
            jax.ShapeDtypeStruct((R, ff), F32),
            jax.ShapeDtypeStruct((R, ff), F32),
            jax.ShapeDtypeStruct((R, ff), F32),
            jax.ShapeDtypeStruct((8, R), F32),
        ),
        in_specs=[ANY, VMEM, VMEM, VMEM, VMEM] + [ANY] * 6,
        out_specs=(VMEM,) * 9,
        scratch_shapes=names.shapes,
        compiler_params=pltpu.CompilerParams(collective_id=4, has_side_effects=True, vmem_limit_bytes=VMEM_LIMIT),
        name="last_sums",
    )(terms, tokens, g_mixed, gains, gain_sum, g_qkv, g_o, g_gu, g_d, first_gu, first_d)


def rows_dot(left, right):
    return lax.dot_general(left, right, (((0,), (0,)), ((), ())), preferred_element_type=F32)


def cols_dot(left, right):
    return lax.dot_general(left, right, (((1,), (1,)), ((), ())), preferred_element_type=F32)


QUERIES = 256


def rope_tables(positions):
    half_dim = HEAD_DIM // 2
    frequency = rope_base ** (-(jnp.arange(half_dim).astype(F32) * 2.0) / HEAD_DIM)
    angles = positions.astype(F32)[:, :, None] * frequency
    cosine, sine = jnp.cos(angles), jnp.sin(angles)
    return jnp.concatenate([cosine] * 4, axis=-1), jnp.concatenate([-sine, sine] * 2, axis=-1)


def rotate(values, cosine, sine):
    half_dim = HEAD_DIM // 2
    parts = []
    for g in range(values.shape[1] // 128):
        part = values[:, g * 128 : (g + 1) * 128]
        lane = lax.broadcasted_iota(jnp.int32, part.shape, 1)
        swapped = jnp.where(
            lane % HEAD_DIM < half_dim, pltpu.roll(part, 128 - half_dim, 1), pltpu.roll(part, half_dim, 1)
        )
        parts.append(part * cosine + swapped * sine)
    return jnp.concatenate(parts, axis=1) if len(parts) > 1 else parts[0]


def only_head(values, h):
    lane = lax.broadcasted_iota(jnp.int32, values.shape, 1)
    return jnp.where(lane // HEAD_DIM == h, values, jnp.zeros_like(values))


def masked_scores(keys, query, starts, first):
    scores = cols_dot(keys, query)
    key_index = lax.broadcasted_iota(jnp.int32, scores.shape, 0)
    query_index = lax.broadcasted_iota(jnp.int32, scores.shape, 1) + first
    return jnp.where((key_index >= starts) & (key_index <= query_index), scores, masked_value)


def attend(qkv, starts, lse, attended, h, W):
    S = qkv.shape[0]
    scale = HEAD_DIM**-0.5
    block = min(QUERIES, S)
    for i in range(S // block):
        rows = pl.ds(i * block, block)
        width = (i + 1) * block
        query = only_head(qkv[rows, 0:W], h) * jnp.asarray(scale, BF16)
        scores = masked_scores(qkv[0:width, W : 2 * W], query, starts[:, rows], i * block)
        top = jnp.max(scores, axis=0, keepdims=True)
        weights = jnp.exp(scores - top)
        total = jnp.sum(weights, axis=0, keepdims=True)
        lse[pl.ds(h, 1), rows] = top + jnp.log(total)
        probs = (weights * (1.0 / total)).astype(BF16)
        out = rows_dot(probs, qkv[0:width, 2 * W : 3 * W]).astype(BF16)
        lane = lax.broadcasted_iota(jnp.int32, out.shape, 1)
        attended[rows, :] = jnp.where(lane // HEAD_DIM == h, out, attended[rows, :])


def attend_back(qkv, starts, lse, grad, g_query, g_key, g_value, h, W):
    S = qkv.shape[0]
    scale = HEAD_DIM**-0.5
    block = min(QUERIES, S)
    for i in range(S // block):
        rows = pl.ds(i * block, block)
        width = (i + 1) * block
        query = only_head(qkv[rows, 0:W], h) * jnp.asarray(scale, BF16)
        keys = qkv[0:width, W : 2 * W]
        scores = masked_scores(keys, query, starts[:, rows], i * block)
        probs = jnp.exp(scores - lse[pl.ds(h, 1), rows])
        back = only_head(grad[rows, :], h)
        g_prob = cols_dot(qkv[0:width, 2 * W : 3 * W], back)
        delta = jnp.sum(probs * g_prob, axis=0, keepdims=True)
        g_score = (probs * (g_prob - delta)).astype(BF16)
        g_value[0:width, :] += jnp.dot(probs.astype(BF16), back, preferred_element_type=F32)
        g_key[0:width, :] += jnp.dot(g_score, query, preferred_element_type=F32)
        g_query[rows, :] += only_head(rows_dot(g_score, keys) * scale, h)


def attention_forward(attn_in, w_qkv, w_o, cosine, sine, starts):
    rows, S, D = attn_in.shape
    W = w_o.shape[1]
    heads = W // HEAD_DIM
    step = min(256, S)

    def kernel(x, wq, wo, cos, sin, st, qkv, lse, attended, terms):
        @pl.loop(0, S // step)
        def _(b):
            part = pl.ds(pl.multiple_of(b * step, step), step)
            lin = jnp.dot(x[0, part, :], wq[...], preferred_element_type=F32)
            c, s = cos[0, part, :], sin[0, part, :]
            qkv[0, part, 0:W] = rotate(lin[:, :W], c, s).astype(BF16)
            qkv[0, part, W : 2 * W] = rotate(lin[:, W : 2 * W], c, s).astype(BF16)
            qkv[0, part, 2 * W : 3 * W] = lin[:, 2 * W :].astype(BF16)

        @pl.loop(0, heads)
        def _(h):
            attend(qkv.at[0], st.at[0], lse.at[0], attended.at[0], h, W)

        @pl.loop(0, S // step)
        def _(b):
            part = pl.ds(pl.multiple_of(b * step, step), step)
            terms[0, part, :] = cols_dot(attended[0, part, :], wo[...]).astype(BF16)

    def row(*shape):
        return pl.BlockSpec((1,) + shape, lambda r: (r, 0, 0))

    return pl.pallas_call(
        kernel,
        grid=(rows,),
        out_shape=(
            jax.ShapeDtypeStruct((rows, S, 3 * W), BF16),
            jax.ShapeDtypeStruct((rows, 8, S), F32),
            jax.ShapeDtypeStruct((rows, S, W), BF16),
            jax.ShapeDtypeStruct((rows, S, D), BF16),
        ),
        in_specs=[
            row(S, D),
            pl.BlockSpec((D, 3 * W), lambda r: (0, 0)),
            pl.BlockSpec((D, W), lambda r: (0, 0)),
            row(S, 128),
            row(S, 128),
            row(1, S),
        ],
        out_specs=(row(S, 3 * W), row(8, S), row(S, W), row(S, D)),
        compiler_params=pltpu.CompilerParams(vmem_limit_bytes=VMEM_LIMIT),
        name="attention_forward",
    )(attn_in, w_qkv, w_o, cosine, sine, starts)


def attention_backward(g_att, attended, qkv, lse, attn_in, w_qkv, w_o, cosine, sine, starts):
    rows, S, D = attn_in.shape
    W = w_o.shape[1]
    heads = W // HEAD_DIM
    step = min(256, S)
    wide = min(512, D)

    def kernel(ga, att, qkv, ls, x, wq, wo, cos, sin, st, terms, grad_qkv, grad_o, gat, gq, gk, gv, gqkv, sum_qkv, sum_o):
        r = pl.program_id(0)

        @pl.when(r == 0)
        def _():
            sum_qkv[...] = jnp.zeros_like(sum_qkv)
            sum_o[...] = jnp.zeros_like(sum_o)

        gq[...] = jnp.zeros_like(gq)
        gk[...] = jnp.zeros_like(gk)
        gv[...] = jnp.zeros_like(gv)

        @pl.loop(0, S // step)
        def _(b):
            part = pl.ds(pl.multiple_of(b * step, step), step)
            gat[part, :] = jnp.dot(ga[0, part, :], wo[...], preferred_element_type=F32).astype(BF16)

        @pl.loop(0, heads)
        def _(h):
            attend_back(qkv.at[0], st.at[0], ls.at[0], gat, gq, gk, gv, h, W)

        @pl.loop(0, S // step)
        def _(b):
            part = pl.ds(pl.multiple_of(b * step, step), step)
            c, s = cos[0, part, :], -sin[0, part, :]
            gqkv[part, 0:W] = rotate(gq[part, :], c, s).astype(BF16)
            gqkv[part, W : 2 * W] = rotate(gk[part, :], c, s).astype(BF16)
            gqkv[part, 2 * W : 3 * W] = gv[part, :].astype(BF16)
            terms[0, part, :] = cols_dot(gqkv[part, :], wq[...]).astype(BF16)

        @pl.loop(0, D // wide)
        def _(j):
            cols = pl.ds(pl.multiple_of(j * wide, wide), wide)
            sum_qkv[:, cols] += rows_dot(gqkv[...], x[0, :, cols])
            sum_o[:, cols] += rows_dot(att[0], ga[0, :, cols])

        @pl.when(r == rows - 1)
        def _():
            @pl.loop(0, D // wide)
            def _(j):
                cols = pl.ds(pl.multiple_of(j * wide, wide), wide)
                grad_qkv[cols, :] = sum_qkv[:, cols].T.astype(BF16)
                grad_o[cols, :] = sum_o[:, cols].T.astype(BF16)

    def row(*shape):
        return pl.BlockSpec((1,) + shape, lambda r: (r, 0, 0))

    def whole(*shape):
        return pl.BlockSpec(shape, lambda r: (0, 0))

    return pl.pallas_call(
        kernel,
        grid=(rows,),
        out_shape=(
            jax.ShapeDtypeStruct((rows, S, D), BF16),
            jax.ShapeDtypeStruct((D, 3 * W), BF16),
            jax.ShapeDtypeStruct((D, W), BF16),
        ),
        in_specs=[
            row(S, D),
            row(S, W),
            row(S, 3 * W),
            row(8, S),
            row(S, D),
            whole(D, 3 * W),
            whole(D, W),
            row(S, 128),
            row(S, 128),
            row(1, S),
        ],
        out_specs=(row(S, D), whole(D, 3 * W), whole(D, W)),
        scratch_shapes=[
            pltpu.VMEM((S, W), BF16),
            pltpu.VMEM((S, W), F32),
            pltpu.VMEM((S, W), F32),
            pltpu.VMEM((S, W), F32),
            pltpu.VMEM((S, 3 * W), BF16),
            pltpu.VMEM((3 * W, D), F32),
            pltpu.VMEM((W, D), F32),
        ],
        compiler_params=pltpu.CompilerParams(vmem_limit_bytes=VMEM_LIMIT),
        name="attention_backward",
    )(g_att, attended, qkv, lse, attn_in, w_qkv, w_o, cosine, sine, starts)


def per_device(
    n,
    H,
    tokens,
    segment_ids,
    position_ids,
    w_query,
    w_key,
    w_value,
    w_output,
    w_gate,
    w_up,
    w_down,
    attn_gain,
    mlp_gain,
    cotangent,
):
    rows, T, D = tokens.shape
    S = T * H
    R, hw = w_query.shape
    ff = w_gate.shape[1]
    shard_gains = jnp.concatenate(
        [attn_gain.astype(F32)[None], mlp_gain.astype(F32)[None], jnp.zeros((6, R), F32)], axis=0
    )
    attn_in, ct_full, w_qkv, w_o, w_gu, w_d, gains = gather_all(
        n, H, tokens, cotangent, shard_gains, (w_query, w_key, w_value, w_output, w_gate, w_up, w_down)
    )
    w_qkv = w_qkv.reshape(D, 3 * hw)
    w_o = w_o.reshape(D, hw)
    w_gu = w_gu.reshape(D, 2 * ff)
    w_d = w_d.reshape(D, ff)

    cosine, sine = rope_tables(position_ids)
    starts = (jnp.arange(S, dtype=jnp.int32)[None, :] - position_ids)[:, None, :]
    qkv, lse, attended, terms = attention_forward(attn_in.reshape(rows, S, D), w_qkv, w_o, cosine, sine, starts)
    terms = terms.reshape(rows, H, T, D)
    _, g_att, _, _, grad_gu, grad_d, first_gu, first_d, g_mixed, layer_out, gain_sum = feed_forward(
        n, H, terms, ct_full, tokens, cotangent, gains, w_gu, w_d
    )
    in_terms, grad_qkv, grad_o = attention_backward(
        g_att.reshape(rows, S, D), attended, qkv, lse, attn_in.reshape(rows, S, D), w_qkv, w_o, cosine, sine, starts
    )
    in_terms = in_terms.reshape(rows, H, T, D)
    grad_qkv = grad_qkv.reshape(n, R, 3 * hw)
    grad_o = grad_o.reshape(n, R, hw)
    grad_input, grad_q, grad_k, grad_v, grad_out, grad_gate, grad_up, grad_down, gain_grads = last_sums(
        n, H, in_terms, tokens, g_mixed, gains, gain_sum, grad_qkv, grad_o, grad_gu, grad_d, first_gu, first_d
    )
    return (
        layer_out,
        grad_input,
        grad_q,
        grad_k,
        grad_v,
        grad_out,
        grad_gate,
        grad_up,
        grad_down,
        gain_grads[0],
        gain_grads[1],
    )


def solution(mesh):
    row = P("batch", "head", None)
    ids = P("batch", None)
    weight = P("batch", "head")
    gain = P("batch")
    return jax.shard_map(
        functools.partial(per_device, mesh.shape["batch"], mesh.shape["head"]),
        mesh=mesh,
        in_specs=(row, ids, ids) + (weight,) * 7 + (gain, gain, row),
        out_specs=(row, row) + (weight,) * 7 + (gain, gain),
        check_vma=False,
    )
```

```python
import functools

import jax
import jax.numpy as jnp
from jax import lax
from jax.experimental import pallas as pl
from jax.experimental.pallas import tpu as pltpu
from jax.sharding import PartitionSpec as P

HEAD_DIM = 64
epsilon = 1e-05
rope_base = 130000.0
masked_value = -1000000000.0
MESH = pl.DeviceIdType.MESH
F32 = jnp.float32
BF16 = jnp.bfloat16
DMA = pltpu.SemaphoreType.DMA
ANY = pl.BlockSpec(memory_space=pl.ANY)
VMEM = pl.BlockSpec(memory_space=pltpu.VMEM)
VMEM_LIMIT = 60 * 2**20
BACK_LIMIT = 63 * 2**20


class Place:
    def __init__(self, batch, head):
        self.n, self.H = batch, head
        self.L = head // 2
        self.b = lax.axis_index("batch")
        self.h = lax.axis_index("head")
        self.z = self.h // 2
        self.c = self.h % 2
        self.sib = self.z * 2 + (1 - self.c)
        self.up = self.h + 2
        self.down = self.h - 2
        self.x, self.y = self.b % 2, self.b // 2
        self.xn = self.y * 2 + (1 - self.x)
        self.yn = (1 - self.y) * 2 + self.x
        self.dg = (1 - self.y) * 2 + (1 - self.x)
        self.square = batch == 4

    def greet(self, line=True, batch=True, all_heads=False):
        barrier = pltpu.get_barrier_semaphore()
        me, L = self, self.L

        def hello(device):
            pl.semaphore_signal(barrier, inc=1, device_id=device, device_id_type=MESH)

        count = 0
        if all_heads:
            for off in range(1, self.H):
                hello({"head": (me.h + off) % self.H})
                count += 1
        elif line:
            hello({"head": me.sib})
            count += 1

            @pl.when(me.z > 0)
            def _():
                hello({"head": me.down})

            @pl.when(me.z < L - 1)
            def _():
                hello({"head": me.up})

        if batch:
            if self.square and not all_heads:
                hello({"batch": me.xn})
                hello({"batch": me.yn})
                count += 2
            else:
                for off in range(1, self.n):
                    hello({"batch": (me.b + off) % self.n})
                    count += 1
        if line and not all_heads:
            count = count + jnp.minimum(me.z, 1) + jnp.minimum(L - 1 - me.z, 1)
        pl.semaphore_wait(barrier, count)


def remote(src, dst, ssem, rsem, device):
    return pltpu.make_async_remote_copy(
        src_ref=src, dst_ref=dst, send_sem=ssem, recv_sem=rsem, device_id=device, device_id_type=MESH
    )


class Gather:
    def __init__(self, at, own, out, sems):
        self.at, self.own, self.out = at, own, out
        self.line_recv, self.sib_recv, self.up_send, self.down_send, self.sib_send, self.local = sems

    @staticmethod
    def sems(at_L):
        return [DMA((at_L,))] * 5 + [DMA]

    def _up(self, zb, src):
        at = self.at
        return remote(src, self.out.at[zb * 2 + at.c], self.up_send.at[zb], self.line_recv.at[zb], {"head": at.up})

    def _down(self, zb, src):
        at = self.at
        return remote(src, self.out.at[zb * 2 + at.c], self.down_send.at[zb], self.line_recv.at[zb], {"head": at.down})

    def _sib(self, zb, src):
        at = self.at
        return remote(src, self.out.at[zb * 2 + at.c], self.sib_send.at[zb], self.sib_recv.at[zb], {"head": at.sib})

    def _mine(self):
        return pltpu.make_async_copy(self.own, self.out.at[self.at.h], self.local)

    def start(self):
        at = self.at

        @pl.when(at.z < at.L - 1)
        def _():
            self._up(at.z, self.own).start()

        @pl.when(at.z > 0)
        def _():
            self._down(at.z, self.own).start()

        self._sib(at.z, self.own).start()
        self._mine().start()

    def step(self, k):
        at = self.at
        below, above = at.z - k, at.z + k

        @pl.when(below >= 0)
        def _():
            block = self.out.at[below * 2 + at.c]
            self._up(below, block).wait_recv()

            @pl.when(at.z < at.L - 1)
            def _():
                self._up(below, block).start()

            self._sib(below, block).start()

        @pl.when(above <= at.L - 1)
        def _():
            block = self.out.at[above * 2 + at.c]
            self._down(above, block).wait_recv()

            @pl.when(at.z > 0)
            def _():
                self._down(above, block).start()

            self._sib(above, block).start()

    def finish(self):
        at = self.at
        self._mine().wait()
        for zb in range(at.L):
            block = self.out.at[zb * 2 + at.c]
            self._sib(zb, block).wait_send()
            other = self.out.at[zb * 2 + 1 - at.c]
            remote(other, other, self.sib_send.at[zb], self.sib_recv.at[zb], {"head": at.sib}).wait_recv()

            @pl.when((zb <= at.z) & (at.z < at.L - 1))
            def _():
                self._up(zb, block).wait_send()

            @pl.when((zb >= at.z) & (at.z > 0))
            def _():
                self._down(zb, block).wait_send()


class Reduce:
    def __init__(self, at, src, own, sib, recv, sems):
        self.at, self.src, self.own, self.sib, self.recv = at, src, own, sib, recv
        self.load, self.sib_send, self.sib_recv, self.fwd_send, self.recv_sem = sems

    @staticmethod
    def sems(L):
        return [DMA((L,)), DMA((L,)), DMA((L,)), DMA((L,)), DMA((L + 1,))]

    @staticmethod
    def bufs(L, T, D):
        return [pltpu.VMEM((L, T, D), BF16), pltpu.VMEM((L, T, D), BF16), pltpu.VMEM((L + 1, T, D), BF16)]

    def _load(self, zd):
        return pltpu.make_async_copy(self.src.at[zd * 2 + self.at.c], self.own.at[zd], self.load.at[zd])

    def _sib(self, zd):
        at = self.at
        return remote(
            self.src.at[zd * 2 + 1 - at.c], self.sib.at[zd], self.sib_send.at[zd], self.sib_recv.at[zd], {"head": at.sib}
        )

    def _fwd(self, zd, slot, device):
        return remote(self.recv.at[zd], self.recv.at[slot], self.fwd_send.at[zd], self.recv_sem.at[slot], {"head": device})

    def start(self):
        at, L = self.at, self.at.L
        order = []
        for k in range((L + 1) // 2):
            order += [L - 1 - k] + ([k] if k != L - 1 - k else [])
        for zd in order:
            self._sib(zd).start()
            self._load(zd).start()

    def _chunks(self, fn):
        T = self.own.shape[1]
        step = 32 if T % 32 == 0 else T

        @pl.loop(0, T // step)
        def _(i):
            fn(pl.ds(pl.multiple_of(i * step, step), step))

    def _hop(self, zd, first, slot, device, which):
        @pl.when(first)
        def _():
            if which in ("first", "both"):
                self._load(zd).wait()
                self._sib(zd).wait_recv()

                def add(rows):
                    self.recv[zd, rows, :] = (self.own[zd, rows, :].astype(F32) + self.sib[zd, rows, :].astype(F32)).astype(
                        BF16
                    )

                self._chunks(add)
                self._fwd(zd, slot, device).start()

        @pl.when(jnp.logical_not(first))
        def _():
            if which in ("mid", "both"):
                self._load(zd).wait()
                self._sib(zd).wait_recv()
                self._fwd(zd, zd, device).wait_recv()

                def add(rows):
                    self.recv[zd, rows, :] = (
                        self.own[zd, rows, :].astype(F32)
                        + self.sib[zd, rows, :].astype(F32)
                        + self.recv[zd, rows, :].astype(F32)
                    ).astype(BF16)

                self._chunks(add)
                self._fwd(zd, slot, device).start()

    def hops(self, k, which="both"):
        at, L = self.at, self.at.L
        far, near = L - 1 - k, k

        @pl.when(far > at.z)
        def _():
            self._hop(far, at.z == 0, far, at.up, which)

        @pl.when(near < at.z)
        def _():
            self._hop(near, at.z == L - 1, jnp.where(at.z - 1 == near, L, near), at.down, which)

    def final(self, add):
        at, L = self.at, self.at.L
        z = at.z
        self._load(z).wait()
        self._sib(z).wait_recv()

        @pl.when(z > 0)
        def _():
            self._fwd(z, z, at.up).wait_recv()

        @pl.when(z < L - 1)
        def _():
            self._fwd(z, L, at.down).wait_recv()

        def base(rows):
            return self.own[z, rows, :].astype(F32) + self.sib[z, rows, :].astype(F32)

        @pl.when(z == 0)
        def _():
            self._chunks(lambda rows: add(rows, base(rows) + self.recv[L, rows, :].astype(F32)))

        @pl.when(z == L - 1)
        def _():
            self._chunks(lambda rows: add(rows, base(rows) + self.recv[z, rows, :].astype(F32)))

        @pl.when((z > 0) & (z < L - 1))
        def _():
            self._chunks(
                lambda rows: add(
                    rows, base(rows) + self.recv[z, rows, :].astype(F32) + self.recv[L, rows, :].astype(F32)
                )
            )

    def finish(self):
        at = self.at
        for zd in range(at.L):
            self._sib(zd).wait_send()

            @pl.when(zd != at.z)
            def _():
                self._fwd(zd, zd, at.up).wait_send()


class BatchGather:
    def __init__(self, at, own, out, sems):
        self.at, self.own, self.out = at, own, out
        self.send, self.recv, self.local = sems

    @staticmethod
    def sems(n):
        m = 4 if n == 4 else n
        return [DMA((m,)), DMA((m,)), DMA]

    def _half(self, b, i):
        half = self.own.shape[0] // 2
        return self.out(b, pl.ds(i * half, half))

    def _all(self, b):
        return self.out(b, pl.ds(0, self.own.shape[0]))

    def _direct(self, i, device):
        at = self.at
        return remote(self.own, self._all(at.b), self.send.at[i], self.recv.at[i], {"batch": device})

    def start(self):
        at = self.at
        pltpu.make_async_copy(self.own, self._all(at.b), self.local).start()
        if at.square:
            self._direct(0, at.xn).start()
            self._direct(1, at.yn).start()
        else:
            for off in range(1, at.n):
                remote(
                    self.own, self._all(at.b), self.send.at[off], self.recv.at[off], {"batch": (at.b + off) % at.n}
                ).start()

    def forward(self):
        at = self.at
        if at.square:
            block = self._all(at.xn)
            remote(block, block, self.send.at[0], self.recv.at[0], {"batch": at.xn}).wait_recv()
            half = self._half(at.xn, 0)
            remote(half, half, self.send.at[2], self.recv.at[2], {"batch": at.yn}).start()
            block = self._all(at.yn)
            remote(block, block, self.send.at[1], self.recv.at[1], {"batch": at.yn}).wait_recv()
            half = self._half(at.yn, 1)
            remote(half, half, self.send.at[3], self.recv.at[3], {"batch": at.xn}).start()

    def finish(self):
        at = self.at
        pltpu.make_async_copy(self.own, self._all(at.b), self.local).wait()
        if at.square:
            self._direct(0, at.xn).wait_send()
            self._direct(1, at.yn).wait_send()
            half = self._half(at.dg, 0)
            remote(half, half, self.send.at[2], self.recv.at[2], {"batch": at.yn}).wait()
            half = self._half(at.dg, 1)
            remote(half, half, self.send.at[3], self.recv.at[3], {"batch": at.xn}).wait()
        else:
            for off in range(1, at.n):
                block = self._all((at.b + at.n - off) % at.n)
                remote(block, block, self.send.at[off], self.recv.at[off], {"batch": (at.b + off) % at.n}).wait()


class BatchReduce:
    def __init__(self, at, src, bufs, sems, before=None):
        self.at, self.src, self.before = at, src, before
        if at.square:
            self.first, self.mine, self.second = bufs
        else:
            (self.slots,) = bufs
        self.send, self.recv, self.load = sems

    @staticmethod
    def sems(n):
        m = 6 if n == 4 else n
        return [DMA((m,)), DMA((m,)), DMA((4,))]

    @staticmethod
    def bufs(n, R, K):
        if n == 4:
            return [
                pltpu.VMEM((4, R // 2, K), BF16),
                pltpu.VMEM((4, R // 2, K), BF16),
                pltpu.VMEM((2, R // 2, K), BF16),
            ]
        return [pltpu.VMEM((n, R, K), BF16)]

    def _first(self, i):
        at, half = self.at, self.src.shape[1] // 2
        if i < 2:
            src = self.src.at[i * 2 + 1 - at.x, pl.ds(0, half), :]
            device = {"batch": at.xn}
        else:
            src = self.src.at[(1 - at.y) * 2 + i - 2, pl.ds(half, half), :]
            device = {"batch": at.yn}
        return remote(src, self.first.at[i], self.send.at[i], self.recv.at[i], device)

    def _taken(self, i):
        if self.before is None:
            return self._first(i)
        return pltpu.make_async_copy(self.before.at[i], self.first.at[i], self.recv.at[i])

    def _load(self, i):
        at, half = self.at, self.src.shape[1] // 2
        if i < 2:
            src = self.src.at[i * 2 + at.x, pl.ds(0, half), :]
        else:
            src = self.src.at[at.y * 2 + i - 2, pl.ds(half, half), :]
        return pltpu.make_async_copy(src, self.mine.at[i], self.load.at[i])

    def _second(self, j):
        at = self.at
        if j == 0:
            return remote(
                self.mine.at[1 - at.y], self.second.at[0], self.send.at[4], self.recv.at[4], {"batch": at.yn}
            )
        return remote(self.mine.at[3 - at.x], self.second.at[1], self.send.at[5], self.recv.at[5], {"batch": at.xn})

    def _direct(self, off):
        at = self.at
        to = (at.b + off) % at.n
        return remote(self.src.at[to], self.slots.at[off], self.send.at[off], self.recv.at[off], {"batch": to})

    def start(self):
        at = self.at
        if at.square:
            for i in (0, 2, 1, 3):
                self._taken(i).start()
                self._load(i).start()
        else:
            for off in range(1, at.n):
                self._direct(off).start()
            pltpu.make_async_copy(self.src.at[at.b], self.slots.at[0], self.load.at[0]).start()

    def _chunks(self, R, fn):
        step = 16

        @pl.loop(0, R // step)
        def _(i):
            fn(pl.multiple_of(i * step, step), step)

    def second_step(self):
        at = self.at
        if at.square:
            for i in range(4):
                self._load(i).wait()
                if self.before is None:
                    self._first(i).wait_recv()
                else:
                    self._taken(i).wait()
            for j, i in ((0, 1 - at.y), (1, 3 - at.x)):

                def add(r, step, i=i):
                    rows = pl.ds(r, step)
                    self.mine[i, rows, :] = (
                        self.mine[i, rows, :].astype(F32) + self.first[i, rows, :].astype(F32)
                    ).astype(BF16)

                self._chunks(self.mine.shape[1], add)
                self._second(j).start()

    def final(self, put):
        at = self.at
        if at.square:
            half = self.src.shape[1] // 2
            for j, i in ((0, at.y), (1, 2 + at.x)):
                self._second(j).wait_recv()

                def add(r, step, i=i, j=j):
                    rows = pl.ds(r, step)
                    put(
                        pl.ds(r + j * half, step),
                        self.mine[i, rows, :].astype(F32)
                        + self.first[i, rows, :].astype(F32)
                        + self.second[j, rows, :].astype(F32),
                    )

                self._chunks(half, add)
        else:
            pltpu.make_async_copy(self.src.at[at.b], self.slots.at[0], self.load.at[0]).wait()
            for off in range(1, at.n):
                self._direct(off).wait_recv()

            def add(r, step):
                rows = pl.ds(r, step)
                total = self.slots[0, rows, :].astype(F32)
                for off in range(1, at.n):
                    total = total + self.slots[off, rows, :].astype(F32)
                put(rows, total)

            self._chunks(self.src.shape[1], add)

    def finish(self):
        at = self.at
        if at.square:
            for i in range(4 if self.before is None else 0):
                self._first(i).wait_send()
            self._second(0).wait_send()
            self._second(1).wait_send()
        else:
            for off in range(1, at.n):
                self._direct(off).wait_send()


class Names:
    def __init__(self):
        self.shapes = []

    def add(self, shapes):
        start = len(self.shapes)
        self.shapes += list(shapes)
        return slice(start, len(self.shapes))


def chunk_loop(rows, step, fn):
    step = min(step, rows)

    @pl.loop(0, rows // step)
    def _(i):
        fn(pl.ds(pl.multiple_of(i * step, step), step))


def inv_root_of(values):
    return lax.rsqrt(jnp.mean(values * values, axis=-1, keepdims=True) + epsilon)


def far_first(L, z):
    return sorted(range(L), key=lambda zd: (-abs(zd - z), -zd))


class Plan:
    def __init__(self, L, rank, reduces, early, follow, begin, tasks):
        self.L = L
        order = [far_first(L, z) for z in range(L)]
        never = 10**6
        jobs = list(rank)
        ready = {j: [[never] * L for _ in range(L)] for j in reduces}
        own = {j: begin.get(j, never) for j in jobs if j not in reduces}
        arrive = {j: {} for j in jobs}
        sent = {j: set() for j in jobs}
        for j, when in early.items():
            for z in range(L):
                for i in range(L):
                    ready[j][z][order[z][i]] = when[i]
        self.final, self.complete, self.tasks, self.sends = {}, {}, {}, []
        todo = list(tasks)
        total = L * (L - 1) * 2
        last = {j: -1 for j in jobs}
        s = free = 0

        def close():
            for j in jobs:
                if len(sent[j]) == total:
                    if j in reduces and j not in self.final:
                        self.final[j] = max(last[j] + 1, max(ready[j][z][z] for z in range(L)) - 1, s - 1)
                        if j in follow:
                            own[follow[j]] = self.final[j] + 1
                    if j in own and j not in self.complete:
                        self.complete[j] = last[j] + 2

        while any(len(sent[j]) < total for j in jobs) or todo:
            close()
            now = {}
            for z in range(L):
                for way in (1, -1):
                    if not 0 <= z + way < L:
                        continue
                    for j in jobs:
                        best = []
                        for block in range(L):
                            for half in (0, 1):
                                if (z, way, block, half) in sent[j]:
                                    continue
                                came = arrive[j].get((z, way, block, half), never)
                                if j in reduces:
                                    first = not 0 <= z - way < L
                                    if (block - z) * way > 0 and ready[j][z][block] <= s and (first or came + 2 <= s):
                                        best.append((-abs(block - z), half, block))
                                elif (z - block) * way >= 0 and (own[j] <= s if block == z else came + 2 <= s):
                                    best.append((abs(block - z), half, block))
                        if best:
                            _, half, block = min(best)
                            now[(z, way)] = (j, block, half)
                            break
            for (z, way), (j, block, half) in now.items():
                sent[j].add((z, way, block, half))
                arrive[j][(z + way, way, block, half)] = s
                last[j] = s
            self.sends.append(now)
            if todo and s >= free:
                name, needs, makes, i, length = todo[0]
                if all(self.complete.get(j, never) <= s for j in needs):
                    self.tasks[s] = todo.pop(0)
                    free = s + length
                    for j in makes:
                        for z in range(L):
                            ready[j][z][order[z][i]] = s + 2
            s += 1
        close()
        self.jobs, self.reduces, self.order = jobs, reduces, order
        self.ready, self.arrive, self.own = ready, arrive, own
        self.slots = 1 + max(list(self.final.values()) + list(self.complete.values()) + [s + 1 for s in self.tasks])

    def block(self, z, i):
        return pick(z, [self.order[q][i] for q in range(self.L)])


def run_plan(plan, at, jobs, task, after, finish):
    z, L = at.z, at.L
    for s in range(plan.slots):
        now = plan.sends[s] if s < len(plan.sends) else {}
        for q in range(L):
            mine = [(way, now[(q, way)]) for way in (1, -1) if (q, way) in now]
            if mine:

                @pl.when(z == q)
                def _():
                    for way, (j, block, half) in mine:
                        jobs[j].copy(q, way, block, half).start()

        if s in plan.tasks:
            task(plan.tasks[s][0])
        after(s)
        past = plan.sends[s - 1] if 0 <= s - 1 < len(plan.sends) else {}
        for q in range(L):
            came = [(way, past[(q - way, way)]) for way in (1, -1) if (q - way, way) in past]
            adds = []
            for j in plan.reduces:
                for (zq, way, block, half), when in plan.arrive[j].items():
                    if zq == q and block != q and max(when + 1, plan.ready[j][q][block] - 1) == s:
                        adds.append((j, block, half))
            if came or adds:

                @pl.when(z == q)
                def _():
                    for way, (j, block, half) in came:
                        jobs[j].landed(q, way, block, half).wait_recv()
                        if j not in plan.reduces:
                            jobs[j].share(block, half).start()
                    for j, block, half in adds:
                        jobs[j].add(block, half)

        for j, when in plan.final.items():
            if when == s:
                finish(j)


def pick(z, values):
    if len(set(values)) == 1:
        return values[0]
    out = jnp.int32(values[0])
    for i, v in enumerate(values[1:], 1):
        out = jnp.where(z == i, v, out)
    return out


class SlotReduce:
    def __init__(self, at, sib, recv, sems):
        self.at, self.sib, self.recv = at, sib, recv
        self.sib_send, self.sib_recv, self.fwd_send, self.recv_sem = sems
        self.half = sib.shape[1] // 2

    @staticmethod
    def sems(L):
        return [DMA((L,)), DMA((L,)), DMA((L, 2)), DMA((L + 1, 2))]

    @staticmethod
    def bufs(L, T, D):
        return [pltpu.VMEM((L, T, D), BF16), pltpu.VMEM((L + 1, T, D), BF16)]

    def part(self, half):
        return pl.ds(half * self.half, self.half)

    def slot(self, z, way, zd):
        return self.at.L if way < 0 and z == zd else zd

    def copy(self, z, way, zd, half):
        at, part = self.at, self.part(half)
        first = not 0 <= z - way < at.L
        src = (self.sib if first else self.recv).at[zd, part, :]
        slot = self.slot(z + way, way, zd)
        device = {"head": at.up if way > 0 else at.down}
        return remote(src, self.recv.at[slot, part, :], self.fwd_send.at[zd, half], self.recv_sem.at[slot, half], device)

    def landed(self, z, way, zd, half):
        at, part = self.at, self.part(half)
        slot = self.slot(z, way, zd)
        block = self.recv.at[slot, part, :]
        device = {"head": at.down if way > 0 else at.up}
        return remote(block, block, self.fwd_send.at[zd, half], self.recv_sem.at[slot, half], device)

    def exchange(self, zd, src):
        return remote(src, self.sib.at[zd], self.sib_send.at[zd], self.sib_recv.at[zd], {"head": self.at.sib})

    def combine(self, zd, mine):
        def add(rows):
            self.sib[zd, rows, :] = (self.sib[zd, rows, :].astype(F32) + mine[rows, :].astype(F32)).astype(BF16)

        chunk_loop(self.sib.shape[1], 32, add)

    def add(self, zd, half):
        def one(rows):
            self.recv[zd, rows, :] = (self.recv[zd, rows, :].astype(F32) + self.sib[zd, rows, :].astype(F32)).astype(BF16)

        step = min(32, self.half)

        @pl.loop(0, self.half // step)
        def _(i):
            one(pl.ds(pl.multiple_of(half * self.half + i * step, step), step))

    def final(self, put):
        at, z = self.at, self.at.z

        def run(extra):
            def part(rows):
                value = self.sib[z, rows, :].astype(F32)
                for slot in extra:
                    value = value + self.recv[slot, rows, :].astype(F32)
                put(rows, value)

            chunk_loop(self.sib.shape[1], 32, part)

        @pl.when(z == 0)
        def _():
            run((at.L,))

        @pl.when(z == at.L - 1)
        def _():
            run((z,))

        @pl.when((z > 0) & (z < at.L - 1))
        def _():
            run((z, at.L))

    def sent(self):
        at = self.at
        for zd in range(at.L):

            @pl.when(zd != at.z)
            def _():
                for half in (0, 1):
                    block = self.recv.at[zd, self.part(half), :]
                    remote(block, block, self.fwd_send.at[zd, half], self.recv_sem.at[zd, half], {"head": at.up}).wait_send()


class SlotGather:
    def __init__(self, at, own, out, sems):
        self.at, self.own, self.out = at, own, out
        self.line_recv, self.up_send, self.down_send, self.sib_send, self.sib_recv, self.local = sems
        self.half = own.shape[0] // 2

    @staticmethod
    def sems(L):
        return [DMA((L, 2))] * 5 + [DMA]

    def block(self, index, half):
        return self.out.at[index, pl.ds(half * self.half, self.half), :]

    def mine(self, half):
        return self.own.at[pl.ds(half * self.half, self.half), :]

    def copy(self, z, way, zb, half):
        at = self.at
        dst = self.block(zb * 2 + at.c, half)
        src = self.mine(half) if zb == z else dst
        send = (self.up_send if way > 0 else self.down_send).at[zb, half]
        return remote(src, dst, send, self.line_recv.at[zb, half], {"head": at.up if way > 0 else at.down})

    def landed(self, z, way, zb, half):
        at = self.at
        dst = self.block(zb * 2 + at.c, half)
        return remote(dst, dst, self.up_send.at[zb, half], self.line_recv.at[zb, half], {"head": at.down if way > 0 else at.up})

    def share(self, zb, half, src=None):
        at = self.at
        dst = self.block(zb * 2 + at.c, half)
        return remote(dst if src is None else src, dst, self.sib_send.at[zb, half], self.sib_recv.at[zb, half], {"head": at.sib})

    def keep(self):
        return pltpu.make_async_copy(self.own, self.out.at[self.at.h], self.local)

    def begin(self):
        for half in (0, 1):
            self.share(self.at.z, half, self.mine(half)).start()
        self.keep().start()

    def finish(self):
        at = self.at
        self.keep().wait()
        for zb in range(at.L):
            for half in (0, 1):
                self.share(zb, half).wait_send()
                other = self.block(zb * 2 + 1 - at.c, half)
                remote(other, other, self.sib_send.at[zb, half], self.sib_recv.at[zb, half], {"head": at.sib}).wait_recv()

            @pl.when((zb <= at.z) & (at.z < at.L - 1))
            def _():
                for half in (0, 1):
                    self.copy(-1, 1, zb, half).wait_send()

            @pl.when((zb >= at.z) & (at.z > 0))
            def _():
                for half in (0, 1):
                    self.copy(-1, -1, zb, half).wait_send()


def norm_back_part(values, gain, grad):
    inv_root = inv_root_of(values)
    unit = values * inv_root
    weighted = grad * gain
    back = inv_root * (weighted - unit * jnp.mean(weighted * unit, axis=-1, keepdims=True))
    return back, jnp.sum(grad * unit, axis=0, keepdims=True)


def attention_in(n, H, tokens, cotangent, gains, weights, cosine, sine, starts):
    rows, T, D = tokens.shape
    R, W = weights[0].shape
    ff = weights[4].shape[1]
    L = H // 2
    S = H * T
    heads = W // HEAD_DIM
    rank = [("x", r) for r in range(rows)] + [("ct", 0)]
    tasks = []
    for r in range(rows):
        kinds = ("qkv", "low", "high", "terms") if r + 1 < rows else ("qkv", "heads", "terms")
        tasks += [((kind, r), (("x", r),), (), 0, 1) for kind in kinds]
    plan = Plan(L, rank, [], {}, {}, {j: 0 for j in rank}, tasks)
    names = Names()
    z_at = [names.add(SlotGather.sems(L)) for _ in range(rows + 1)]
    w_at = [names.add(BatchGather.sems(n)) for _ in range(6)]
    g_at = names.add([DMA((n,)), DMA((n,)), DMA])
    rest = names.add(
        [
            pltpu.VMEM((rows, T, D), BF16),
            pltpu.VMEM((2, 2, T, D), BF16),
            pltpu.VMEM((2, 2, T, D), BF16),
            pltpu.VMEM((D, 3 * W), BF16),
            pltpu.VMEM((D, W), BF16),
            DMA((2,)),
            DMA((2,)),
            DMA((2,)),
        ]
    )
    wide = min(512, D)

    def kernel(
        tok,
        ct,
        gain,
        cos,
        sin,
        st,
        wq,
        wk,
        wv,
        wo,
        wg,
        wu,
        attn_in,
        ct_first,
        w_qkv,
        w_o,
        w_gu,
        terms,
        gains_full,
        qkv,
        lse,
        attended,
        *scratch,
    ):
        at = Place(n, H)
        normed, xb, stage, wqkv, wout, x_sem, o_sem, w_sem = scratch[rest]
        gsend, grecv, glocal = scratch[g_at]
        at.greet()

        def gain_dst(b):
            return gains_full.at[:, pl.ds(pl.multiple_of(b * R, R), R)]

        mine = pltpu.make_async_copy(gain, gain_dst(at.b), glocal)
        mine.start()
        if at.square:
            first = remote(gain, gain_dst(at.b), gsend.at[0], grecv.at[0], {"batch": at.xn})
            own_y = remote(gain, gain_dst(at.b), gsend.at[1], grecv.at[1], {"batch": at.yn})
            first.start()
            own_y.start()
            got = gain_dst(at.xn)
            remote(got, got, gsend.at[0], grecv.at[0], {"batch": at.xn}).wait_recv()
            fwd = remote(got, got, gsend.at[2], grecv.at[2], {"batch": at.yn})
            fwd.start()
            got = gain_dst(at.yn)
            remote(got, got, gsend.at[1], grecv.at[1], {"batch": at.yn}).wait_recv()
            got = gain_dst(at.dg)
            remote(got, got, gsend.at[2], grecv.at[2], {"batch": at.yn}).wait_recv()
            for job in (first, own_y, fwd):
                job.wait_send()
        else:
            for o in range(1, n):
                remote(gain, gain_dst(at.b), gsend.at[o], grecv.at[o], {"batch": (at.b + o) % n}).start()
            for o in range(1, n):
                got = gain_dst((at.b + n - o) % n)
                remote(got, got, gsend.at[o], grecv.at[o], {"batch": (at.b + o) % n}).wait()
        mine.wait()

        gathers = {("x", r): SlotGather(at, normed.at[r], attn_in.at[r], scratch[z_at[r]]) for r in range(rows)}
        gathers[("ct", 0)] = SlotGather(at, ct.at[0], ct_first, scratch[z_at[rows]])

        def norm(r):
            def one(part):
                values = tok[r, part, :].astype(F32)
                normed[r, part, :] = (values * inv_root_of(values) * gains_full[0:1, :]).astype(BF16)

            chunk_loop(T, 32, one)
            gathers[("x", r)].begin()

        outs = []
        for src, dst, col, width in (
            (wq, w_qkv, 0, W),
            (wk, w_qkv, W, W),
            (wv, w_qkv, 2 * W, W),
            (wo, w_o, 0, W),
            (wg, w_gu, 0, ff),
            (wu, w_gu, ff, ff),
        ):
            outs.append((src, lambda b, part, dst=dst, col=col, width=width: dst.at[b, part, pl.ds(col, width)]))
        shards = [BatchGather(at, src, out, scratch[w_at[i]]) for i, (src, out) in enumerate(outs)]
        for job in shards[:4]:
            job.start()
        for r in range(rows):
            norm(r)
        gathers[("ct", 0)].begin()

        def weight_loads():
            return [
                pltpu.make_async_copy(w_qkv.at[b], wqkv.at[pl.ds(b * R, R), :], w_sem.at[0]) for b in range(n)
            ] + [pltpu.make_async_copy(w_o.at[b], wout.at[pl.ds(b * R, R), :], w_sem.at[1]) for b in range(n)]

        def x_load(r, b):
            return pltpu.make_async_copy(attn_in.at[r, pl.ds(2 * b, 2)], xb.at[b % 2], x_sem.at[b % 2])

        def make_qkv(r):
            gathers[("x", r)].finish()
            x_load(r, 0).start()
            x_load(r, 1).start()
            if r == 0:
                pltpu.make_async_copy(wqkv, wqkv, w_sem.at[0]).wait()
                pltpu.make_async_copy(wout, wout, w_sem.at[1]).wait()
            for b in range(L):
                x_load(r, b).wait()
                part = pl.ds(b * 2 * T, 2 * T)
                lin = jnp.dot(xb[b % 2].reshape(2 * T, D), wqkv[...], preferred_element_type=F32)
                if b + 2 < L:
                    x_load(r, b + 2).start()
                c, s = cos[r, part, :], sin[r, part, :]
                qkv[r, part, 0:W] = rotate(lin[:, :W], c, s).astype(BF16)
                qkv[r, part, W : 2 * W] = rotate(lin[:, W : 2 * W], c, s).astype(BF16)
                qkv[r, part, 2 * W : 3 * W] = lin[:, 2 * W :].astype(BF16)

        def head(r, h):
            attend(qkv.at[r], st.at[r], lse.at[r], attended.at[r], h, W)

        def store(r, b):
            return pltpu.make_async_copy(stage.at[b % 2], terms.at[r, pl.ds(2 * b, 2)], o_sem.at[b % 2])

        def make_terms(r):
            for b in range(L):
                if b >= 2:
                    store(r, b - 2).wait()
                for j in range(D // wide):
                    cols = pl.ds(j * wide, wide)
                    value = cols_dot(attended[r, pl.ds(b * 2 * T, 2 * T), :], wout[cols, :]).astype(BF16)
                    stage[b % 2, 0, :, cols] = value[:T]
                    stage[b % 2, 1, :, cols] = value[T:]
                store(r, b).start()
            for b in (L - 2, L - 1):
                store(r, b).wait()

        def task(name):
            kind, r = name
            if kind == "qkv":
                make_qkv(r)
            elif kind == "low":
                pl.loop(0, heads // 2)(lambda h: head(r, h))
            elif kind == "high":
                pl.loop(heads // 2, heads)(lambda h: head(r, h))
            elif kind == "heads":
                pl.loop(0, heads)(lambda h: head(r, h))
            else:
                make_terms(r)

        def after(s):
            if s == 3:
                for job in shards[:4]:
                    job.forward()
                for job in shards[4:]:
                    job.start()
            if s == 6:
                for job in shards[:4]:
                    job.finish()
                for job in weight_loads():
                    job.start()
            if s == 11:
                shards[4].forward()
            if s == 15:
                shards[5].forward()

        run_plan(plan, at, gathers, task, after, None)
        gathers[("ct", 0)].finish()
        for job in shards[4:]:
            job.finish()

    return pl.pallas_call(
        kernel,
        out_shape=(
            jax.ShapeDtypeStruct((rows, H, T, D), BF16),
            jax.ShapeDtypeStruct((H, T, D), BF16),
            jax.ShapeDtypeStruct((n, R, 3 * W), BF16),
            jax.ShapeDtypeStruct((n, R, W), BF16),
            jax.ShapeDtypeStruct((n, R, 2 * ff), BF16),
            jax.ShapeDtypeStruct((rows, H, T, D), BF16),
            jax.ShapeDtypeStruct((8, D), F32),
            jax.ShapeDtypeStruct((rows, S, 3 * W), BF16),
            jax.ShapeDtypeStruct((rows, 8, S), F32),
            jax.ShapeDtypeStruct((rows, S, W), BF16),
        ),
        in_specs=[VMEM, ANY] + [VMEM] * 4 + [ANY] * 6,
        out_specs=(ANY,) * 6 + (VMEM,) * 4,
        scratch_shapes=names.shapes,
        compiler_params=pltpu.CompilerParams(collective_id=1, has_side_effects=True, vmem_limit_bytes=VMEM_LIMIT),
        name="attention_in",
    )(tokens, cotangent, gains, cosine, sine, starts, *weights)


def feed_forward(n, H, terms, ct_first, tokens, cotangent, gains, w_gu, w_d):
    rows, T, D = tokens.shape
    L = H // 2
    ff = w_d.shape[1]
    S = H * T
    R = w_d.shape[0]
    U = R // 2
    square = n == 4
    rank = []
    for kinds in (("mix", "in"), ("sum", "att"), ("out",)):
        rank += [(kind, r) for r in range(rows) for kind in kinds]
    rank[2:2] = [("ct", r) for r in range(1, rows)]
    tasks = []
    for r in range(rows):
        for i in range(L):
            tasks.append((("first", r, i), (("in", r),) + ((("ct", r),) if r else ()), (), i, 1))
            tasks.append((("second", r, i), (), (("sum", r), ("out", r)), i, 1))
    tasks += [(("grad", k, 0), (), (), 0, 1) for k in range(2 * n)]
    plan = Plan(
        L,
        rank,
        [j for j in rank if j[0] in ("mix", "sum", "out")],
        {("mix", r): [r * L + i for i in range(L)] for r in range(rows)},
        {(a, r): (b, r) for a, b in (("mix", "in"), ("sum", "att")) for r in range(rows)},
        {("ct", r): 0 for r in range(1, rows)},
        tasks,
    )
    names = Names()
    n_bufs = [names.add(SlotReduce.bufs(L, T, D)) for _ in range(2 * rows)]
    n_sems = [names.add(SlotReduce.sems(L)) for _ in range(2 * rows)]
    n_gsem = [names.add(SlotGather.sems(L)) for _ in range(2 * rows)]
    n_wsem = names.add(BatchGather.sems(n))
    rest = names.add(
        [
            pltpu.VMEM((rows, T, D), BF16),
            pltpu.VMEM((rows, T, D), BF16),
            pltpu.VMEM((rows, T, D), F32),
            pltpu.VMEM((2, 2, T, D), BF16),
            pltpu.VMEM((2, 2, T, D), BF16),
            pltpu.VMEM((max(D, rows * S), 2 * ff), BF16),
            pltpu.VMEM((max(D, rows * S), ff), BF16),
            pltpu.VMEM((2, 2, T, D), BF16),
            pltpu.VMEM((2, 2, T, D), BF16),
            pltpu.VMEM((2, max(2 * T, U), ff), BF16),
            pltpu.VMEM((2, max(2 * T, U), 2 * ff), BF16),
            pltpu.VMEM((2, rows, H, T, U), BF16),
            pltpu.VMEM((2, rows, H, T, U), BF16),
            DMA((6,)),
            DMA((2, 4)),
            DMA((2, 4)),
            DMA((2,)),
            DMA((rows, L)),
            DMA((2,)),
            DMA((2,)),
            DMA((2,)),
            DMA((2,)),
        ]
    )
    tile = min(256, ff)
    wide = min(512, D)

    def kernel(
        src,
        ct_row,
        tok,
        ct,
        gain,
        wgu_hbm,
        wd_own,
        ctf,
        mlp_in,
        g_att,
        hid_hbm,
        ggu_hbm,
        grad_gu,
        grad_d,
        first_gu,
        first_d,
        g_mixed,
        layer_out,
        gain_sum,
        *scratch,
    ):
        at = Place(n, H)
        z = at.z
        (
            normed,
            att,
            mixed,
            stage_g,
            stage_o,
            wgu,
            wd,
            xb,
            cb,
            hb,
            gb,
            xt,
            ct_t,
            t_sem,
            gsend,
            grecv,
            w_sem,
            own_sem,
            x_sem,
            c_sem,
            h_sem,
            g_sem,
        ) = scratch[rest]
        loads = [pltpu.make_async_copy(wgu_hbm, wgu.at[pl.ds(0, D), :], w_sem.at[0])]
        down = BatchGather(
            at,
            wd_own,
            lambda b, part: wd.at[pl.ds(pl.multiple_of(b * R + part.start, U), part.size), :],
            scratch[n_wsem],
        )
        red, gat = {}, {}
        for r in range(rows):
            for kind in ("mix", "sum"):
                red[(kind, r)] = SlotReduce(at, *scratch[n_bufs[r]], scratch[n_sems[r]])
            red[("out", r)] = SlotReduce(at, *scratch[n_bufs[rows + r]], scratch[n_sems[rows + r]])
            gat[("in", r)] = SlotGather(at, normed.at[r], mlp_in.at[r], scratch[n_gsem[r]])
            gat[("att", r)] = SlotGather(at, att.at[r], g_att.at[r], scratch[n_gsem[r]])
            if r:
                gat[("ct", r)] = SlotGather(at, ct.at[r], ctf.at[r - 1], scratch[n_gsem[rows + r]])
        both = {**red, **gat}
        at.greet()
        down.start()

        def mine_of(r, zd):
            return red[("out", r)].recv.at[zd]

        def own_load(r, zd):
            return pltpu.make_async_copy(src.at[r, zd * 2 + at.c], mine_of(r, zd), own_sem.at[r, zd])

        def exchange(r, zd):
            return red[("mix", r)].exchange(zd, src.at[r, zd * 2 + 1 - at.c])

        for r in range(rows):
            for i in range(L):
                zd = plan.block(z, i)
                exchange(r, zd).start()
                own_load(r, zd).start()
        for r in range(1, rows):
            gat[("ct", r)].begin()
        for job in loads:
            job.start()
        gain_sum[...] = jnp.zeros_like(gain_sum)

        def combine_mix(r, i):
            zd = plan.block(z, i)
            own_load(r, zd).wait()
            exchange(r, zd).wait()
            red[("mix", r)].combine(zd, mine_of(r, zd))

        def combine_terms(r, i):
            zd = plan.block(z, i)
            for kind, stage in (("sum", stage_g), ("out", stage_o)):
                job = red[(kind, r)]
                job.exchange(zd, stage.at[i % 2, 1 - at.c]).wait()
                job.combine(zd, stage.at[i % 2, at.c])

        def x_load(r, i):
            blk = plan.block(z, i)
            return (
                pltpu.make_async_copy(mlp_in.at[r, pl.ds(2 * blk, 2)], xb.at[i % 2], x_sem.at[i % 2]),
                pltpu.make_async_copy(
                    (ctf.at[r - 1] if r else ct_row).at[pl.ds(2 * blk, 2)], cb.at[i % 2], c_sem.at[i % 2]
                ),
            )

        def act_store(r, i):
            blk = plan.block(z, i)
            at_row = pl.ds(pl.multiple_of(r * S + blk * 2 * T, 2 * T), 2 * T)
            return (
                pltpu.make_async_copy(hb.at[i % 2, pl.ds(0, 2 * T), :], hid_hbm.at[at_row, :], h_sem.at[i % 2]),
                pltpu.make_async_copy(gb.at[i % 2, pl.ds(0, 2 * T), :], ggu_hbm.at[at_row, :], g_sem.at[i % 2]),
            )

        def first_part(r, i):
            if i == 0:
                gat[("in", r)].finish()
                if r:
                    gat[("ct", r)].finish()
                for job in x_load(r, 0):
                    job.start()
                if r == 0:
                    down.finish()
                    for job in loads:
                        job.wait()
            for job in x_load(r, i):
                job.wait()
            if i + 1 < L:
                for job in x_load(r, i + 1):
                    job.start()
            if r * L + i >= 2:
                before = (r, i - 2) if i >= 2 else (r - 1, L + i - 2)
                for job in act_store(*before):
                    job.wait()
            k = i % 2

            @pl.loop(0, ff // tile)
            def _(j):
                cols = pl.ds(pl.multiple_of(j * tile, tile), tile)
                up_cols = pl.ds(pl.multiple_of(ff + j * tile, tile), tile)
                x = xb[k].reshape(2 * T, D)
                gate = jnp.dot(x, wgu[0:D, cols], preferred_element_type=F32)
                up = jnp.dot(x, wgu[0:D, up_cols], preferred_element_type=F32)
                back = jnp.dot(cb[k].reshape(2 * T, D), wd[0:D, cols], preferred_element_type=F32)
                sig = 1.0 / (1.0 + jnp.exp(-gate))
                silu = gate * sig
                hb[k, 0 : 2 * T, cols] = (silu * up).astype(BF16)
                gb[k, 0 : 2 * T, cols] = (back * up * (sig * (1.0 + gate * (1.0 - sig)))).astype(BF16)
                gb[k, 0 : 2 * T, up_cols] = (back * silu).astype(BF16)

            for job in act_store(r, i):
                job.start()

        def second_part(r, i):
            k = i % 2

            @pl.loop(0, D // wide)
            def _(j):
                cols = pl.ds(pl.multiple_of(j * wide, wide), wide)
                back = cols_dot(gb[k, 0 : 2 * T, :], wgu[cols, :]).astype(BF16)
                stage_g[k, 0, :, cols] = back[:T]
                stage_g[k, 1, :, cols] = back[T:]
                out = cols_dot(hb[k, 0 : 2 * T, :], wd[cols, :]).astype(BF16)
                stage_o[k, 0, :, cols] = out[:T]
                stage_o[k, 1, :, cols] = out[T:]

            zd = plan.block(z, i)
            for kind, stage in (("sum", stage_g), ("out", stage_o)):
                red[(kind, r)].exchange(zd, stage.at[k, 1 - at.c]).start()

        def finish_mix(r):
            def put(part, value):
                value = value + tok[r, part, :].astype(F32)
                mixed[r, part, :] = value
                normed[r, part, :] = (value * inv_root_of(value) * gain[1:2, :]).astype(BF16)

            red[("mix", r)].final(put)
            red[("mix", r)].sent()
            gat[("in", r)].begin()

        def finish_sum(r):
            def put(part, value):
                back, gain_part = norm_back_part(mixed[r, part, :], gain[1:2, :], value)
                total = ct[r, part, :].astype(F32) + back
                g_mixed[r, part, :] = total
                att[r, part, :] = total.astype(BF16)
                gain_sum[1:2, :] += gain_part

            red[("sum", r)].final(put)
            red[("sum", r)].sent()
            gat[("att", r)].begin()

        def finish_out(r):
            def put(part, value):
                layer_out[r, part, :] = (mixed[r, part, :] + value).astype(BF16)

            red[("out", r)].final(put)
            red[("out", r)].sent()

        units = send_units(at, square, n)
        again = [
            pltpu.make_async_copy(ggu_hbm, wgu.at[pl.ds(0, rows * S), :], w_sem.at[0]),
            pltpu.make_async_copy(hid_hbm, wd.at[pl.ds(0, rows * S), :], w_sem.at[1]),
        ]

        def columns(k):
            cols = pl.ds(pl.multiple_of((units[k][0] * 2 + units[k][1]) * U, U), U)
            return [
                pltpu.make_async_copy(mlp_in.at[:, :, :, cols], xt.at[k % 2], t_sem.at[k % 2]),
                pltpu.make_async_copy(ct_row.at[:, :, cols], ct_t.at[k % 2, 0], t_sem.at[2 + k % 2]),
                pltpu.make_async_copy(
                    ctf.at[:, :, :, cols], ct_t.at[k % 2, pl.ds(1, rows - 1)], t_sem.at[4 + k % 2]
                ),
            ]

        def grad_store(k):
            b, half = units[k][:2]
            part = pl.ds(half * U, U)
            return [
                pltpu.make_async_copy(hb.at[k % 2, pl.ds(0, U), :], grad_d.at[b, part, :], h_sem.at[k % 2]),
                pltpu.make_async_copy(gb.at[k % 2, pl.ds(0, U), :], grad_gu.at[b, part, :], g_sem.at[k % 2]),
            ]

        def grad_sends(k):
            b, half, slot, to = units[k]
            part = pl.ds(half * U, U)
            return [
                remote(src.at[b, part, :], dst.at[slot], gsend.at[a, k], grecv.at[a, slot], {"batch": to})
                for a, (src, dst) in enumerate(((grad_d, first_d), (grad_gu, first_gu)))
            ]

        def prepare_grads():
            for i in (L - 2, L - 1):
                for job in act_store(rows - 1, i):
                    job.wait()
            for job in again + columns(0):
                job.start()

        def grad(k):
            if k == 0:
                for job in again:
                    job.wait()
            for job in columns(k):
                job.wait()
            if k + 1 < 2 * n:
                for job in columns(k + 1):
                    job.start()
            ring = k % 2

            @pl.loop(0, 2 * ff // tile)
            def _(j):
                cols = pl.ds(pl.multiple_of(j * tile, tile), tile)
                x = xt[ring].reshape(rows * S, U)
                gb[ring, 0:U, cols] = rows_dot(x, wgu[0 : rows * S, cols]).astype(BF16)

            @pl.loop(0, ff // tile)
            def _(j):
                cols = pl.ds(pl.multiple_of(j * tile, tile), tile)
                x = ct_t[ring].reshape(rows * S, U)
                hb[ring, 0:U, cols] = rows_dot(x, wd[0 : rows * S, cols]).astype(BF16)

            for job in grad_store(k):
                job.start()

        def task(name):
            kind, r, i = name
            if kind == "first":
                first_part(r, i)
            elif kind == "second":
                second_part(r, i)
                if (r, i) == (rows - 1, L - 1):
                    prepare_grads()
            else:
                grad(r)

        def after(s):
            if s == 7:
                down.forward()
            if s + 1 < rows * L:
                combine_mix((s + 1) // L, (s + 1) % L)
            name = plan.tasks[s - 1][0] if s - 1 in plan.tasks else None
            if name and name[0] == "second":
                combine_terms(*name[1:])
            if name and name[0] == "grad":
                for job in grad_store(name[1]):
                    job.wait()
                if units[name[1]][3] is not None:
                    for job in grad_sends(name[1]):
                        job.start()

        def finish(j):
            {"mix": finish_mix, "sum": finish_sum, "out": finish_out}[j[0]](j[1])

        combine_mix(0, 0)
        run_plan(plan, at, both, task, after, finish)
        if square:
            for k in range(4):
                for job in grad_sends(k):
                    job.wait()
        for r in range(rows):
            gat[("att", r)].finish()

    return pl.pallas_call(
        kernel,
        out_shape=(
            jax.ShapeDtypeStruct((rows - 1, H, T, D), BF16),
            jax.ShapeDtypeStruct((rows, H, T, D), BF16),
            jax.ShapeDtypeStruct((rows, H, T, D), BF16),
            jax.ShapeDtypeStruct((rows * S, ff), BF16),
            jax.ShapeDtypeStruct((rows * S, 2 * ff), BF16),
            jax.ShapeDtypeStruct((n, 2 * U, 2 * ff), BF16),
            jax.ShapeDtypeStruct((n, 2 * U, ff), BF16),
            jax.ShapeDtypeStruct((4, U, 2 * ff), BF16),
            jax.ShapeDtypeStruct((4, U, ff), BF16),
            jax.ShapeDtypeStruct((rows, T, D), F32),
            jax.ShapeDtypeStruct((rows, T, D), BF16),
            jax.ShapeDtypeStruct((8, D), F32),
        ),
        in_specs=[ANY, ANY, VMEM, VMEM, VMEM, ANY, ANY],
        out_specs=(ANY,) * 9 + (VMEM, VMEM, VMEM),
        scratch_shapes=names.shapes,
        compiler_params=pltpu.CompilerParams(collective_id=2, has_side_effects=True, vmem_limit_bytes=VMEM_LIMIT),
        name="feed_forward",
    )(terms, ct_first, tokens, cotangent, gains, w_gu, w_d)


class LateReduce:
    def __init__(self, at, src, first, bufs, sems):
        self.at, self.src, self.first = at, src, first
        self.mine, self.came, self.second = bufs
        self.load, self.send, self.recv = sems
        self.U = first.shape[1]

    @staticmethod
    def bufs(U, K):
        return [pltpu.VMEM((2, U, K), BF16)] * 3

    @staticmethod
    def sems():
        return [DMA((4,)), DMA((2,)), DMA((2,))]

    def loads(self, j, own):
        at, U = self.at, self.U
        if j == 0:
            y = at.y if own else 1 - at.y
            b, slot = y * 2 + at.x, y
        else:
            x = at.x if own else 1 - at.x
            b, slot = at.y * 2 + x, 2 + x
        return [
            pltpu.make_async_copy(self.src.at[b, pl.ds(j * U, U), :], self.mine.at[j], self.load.at[2 * j]),
            pltpu.make_async_copy(self.first.at[slot], self.came.at[j], self.load.at[2 * j + 1]),
        ]

    def pass_on(self, j):
        to = {"batch": self.at.xn if j else self.at.yn}
        return remote(self.mine.at[j], self.second.at[j], self.send.at[j], self.recv.at[j], to)

    def start(self):
        for j in (0, 1):
            for job in self.loads(j, False):
                job.start()

    def second_step(self):
        for j in (0, 1):
            for job in self.loads(j, False):
                job.wait()

            def add(rows, j=j):
                self.mine[j, rows, :] = (self.mine[j, rows, :].astype(F32) + self.came[j, rows, :].astype(F32)).astype(BF16)

            chunk_loop(self.U, 16, add)
            self.pass_on(j).start()

    def reload(self):
        for j in (0, 1):
            self.pass_on(j).wait()
            for job in self.loads(j, True):
                job.start()

    def final(self, j, step, put):
        for job in self.loads(j, True):
            job.wait()

        @pl.loop(0, self.U // step)
        def _(i):
            rows = pl.ds(pl.multiple_of(i * step, step), step)
            put(
                i,
                self.mine[j, rows, :].astype(F32) + self.came[j, rows, :].astype(F32) + self.second[j, rows, :].astype(F32),
            )


def send_units(at, square, n):
    if not square:
        return [(k // 2, k % 2, None, None) for k in range(2 * n)]
    return [
        ((1 - at.y) * 2 + 1 - at.x, 0, 1 - at.y, at.xn),
        ((1 - at.y) * 2 + 1 - at.x, 1, 3 - at.x, at.yn),
        (at.y * 2 + 1 - at.x, 0, at.y, at.xn),
        ((1 - at.y) * 2 + at.x, 1, 2 + at.x, at.yn),
        ((1 - at.y) * 2 + at.x, 0, None, None),
        (at.y * 2 + 1 - at.x, 1, None, None),
        (at.b, 0, None, None),
        (at.b, 1, None, None),
    ]


def attention_back(
    n,
    H,
    g_att,
    attended,
    qkv,
    lse,
    attn_in,
    w_qkv,
    w_o,
    cosine,
    sine,
    starts,
    tokens,
    g_mixed,
    gains,
    gain_sum,
    g_gu,
    g_d,
    first_gu,
    first_d,
):
    rows, T, D = tokens.shape
    L = H // 2
    S = H * T
    R, ff = g_d.shape[1], g_d.shape[2]
    W = w_o.shape[1]
    heads = W // HEAD_DIM
    U = R // 2
    square = n == 4
    step = min(256, S)
    wide = min(512, D)
    blocks = S // step
    rank = [("in", r) for r in range(rows)]
    tasks = []
    for r in range(rows):
        tasks.append((("prob", r, 0), (), (), 0, 1))
        if r == 0:
            tasks.append((("heads", r, 0), (), (), 0, 1))
        else:
            tasks += [(("head", r, h), (), (), 0, 1) for h in range(heads)]
        tasks += [(("terms", r, i), (), (("in", r),), i, 1) for i in range(L)]
    tasks += [(("grad", k, 0), (), (), 0, 1) for k in range(n)]
    plan = Plan(L, rank, rank, {}, {}, {}, tasks)
    names = Names()
    r_bufs = [names.add(SlotReduce.bufs(L, T, D)) for _ in range(rows)]
    r_sems = [names.add(SlotReduce.sems(L)) for _ in range(rows)]
    if square:
        m_bufs = [names.add(LateReduce.bufs(U, K)) for K in (ff, 2 * ff)]
        m_sems = [names.add(LateReduce.sems()) for _ in range(2)]
        a_bufs = names.add([pltpu.VMEM((4, U, 4 * W), BF16), pltpu.VMEM((2, U, 4 * W), BF16)])
        a_sems = names.add([DMA((6,)), DMA((6,))])
    else:
        m_bufs = [names.add(BatchReduce.bufs(n, R, K)) for K in (ff, 2 * ff)]
        m_sems = [names.add(BatchReduce.sems(n)) for _ in range(2)]
        a_bufs = names.add([pltpu.VMEM((n, 2, U, 4 * W), BF16)])
        a_sems = names.add([DMA((n,)), DMA((n,))])
    s_at = names.add(
        [pltpu.VMEM((8, D), F32), pltpu.VMEM((n, 8, R), F32), pltpu.VMEM((H, 8, R), F32)]
        + [DMA((n,)), DMA((n,)), DMA((H,)), DMA((H,)), DMA]
    )
    rest = names.add(
        [
            pltpu.VMEM((2, step, D), BF16),
            pltpu.VMEM((S, W), BF16),
            pltpu.VMEM((S, W), F32),
            pltpu.VMEM((S, W), F32),
            pltpu.VMEM((S, W), F32),
            pltpu.VMEM((rows * S, 3 * W), BF16),
            pltpu.VMEM((2, 2, T, D), BF16),
            pltpu.VMEM((2, rows * S, U), BF16),
            pltpu.VMEM((2, rows * S, U), BF16),
            pltpu.VMEM((2 * n, U, 4 * W), BF16),
            pltpu.VMEM((4, 32, 2 * ff), F32),
            DMA((2,)),
            DMA((4,)),
            DMA((4, 2)),
            DMA,
        ]
    )

    def kernel(
        ga,
        att,
        qkv,
        ls,
        x_hbm,
        wq,
        wo,
        cos,
        sin,
        st,
        tok,
        gmix,
        gain,
        gain_in,
        ggu,
        gd,
        fgu,
        fd,
        grad_in,
        out_q,
        out_k,
        out_v,
        out_o,
        ggate,
        gup,
        gdown,
        gain_out,
        *scratch,
    ):
        at = Place(n, H)
        z = at.z
        small, over_batch, over_head, bsend, brecv, hsend, hrecv, local = scratch[s_at]
        gab, gat, gq, gk, gv, gqkv, stage, xt, gt, units_buf, out_buf, ga_sem, t_sem, o_sem, mix_sem = scratch[rest]
        sums = {("in", r): SlotReduce(at, *scratch[r_bufs[r]], scratch[r_sems[r]]) for r in range(rows)}
        asend, arecv = scratch[a_sems]
        units = send_units(at, square, n)
        take_mix = pltpu.make_async_copy(gmix, grad_in, mix_sem)
        take_mix.start()

        def ga_load(g):
            return pltpu.make_async_copy(
                ga.at[g // blocks, pl.ds(g % blocks * step, step), :], gab.at[g % 2], ga_sem.at[g % 2]
            )

        ga_load(0).start()
        ga_load(1).start()
        at.greet(all_heads=True)
        if square:
            mlp = [
                LateReduce(at, src, first, scratch[m_bufs[i]], scratch[m_sems[i]])
                for i, (src, first) in enumerate(((gd, fd), (ggu, fgu)))
            ]
        else:
            mlp = [BatchReduce(at, src, scratch[m_bufs[i]], scratch[m_sems[i]]) for i, src in enumerate((gd, ggu))]
        for job in mlp:
            job.start()
        small[...] = gain_in[...]
        for job in mlp:
            job.second_step()

        def prob(r):
            gq[...] = jnp.zeros_like(gq)
            gk[...] = jnp.zeros_like(gk)
            gv[...] = jnp.zeros_like(gv)
            for b in range(blocks):
                g = r * blocks + b
                ga_load(g).wait()
                gat[b * step : (b + 1) * step, :] = jnp.dot(gab[g % 2], wo[...], preferred_element_type=F32).astype(BF16)
                if g + 2 < rows * blocks:
                    ga_load(g + 2).start()

        def head(r, h):
            attend_back(qkv.at[r], st.at[r], ls.at[r], gat, gq, gk, gv, h, W)

        def terms(r, i):
            zd = plan.block(z, i)
            k = i % 2
            part = pl.ds(pl.multiple_of(zd * 2 * T, 2 * T), 2 * T)
            c, s = cos[r, part, :], -sin[r, part, :]
            keep = pl.ds(pl.multiple_of(r * S + zd * 2 * T, 2 * T), 2 * T)
            gqkv[keep, 0:W] = rotate(gq[part, :], c, s).astype(BF16)
            gqkv[keep, W : 2 * W] = rotate(gk[part, :], c, s).astype(BF16)
            gqkv[keep, 2 * W : 3 * W] = gv[part, :].astype(BF16)

            @pl.loop(0, D // wide)
            def _(j):
                cols = pl.ds(pl.multiple_of(j * wide, wide), wide)
                back = cols_dot(gqkv[keep, :], wq[cols, :]).astype(BF16)
                stage[k, 0, :, cols] = back[:T]
                stage[k, 1, :, cols] = back[T:]

            sums[("in", r)].exchange(zd, stage.at[k, 1 - at.c]).start()

        def combine_terms(r, i):
            zd = plan.block(z, i)
            job = sums[("in", r)]
            job.exchange(zd, stage.at[i % 2, 1 - at.c]).wait()
            job.combine(zd, stage.at[i % 2, at.c])

        def columns(k):
            cols = pl.ds(pl.multiple_of((units[k][0] * 2 + units[k][1]) * U, U), U)
            return [pltpu.make_async_copy(x_hbm.at[:, cols], xt.at[k % 2], t_sem.at[k % 2])] + [
                pltpu.make_async_copy(
                    ga.at[r, :, cols], gt.at[k % 2, pl.ds(r * S, S), :], t_sem.at[2 + k % 2]
                )
                for r in range(rows)
            ]

        def columns_wait(k):
            pltpu.make_async_copy(xt.at[k % 2], xt.at[k % 2], t_sem.at[k % 2]).wait()
            pltpu.make_async_copy(gt.at[k % 2], gt.at[k % 2], t_sem.at[2 + k % 2]).wait()

        def grad(k):
            if k == 0:
                for job in columns(0):
                    job.start()
            columns_wait(k)
            if k + 1 < 2 * n:
                for job in columns(k + 1):
                    job.start()
            units_buf[k, :, 0 : 3 * W] = rows_dot(xt[k % 2], gqkv[...]).astype(BF16)
            units_buf[k, :, 3 * W : 4 * W] = rows_dot(gt[k % 2], att[...].reshape(rows * S, W)).astype(BF16)
            if units[k][3] is not None:
                unit_send(k).start()

        if square:
            a_first, a_second = scratch[a_bufs]

            def unit_send(k):
                _, _, slot, to = units[k]
                return remote(units_buf.at[k], a_first.at[slot], asend.at[k], arecv.at[slot], {"batch": to})

            def unit_pass(j):
                to = at.xn if j else at.yn
                return remote(units_buf.at[4 + j], a_second.at[j], asend.at[4 + j], arecv.at[4 + j], {"batch": to})

            def unit_second():
                for j, k, slot in ((0, 0, 1 - at.y), (1, 1, 3 - at.x)):
                    unit_send(k).wait_recv()

                    def add(part, j=j, slot=slot):
                        units_buf[4 + j, part, :] = (
                            units_buf[4 + j, part, :].astype(F32) + a_first[slot, part, :].astype(F32)
                        ).astype(BF16)

                    chunk_loop(U, 16, add)
                    unit_pass(j).start()

            def unit_final(put):
                for j, k, slot in ((0, 2, at.y), (1, 3, 2 + at.x)):
                    unit_send(k).wait_recv()
                    unit_pass(j).wait_recv()

                    @pl.loop(0, U // 16)
                    def _(i, j=j, slot=slot):
                        r = pl.multiple_of(i * 16, 16)
                        part = pl.ds(r, 16)
                        put(
                            pl.ds(r + j * U, 16),
                            units_buf[6 + j, part, :].astype(F32)
                            + a_first[slot, part, :].astype(F32)
                            + a_second[j, part, :].astype(F32),
                        )

                for k in range(4):
                    unit_send(k).wait_send()
                for j in (0, 1):
                    unit_pass(j).wait_send()

        else:
            (a_slots,) = scratch[a_bufs]

            def unit_direct(off):
                to = (at.b + off) % n
                return remote(
                    units_buf.at[pl.ds(2 * to, 2)], a_slots.at[off], asend.at[off], arecv.at[off], {"batch": to}
                )

            def unit_second():
                for off in range(1, n):
                    unit_direct(off).start()

            def unit_final(put):
                for off in range(1, n):
                    unit_direct(off).wait()
                for j in (0, 1):

                    @pl.loop(0, U // 16)
                    def _(i, j=j):
                        r = pl.multiple_of(i * 16, 16)
                        part = pl.ds(r, 16)
                        total = units_buf[2 * at.b + j, part, :].astype(F32)
                        for off in range(1, n):
                            total = total + a_slots[off, j, part, :].astype(F32)
                        put(pl.ds(r + j * U, 16), total)

        def finish(j):
            r = j[1]

            def put(part, value):
                back, gain_part = norm_back_part(tok[r, part, :].astype(F32), gain[0:1, :], value)
                grad_in[r, part, :] += back
                small[0:1, :] += gain_part

            sums[j].final(put)
            sums[j].sent()

        def task(name):
            kind, r, i = name
            if kind == "prob":
                prob(r)
                if r == 0:
                    take_mix.wait()
            elif kind == "heads":
                pl.loop(0, heads)(lambda h: head(r, h))
            elif kind == "head":
                head(r, i)
            elif kind == "terms":
                terms(r, i)
            else:
                grad(2 * r)
                grad(2 * r + 1)

        def out_copies(outs, r, ring, step):
            return [
                pltpu.make_async_copy(
                    out_buf.at[ring, pl.ds(0, step), pl.ds(a * ff, ff)], dst.at[pl.ds(r, step), :], o_sem.at[ring, a]
                )
                for a, dst in enumerate(outs)
            ]

        mlp_outs = ((gdown,), (ggate, gup))

        def mlp_half(a, j):
            step = min(32, U)
            count = U // step
            outs = mlp_outs[a]

            def put(i, value):
                ring = i % 4

                @pl.when(i >= 4)
                def _():
                    for copy in out_copies(outs, j * U, ring, step):
                        copy.wait()

                out_buf[ring, 0:step, 0 : len(outs) * ff] = value
                for copy in out_copies(outs, pl.multiple_of(j * U + i * step, step), ring, step):
                    copy.start()

            mlp[a].final(j, step, put)
            for ring in range(min(4, count)):
                for copy in out_copies(outs, j * U, ring, step):
                    copy.wait()

        def mlp_whole(a):
            outs = mlp_outs[a]

            def put(part, value):
                out_buf[0, 0:16, 0 : len(outs) * ff] = value
                for copy in out_copies(outs, part.start, 0, 16):
                    copy.start()
                for copy in out_copies(outs, part.start, 0, 16):
                    copy.wait()

            mlp[a].final(put)
            mlp[a].finish()

        grads_at = min(s for s, task in plan.tasks.items() if task[0][0] == "grad")

        def after(s):
            name = plan.tasks[s - 1][0] if s - 1 in plan.tasks else None
            if name and name[0] == "terms":
                combine_terms(*name[1:])
            if square:
                if s == grads_at + 1:
                    for job in mlp:
                        job.reload()
                if s == grads_at + 2:
                    mlp_half(0, 0)
                    mlp_half(0, 1)
                if s == grads_at + 4:
                    mlp_half(1, 0)
            if s == grads_at + n - 1:
                unit_second()

        run_plan(plan, at, sums, task, after, finish)

        def slice_of(b):
            return small.at[:, pl.ds(pl.multiple_of(b * R, R), R)]

        def batch_job(off):
            to = (at.b + off) % n
            return remote(slice_of(to), over_batch.at[off], bsend.at[off], brecv.at[off], {"batch": to})

        for off in range(1, n):
            batch_job(off).start()
        mine = pltpu.make_async_copy(slice_of(at.b), over_batch.at[0], local)
        mine.start()
        if square:
            mlp_half(1, 1)
        else:
            mlp_whole(0)
            mlp_whole(1)
        mine.wait()
        total = over_batch[0]
        for off in range(1, n):
            batch_job(off).wait_recv()
            total = total + over_batch[off]
        over_head[at.h] = total

        def head_job(off, block):
            to = (at.h + off) % H
            return remote(over_head.at[block], over_head.at[block], hsend.at[off], hrecv.at[off], {"head": to})

        for off in range(1, H):
            head_job(off, at.h).start()

        def put_units(part, value):
            out_q[part, :] = value[:, :W]
            out_k[part, :] = value[:, W : 2 * W]
            out_v[part, :] = value[:, 2 * W : 3 * W]
            out_o[part, :] = value[:, 3 * W :]

        unit_final(put_units)
        for off in range(1, H):
            head_job(off, (at.h + H - off) % H).wait_recv()
        total = over_head[0]
        for h in range(1, H):
            total = total + over_head[h]
        gain_out[...] = total
        for off in range(1, n):
            batch_job(off).wait_send()
        for off in range(1, H):
            head_job(off, at.h).wait_send()

    weight = jax.ShapeDtypeStruct((R, W), F32)
    wide_weight = jax.ShapeDtypeStruct((R, ff), F32)
    return pl.pallas_call(
        kernel,
        out_shape=(
            jax.ShapeDtypeStruct((rows, T, D), F32),
            weight,
            weight,
            weight,
            weight,
            wide_weight,
            wide_weight,
            wide_weight,
            jax.ShapeDtypeStruct((8, R), F32),
        ),
        in_specs=[ANY, VMEM, VMEM, VMEM, ANY] + [VMEM] * 6 + [ANY, VMEM, VMEM] + [ANY] * 4,
        out_specs=(VMEM,) * 5 + (ANY,) * 3 + (VMEM,),
        scratch_shapes=names.shapes,
        compiler_params=pltpu.CompilerParams(collective_id=4, has_side_effects=True, vmem_limit_bytes=BACK_LIMIT),
        name="attention_back",
    )(
        g_att,
        attended,
        qkv,
        lse,
        attn_in,
        w_qkv,
        w_o,
        cosine,
        sine,
        starts,
        tokens,
        g_mixed,
        gains,
        gain_sum,
        g_gu,
        g_d,
        first_gu,
        first_d,
    )


def rows_dot(left, right):
    return lax.dot_general(left, right, (((0,), (0,)), ((), ())), preferred_element_type=F32)


def cols_dot(left, right):
    return lax.dot_general(left, right, (((1,), (1,)), ((), ())), preferred_element_type=F32)


QUERIES = 256


def rope_tables(positions):
    half_dim = HEAD_DIM // 2
    frequency = rope_base ** (-(jnp.arange(half_dim).astype(F32) * 2.0) / HEAD_DIM)
    angles = positions.astype(F32)[:, :, None] * frequency
    cosine, sine = jnp.cos(angles), jnp.sin(angles)
    return jnp.concatenate([cosine] * 4, axis=-1), jnp.concatenate([-sine, sine] * 2, axis=-1)


def rotate(values, cosine, sine):
    half_dim = HEAD_DIM // 2
    parts = []
    for g in range(values.shape[1] // 128):
        part = values[:, g * 128 : (g + 1) * 128]
        lane = lax.broadcasted_iota(jnp.int32, part.shape, 1)
        swapped = jnp.where(
            lane % HEAD_DIM < half_dim, pltpu.roll(part, 128 - half_dim, 1), pltpu.roll(part, half_dim, 1)
        )
        parts.append(part * cosine + swapped * sine)
    return jnp.concatenate(parts, axis=1) if len(parts) > 1 else parts[0]


def only_head(values, h):
    lane = lax.broadcasted_iota(jnp.int32, values.shape, 1)
    return jnp.where(lane // HEAD_DIM == h, values, jnp.zeros_like(values))


def masked_scores(keys, query, starts, first):
    scores = cols_dot(keys, query)
    key_index = lax.broadcasted_iota(jnp.int32, scores.shape, 0)
    query_index = lax.broadcasted_iota(jnp.int32, scores.shape, 1) + first
    return jnp.where((key_index >= starts) & (key_index <= query_index), scores, masked_value)


def attend(qkv, starts, lse, attended, h, W):
    S = qkv.shape[0]
    scale = HEAD_DIM**-0.5
    block = min(QUERIES, S)
    for i in range(S // block):
        rows = pl.ds(i * block, block)
        width = (i + 1) * block
        query = only_head(qkv[rows, 0:W], h) * jnp.asarray(scale, BF16)
        scores = masked_scores(qkv[0:width, W : 2 * W], query, starts[:, rows], i * block)
        top = jnp.max(scores, axis=0, keepdims=True)
        weights = jnp.exp(scores - top)
        total = jnp.sum(weights, axis=0, keepdims=True)
        lse[pl.ds(h, 1), rows] = top + jnp.log(total)
        probs = (weights * (1.0 / total)).astype(BF16)
        out = rows_dot(probs, qkv[0:width, 2 * W : 3 * W]).astype(BF16)
        lane = lax.broadcasted_iota(jnp.int32, out.shape, 1)
        attended[rows, :] = jnp.where(lane // HEAD_DIM == h, out, attended[rows, :])


def attend_back(qkv, starts, lse, grad, g_query, g_key, g_value, h, W):
    S = qkv.shape[0]
    scale = HEAD_DIM**-0.5
    block = min(QUERIES, S)
    for i in range(S // block):
        rows = pl.ds(i * block, block)
        width = (i + 1) * block
        query = only_head(qkv[rows, 0:W], h) * jnp.asarray(scale, BF16)
        keys = qkv[0:width, W : 2 * W]
        scores = masked_scores(keys, query, starts[:, rows], i * block)
        probs = jnp.exp(scores - lse[pl.ds(h, 1), rows])
        back = only_head(grad[rows, :], h)
        g_prob = cols_dot(qkv[0:width, 2 * W : 3 * W], back)
        delta = jnp.sum(probs * g_prob, axis=0, keepdims=True)
        g_score = (probs * (g_prob - delta)).astype(BF16)
        g_value[0:width, :] += jnp.dot(probs.astype(BF16), back, preferred_element_type=F32)
        g_key[0:width, :] += jnp.dot(g_score, query, preferred_element_type=F32)
        g_query[rows, :] += only_head(rows_dot(g_score, keys) * scale, h)


def per_device(
    n,
    H,
    tokens,
    segment_ids,
    position_ids,
    w_query,
    w_key,
    w_value,
    w_output,
    w_gate,
    w_up,
    w_down,
    attn_gain,
    mlp_gain,
    cotangent,
):
    rows, T, D = tokens.shape
    S = T * H
    R, hw = w_query.shape
    ff = w_gate.shape[1]
    shard_gains = jnp.concatenate(
        [attn_gain.astype(F32)[None], mlp_gain.astype(F32)[None], jnp.zeros((6, R), F32)], axis=0
    )
    cosine, sine = rope_tables(position_ids)
    starts = (jnp.arange(S, dtype=jnp.int32)[None, :] - position_ids)[:, None, :]
    attn_in, ct_first, w_qkv, w_o, w_gu, terms, gains, qkv, lse, attended = attention_in(
        n, H, tokens, cotangent, shard_gains, (w_query, w_key, w_value, w_output, w_gate, w_up), cosine, sine, starts
    )
    w_qkv = w_qkv.reshape(D, 3 * hw)
    w_o = w_o.reshape(D, hw)
    w_gu = w_gu.reshape(D, 2 * ff)
    _, _, g_att, _, _, grad_gu, grad_d, first_gu, first_d, g_mixed, layer_out, gain_sum = feed_forward(
        n, H, terms, ct_first, tokens, cotangent, gains, w_gu, w_down
    )
    grad_input, grad_q, grad_k, grad_v, grad_out, grad_gate, grad_up, grad_down, gain_grads = attention_back(
        n,
        H,
        g_att.reshape(rows, S, D),
        attended,
        qkv,
        lse,
        attn_in.reshape(rows * S, D),
        w_qkv,
        w_o,
        cosine,
        sine,
        starts,
        tokens,
        g_mixed,
        gains,
        gain_sum,
        grad_gu,
        grad_d,
        first_gu,
        first_d,
    )
    return (
        layer_out,
        grad_input,
        grad_q,
        grad_k,
        grad_v,
        grad_out,
        grad_gate,
        grad_up,
        grad_down,
        gain_grads[0],
        gain_grads[1],
    )


def solution(mesh):
    row = P("batch", "head", None)
    ids = P("batch", None)
    weight = P("batch", "head")
    gain = P("batch")
    return jax.shard_map(
        functools.partial(per_device, mesh.shape["batch"], mesh.shape["head"]),
        mesh=mesh,
        in_specs=(row, ids, ids) + (weight,) * 7 + (gain, gain, row),
        out_specs=(row, row) + (weight,) * 7 + (gain, gain),
        check_vma=False,
    )
```

```python
import functools

import jax
import jax.numpy as jnp
from jax import lax
from jax.experimental import pallas as pl
from jax.experimental.pallas import tpu as pltpu
from jax.sharding import PartitionSpec as P

HEAD_DIM = 64
epsilon = 1e-05
rope_base = 130000.0
masked_value = -1000000000.0
MESH = pl.DeviceIdType.MESH
F32 = jnp.float32
BF16 = jnp.bfloat16
DMA = pltpu.SemaphoreType.DMA
ANY = pl.BlockSpec(memory_space=pl.ANY)
VMEM = pl.BlockSpec(memory_space=pltpu.VMEM)
VMEM_LIMIT = 60 * 2**20
BACK_LIMIT = 63 * 2**20


class Place:
    def __init__(self, batch, head):
        self.n, self.H = batch, head
        self.L = head // 2
        self.b = lax.axis_index("batch")
        self.h = lax.axis_index("head")
        self.z = self.h // 2
        self.c = self.h % 2
        self.sib = self.z * 2 + (1 - self.c)
        self.up = self.h + 2
        self.down = self.h - 2
        self.x, self.y = self.b % 2, self.b // 2
        self.xn = self.y * 2 + (1 - self.x)
        self.yn = (1 - self.y) * 2 + self.x
        self.dg = (1 - self.y) * 2 + (1 - self.x)
        self.square = batch == 4

    def greet(self, line=True, batch=True, all_heads=False):
        barrier = pltpu.get_barrier_semaphore()
        me, L = self, self.L

        def hello(device):
            pl.semaphore_signal(barrier, inc=1, device_id=device, device_id_type=MESH)

        count = 0
        if all_heads:
            for off in range(1, self.H):
                hello({"head": (me.h + off) % self.H})
                count += 1
        elif line:
            hello({"head": me.sib})
            count += 1

            @pl.when(me.z > 0)
            def _():
                hello({"head": me.down})

            @pl.when(me.z < L - 1)
            def _():
                hello({"head": me.up})

        if batch:
            if self.square and not all_heads:
                hello({"batch": me.xn})
                hello({"batch": me.yn})
                count += 2
            else:
                for off in range(1, self.n):
                    hello({"batch": (me.b + off) % self.n})
                    count += 1
        if line and not all_heads:
            count = count + jnp.minimum(me.z, 1) + jnp.minimum(L - 1 - me.z, 1)
        pl.semaphore_wait(barrier, count)


def remote(src, dst, ssem, rsem, device):
    return pltpu.make_async_remote_copy(
        src_ref=src, dst_ref=dst, send_sem=ssem, recv_sem=rsem, device_id=device, device_id_type=MESH
    )


class Gather:
    def __init__(self, at, own, out, sems):
        self.at, self.own, self.out = at, own, out
        self.line_recv, self.sib_recv, self.up_send, self.down_send, self.sib_send, self.local = sems

    @staticmethod
    def sems(at_L):
        return [DMA((at_L,))] * 5 + [DMA]

    def _up(self, zb, src):
        at = self.at
        return remote(src, self.out.at[zb * 2 + at.c], self.up_send.at[zb], self.line_recv.at[zb], {"head": at.up})

    def _down(self, zb, src):
        at = self.at
        return remote(src, self.out.at[zb * 2 + at.c], self.down_send.at[zb], self.line_recv.at[zb], {"head": at.down})

    def _sib(self, zb, src):
        at = self.at
        return remote(src, self.out.at[zb * 2 + at.c], self.sib_send.at[zb], self.sib_recv.at[zb], {"head": at.sib})

    def _mine(self):
        return pltpu.make_async_copy(self.own, self.out.at[self.at.h], self.local)

    def start(self):
        at = self.at

        @pl.when(at.z < at.L - 1)
        def _():
            self._up(at.z, self.own).start()

        @pl.when(at.z > 0)
        def _():
            self._down(at.z, self.own).start()

        self._sib(at.z, self.own).start()
        self._mine().start()

    def step(self, k):
        at = self.at
        below, above = at.z - k, at.z + k

        @pl.when(below >= 0)
        def _():
            block = self.out.at[below * 2 + at.c]
            self._up(below, block).wait_recv()

            @pl.when(at.z < at.L - 1)
            def _():
                self._up(below, block).start()

            self._sib(below, block).start()

        @pl.when(above <= at.L - 1)
        def _():
            block = self.out.at[above * 2 + at.c]
            self._down(above, block).wait_recv()

            @pl.when(at.z > 0)
            def _():
                self._down(above, block).start()

            self._sib(above, block).start()

    def finish(self):
        at = self.at
        self._mine().wait()
        for zb in range(at.L):
            block = self.out.at[zb * 2 + at.c]
            self._sib(zb, block).wait_send()
            other = self.out.at[zb * 2 + 1 - at.c]
            remote(other, other, self.sib_send.at[zb], self.sib_recv.at[zb], {"head": at.sib}).wait_recv()

            @pl.when((zb <= at.z) & (at.z < at.L - 1))
            def _():
                self._up(zb, block).wait_send()

            @pl.when((zb >= at.z) & (at.z > 0))
            def _():
                self._down(zb, block).wait_send()


class Reduce:
    def __init__(self, at, src, own, sib, recv, sems):
        self.at, self.src, self.own, self.sib, self.recv = at, src, own, sib, recv
        self.load, self.sib_send, self.sib_recv, self.fwd_send, self.recv_sem = sems

    @staticmethod
    def sems(L):
        return [DMA((L,)), DMA((L,)), DMA((L,)), DMA((L,)), DMA((L + 1,))]

    @staticmethod
    def bufs(L, T, D):
        return [pltpu.VMEM((L, T, D), BF16), pltpu.VMEM((L, T, D), BF16), pltpu.VMEM((L + 1, T, D), BF16)]

    def _load(self, zd):
        return pltpu.make_async_copy(self.src.at[zd * 2 + self.at.c], self.own.at[zd], self.load.at[zd])

    def _sib(self, zd):
        at = self.at
        return remote(
            self.src.at[zd * 2 + 1 - at.c], self.sib.at[zd], self.sib_send.at[zd], self.sib_recv.at[zd], {"head": at.sib}
        )

    def _fwd(self, zd, slot, device):
        return remote(self.recv.at[zd], self.recv.at[slot], self.fwd_send.at[zd], self.recv_sem.at[slot], {"head": device})

    def start(self):
        at, L = self.at, self.at.L
        order = []
        for k in range((L + 1) // 2):
            order += [L - 1 - k] + ([k] if k != L - 1 - k else [])
        for zd in order:
            self._sib(zd).start()
            self._load(zd).start()

    def _chunks(self, fn):
        T = self.own.shape[1]
        step = 32 if T % 32 == 0 else T

        @pl.loop(0, T // step)
        def _(i):
            fn(pl.ds(pl.multiple_of(i * step, step), step))

    def _hop(self, zd, first, slot, device, which):
        @pl.when(first)
        def _():
            if which in ("first", "both"):
                self._load(zd).wait()
                self._sib(zd).wait_recv()

                def add(rows):
                    self.recv[zd, rows, :] = (self.own[zd, rows, :].astype(F32) + self.sib[zd, rows, :].astype(F32)).astype(
                        BF16
                    )

                self._chunks(add)
                self._fwd(zd, slot, device).start()

        @pl.when(jnp.logical_not(first))
        def _():
            if which in ("mid", "both"):
                self._load(zd).wait()
                self._sib(zd).wait_recv()
                self._fwd(zd, zd, device).wait_recv()

                def add(rows):
                    self.recv[zd, rows, :] = (
                        self.own[zd, rows, :].astype(F32)
                        + self.sib[zd, rows, :].astype(F32)
                        + self.recv[zd, rows, :].astype(F32)
                    ).astype(BF16)

                self._chunks(add)
                self._fwd(zd, slot, device).start()

    def hops(self, k, which="both"):
        at, L = self.at, self.at.L
        far, near = L - 1 - k, k

        @pl.when(far > at.z)
        def _():
            self._hop(far, at.z == 0, far, at.up, which)

        @pl.when(near < at.z)
        def _():
            self._hop(near, at.z == L - 1, jnp.where(at.z - 1 == near, L, near), at.down, which)

    def final(self, add):
        at, L = self.at, self.at.L
        z = at.z
        self._load(z).wait()
        self._sib(z).wait_recv()

        @pl.when(z > 0)
        def _():
            self._fwd(z, z, at.up).wait_recv()

        @pl.when(z < L - 1)
        def _():
            self._fwd(z, L, at.down).wait_recv()

        def base(rows):
            return self.own[z, rows, :].astype(F32) + self.sib[z, rows, :].astype(F32)

        @pl.when(z == 0)
        def _():
            self._chunks(lambda rows: add(rows, base(rows) + self.recv[L, rows, :].astype(F32)))

        @pl.when(z == L - 1)
        def _():
            self._chunks(lambda rows: add(rows, base(rows) + self.recv[z, rows, :].astype(F32)))

        @pl.when((z > 0) & (z < L - 1))
        def _():
            self._chunks(
                lambda rows: add(
                    rows, base(rows) + self.recv[z, rows, :].astype(F32) + self.recv[L, rows, :].astype(F32)
                )
            )

    def finish(self):
        at = self.at
        for zd in range(at.L):
            self._sib(zd).wait_send()

            @pl.when(zd != at.z)
            def _():
                self._fwd(zd, zd, at.up).wait_send()


class BatchGather:
    def __init__(self, at, own, out, sems):
        self.at, self.own, self.out = at, own, out
        self.send, self.recv, self.local = sems

    @staticmethod
    def sems(n):
        m = 4 if n == 4 else n
        return [DMA((m,)), DMA((m,)), DMA]

    def _half(self, b, i):
        half = self.own.shape[0] // 2
        return self.out(b, pl.ds(i * half, half))

    def _all(self, b):
        return self.out(b, pl.ds(0, self.own.shape[0]))

    def _direct(self, i, device):
        at = self.at
        return remote(self.own, self._all(at.b), self.send.at[i], self.recv.at[i], {"batch": device})

    def start(self):
        at = self.at
        pltpu.make_async_copy(self.own, self._all(at.b), self.local).start()
        if at.square:
            self._direct(0, at.xn).start()
            self._direct(1, at.yn).start()
        else:
            for off in range(1, at.n):
                remote(
                    self.own, self._all(at.b), self.send.at[off], self.recv.at[off], {"batch": (at.b + off) % at.n}
                ).start()

    def forward(self):
        at = self.at
        if at.square:
            block = self._all(at.xn)
            remote(block, block, self.send.at[0], self.recv.at[0], {"batch": at.xn}).wait_recv()
            half = self._half(at.xn, 0)
            remote(half, half, self.send.at[2], self.recv.at[2], {"batch": at.yn}).start()
            block = self._all(at.yn)
            remote(block, block, self.send.at[1], self.recv.at[1], {"batch": at.yn}).wait_recv()
            half = self._half(at.yn, 1)
            remote(half, half, self.send.at[3], self.recv.at[3], {"batch": at.xn}).start()

    def finish(self):
        at = self.at
        pltpu.make_async_copy(self.own, self._all(at.b), self.local).wait()
        if at.square:
            self._direct(0, at.xn).wait_send()
            self._direct(1, at.yn).wait_send()
            half = self._half(at.dg, 0)
            remote(half, half, self.send.at[2], self.recv.at[2], {"batch": at.yn}).wait()
            half = self._half(at.dg, 1)
            remote(half, half, self.send.at[3], self.recv.at[3], {"batch": at.xn}).wait()
        else:
            for off in range(1, at.n):
                block = self._all((at.b + at.n - off) % at.n)
                remote(block, block, self.send.at[off], self.recv.at[off], {"batch": (at.b + off) % at.n}).wait()


class BatchReduce:
    def __init__(self, at, src, bufs, sems, before=None):
        self.at, self.src, self.before = at, src, before
        if at.square:
            self.first, self.mine, self.second = bufs
        else:
            (self.slots,) = bufs
        self.send, self.recv, self.load = sems

    @staticmethod
    def sems(n):
        m = 6 if n == 4 else n
        return [DMA((m,)), DMA((m,)), DMA((4,))]

    @staticmethod
    def bufs(n, R, K):
        if n == 4:
            return [
                pltpu.VMEM((4, R // 2, K), BF16),
                pltpu.VMEM((4, R // 2, K), BF16),
                pltpu.VMEM((2, R // 2, K), BF16),
            ]
        return [pltpu.VMEM((n, R, K), BF16)]

    def _first(self, i):
        at, half = self.at, self.src.shape[1] // 2
        if i < 2:
            src = self.src.at[i * 2 + 1 - at.x, pl.ds(0, half), :]
            device = {"batch": at.xn}
        else:
            src = self.src.at[(1 - at.y) * 2 + i - 2, pl.ds(half, half), :]
            device = {"batch": at.yn}
        return remote(src, self.first.at[i], self.send.at[i], self.recv.at[i], device)

    def _taken(self, i):
        if self.before is None:
            return self._first(i)
        return pltpu.make_async_copy(self.before.at[i], self.first.at[i], self.recv.at[i])

    def _load(self, i):
        at, half = self.at, self.src.shape[1] // 2
        if i < 2:
            src = self.src.at[i * 2 + at.x, pl.ds(0, half), :]
        else:
            src = self.src.at[at.y * 2 + i - 2, pl.ds(half, half), :]
        return pltpu.make_async_copy(src, self.mine.at[i], self.load.at[i])

    def _second(self, j):
        at = self.at
        if j == 0:
            return remote(
                self.mine.at[1 - at.y], self.second.at[0], self.send.at[4], self.recv.at[4], {"batch": at.yn}
            )
        return remote(self.mine.at[3 - at.x], self.second.at[1], self.send.at[5], self.recv.at[5], {"batch": at.xn})

    def _direct(self, off):
        at = self.at
        to = (at.b + off) % at.n
        return remote(self.src.at[to], self.slots.at[off], self.send.at[off], self.recv.at[off], {"batch": to})

    def start(self):
        at = self.at
        if at.square:
            for i in (0, 2, 1, 3):
                self._taken(i).start()
                self._load(i).start()
        else:
            for off in range(1, at.n):
                self._direct(off).start()
            pltpu.make_async_copy(self.src.at[at.b], self.slots.at[0], self.load.at[0]).start()

    def _chunks(self, R, fn):
        step = 16

        @pl.loop(0, R // step)
        def _(i):
            fn(pl.multiple_of(i * step, step), step)

    def second_step(self):
        at = self.at
        if at.square:
            for i in range(4):
                self._load(i).wait()
                if self.before is None:
                    self._first(i).wait_recv()
                else:
                    self._taken(i).wait()
            for j, i in ((0, 1 - at.y), (1, 3 - at.x)):

                def add(r, step, i=i):
                    rows = pl.ds(r, step)
                    self.mine[i, rows, :] = (
                        self.mine[i, rows, :].astype(F32) + self.first[i, rows, :].astype(F32)
                    ).astype(BF16)

                self._chunks(self.mine.shape[1], add)
                self._second(j).start()

    def final(self, put):
        at = self.at
        if at.square:
            half = self.src.shape[1] // 2
            for j, i in ((0, at.y), (1, 2 + at.x)):
                self._second(j).wait_recv()

                def add(r, step, i=i, j=j):
                    rows = pl.ds(r, step)
                    put(
                        pl.ds(r + j * half, step),
                        self.mine[i, rows, :].astype(F32)
                        + self.first[i, rows, :].astype(F32)
                        + self.second[j, rows, :].astype(F32),
                    )

                self._chunks(half, add)
        else:
            pltpu.make_async_copy(self.src.at[at.b], self.slots.at[0], self.load.at[0]).wait()
            for off in range(1, at.n):
                self._direct(off).wait_recv()

            def add(r, step):
                rows = pl.ds(r, step)
                total = self.slots[0, rows, :].astype(F32)
                for off in range(1, at.n):
                    total = total + self.slots[off, rows, :].astype(F32)
                put(rows, total)

            self._chunks(self.src.shape[1], add)

    def finish(self):
        at = self.at
        if at.square:
            for i in range(4 if self.before is None else 0):
                self._first(i).wait_send()
            self._second(0).wait_send()
            self._second(1).wait_send()
        else:
            for off in range(1, at.n):
                self._direct(off).wait_send()


class Names:
    def __init__(self):
        self.shapes = []

    def add(self, shapes):
        start = len(self.shapes)
        self.shapes += list(shapes)
        return slice(start, len(self.shapes))


def chunk_loop(rows, step, fn):
    step = min(step, rows)

    @pl.loop(0, rows // step)
    def _(i):
        fn(pl.ds(pl.multiple_of(i * step, step), step))


def inv_root_of(values):
    return lax.rsqrt(jnp.mean(values * values, axis=-1, keepdims=True) + epsilon)


def far_first(L, z):
    return sorted(range(L), key=lambda zd: (-abs(zd - z), -zd))


class Plan:
    def __init__(self, L, rank, reduces, early, follow, begin, tasks):
        self.L = L
        order = [far_first(L, z) for z in range(L)]
        never = 10**6
        jobs = list(rank)
        ready = {j: [[never] * L for _ in range(L)] for j in reduces}
        own = {j: begin.get(j, never) for j in jobs if j not in reduces}
        arrive = {j: {} for j in jobs}
        sent = {j: set() for j in jobs}
        for j, when in early.items():
            for z in range(L):
                for i in range(L):
                    ready[j][z][order[z][i]] = when[i]
        self.final, self.complete, self.tasks, self.sends = {}, {}, {}, []
        todo = list(tasks)
        total = L * (L - 1) * 2
        last = {j: -1 for j in jobs}
        s = free = 0

        def close():
            for j in jobs:
                if len(sent[j]) == total:
                    if j in reduces and j not in self.final:
                        self.final[j] = max(last[j] + 1, max(ready[j][z][z] for z in range(L)) - 1, s - 1)
                        if j in follow:
                            own[follow[j]] = self.final[j] + 1
                    if j in own and j not in self.complete:
                        self.complete[j] = last[j] + 2

        while any(len(sent[j]) < total for j in jobs) or todo:
            close()
            now = {}
            for z in range(L):
                for way in (1, -1):
                    if not 0 <= z + way < L:
                        continue
                    for j in jobs:
                        best = []
                        for block in range(L):
                            for half in (0, 1):
                                if (z, way, block, half) in sent[j]:
                                    continue
                                came = arrive[j].get((z, way, block, half), never)
                                if j in reduces:
                                    first = not 0 <= z - way < L
                                    if (block - z) * way > 0 and ready[j][z][block] <= s and (first or came + 2 <= s):
                                        best.append((-abs(block - z), half, block))
                                elif (z - block) * way >= 0 and (own[j] <= s if block == z else came + 2 <= s):
                                    best.append((abs(block - z), half, block))
                        if best:
                            _, half, block = min(best)
                            now[(z, way)] = (j, block, half)
                            break
            for (z, way), (j, block, half) in now.items():
                sent[j].add((z, way, block, half))
                arrive[j][(z + way, way, block, half)] = s
                last[j] = s
            self.sends.append(now)
            if todo and s >= free:
                name, needs, makes, i, length = todo[0]
                if all(self.complete.get(j, never) <= s for j in needs):
                    self.tasks[s] = todo.pop(0)
                    free = s + length
                    for j in makes:
                        for z in range(L):
                            ready[j][z][order[z][i]] = s + 2
            s += 1
        close()
        self.jobs, self.reduces, self.order = jobs, reduces, order
        self.ready, self.arrive, self.own = ready, arrive, own
        self.slots = 1 + max(list(self.final.values()) + list(self.complete.values()) + [s + 1 for s in self.tasks])

    def block(self, z, i):
        return pick(z, [self.order[q][i] for q in range(self.L)])


def run_plan(plan, at, jobs, task, after, finish):
    z, L = at.z, at.L
    for s in range(plan.slots):
        now = plan.sends[s] if s < len(plan.sends) else {}
        for q in range(L):
            mine = [(way, now[(q, way)]) for way in (1, -1) if (q, way) in now]
            if mine:

                @pl.when(z == q)
                def _():
                    for way, (j, block, half) in mine:
                        jobs[j].copy(q, way, block, half).start()

        if s in plan.tasks:
            task(plan.tasks[s][0])
        after(s)
        past = plan.sends[s - 1] if 0 <= s - 1 < len(plan.sends) else {}
        for q in range(L):
            came = [(way, past[(q - way, way)]) for way in (1, -1) if (q - way, way) in past]
            adds = []
            for j in plan.reduces:
                for (zq, way, block, half), when in plan.arrive[j].items():
                    if zq == q and block != q and max(when + 1, plan.ready[j][q][block] - 1) == s:
                        adds.append((j, block, half))
            if came or adds:

                @pl.when(z == q)
                def _():
                    for way, (j, block, half) in came:
                        jobs[j].landed(q, way, block, half).wait_recv()
                        if j not in plan.reduces:
                            jobs[j].share(block, half).start()
                    for j, block, half in adds:
                        jobs[j].add(block, half)

        for j, when in plan.final.items():
            if when == s:
                finish(j)


def pick(z, values):
    if len(set(values)) == 1:
        return values[0]
    out = jnp.int32(values[0])
    for i, v in enumerate(values[1:], 1):
        out = jnp.where(z == i, v, out)
    return out


class SlotReduce:
    def __init__(self, at, sib, recv, sems):
        self.at, self.sib, self.recv = at, sib, recv
        self.sib_send, self.sib_recv, self.fwd_send, self.recv_sem = sems
        self.half = sib.shape[1] // 2

    @staticmethod
    def sems(L):
        return [DMA((L,)), DMA((L,)), DMA((L, 2)), DMA((L + 1, 2))]

    @staticmethod
    def bufs(L, T, D):
        return [pltpu.VMEM((L, T, D), BF16), pltpu.VMEM((L + 1, T, D), BF16)]

    def part(self, half):
        return pl.ds(half * self.half, self.half)

    def slot(self, z, way, zd):
        return self.at.L if way < 0 and z == zd else zd

    def copy(self, z, way, zd, half):
        at, part = self.at, self.part(half)
        first = not 0 <= z - way < at.L
        src = (self.sib if first else self.recv).at[zd, part, :]
        slot = self.slot(z + way, way, zd)
        device = {"head": at.up if way > 0 else at.down}
        return remote(src, self.recv.at[slot, part, :], self.fwd_send.at[zd, half], self.recv_sem.at[slot, half], device)

    def landed(self, z, way, zd, half):
        at, part = self.at, self.part(half)
        slot = self.slot(z, way, zd)
        block = self.recv.at[slot, part, :]
        device = {"head": at.down if way > 0 else at.up}
        return remote(block, block, self.fwd_send.at[zd, half], self.recv_sem.at[slot, half], device)

    def exchange(self, zd, src):
        return remote(src, self.sib.at[zd], self.sib_send.at[zd], self.sib_recv.at[zd], {"head": self.at.sib})

    def combine(self, zd, mine):
        def add(rows):
            self.sib[zd, rows, :] = (self.sib[zd, rows, :].astype(F32) + mine[rows, :].astype(F32)).astype(BF16)

        chunk_loop(self.sib.shape[1], 32, add)

    def add(self, zd, half):
        def one(rows):
            self.recv[zd, rows, :] = (self.recv[zd, rows, :].astype(F32) + self.sib[zd, rows, :].astype(F32)).astype(BF16)

        step = min(32, self.half)

        @pl.loop(0, self.half // step)
        def _(i):
            one(pl.ds(pl.multiple_of(half * self.half + i * step, step), step))

    def final(self, put):
        at, z = self.at, self.at.z

        def run(extra):
            def part(rows):
                value = self.sib[z, rows, :].astype(F32)
                for slot in extra:
                    value = value + self.recv[slot, rows, :].astype(F32)
                put(rows, value)

            chunk_loop(self.sib.shape[1], 32, part)

        @pl.when(z == 0)
        def _():
            run((at.L,))

        @pl.when(z == at.L - 1)
        def _():
            run((z,))

        @pl.when((z > 0) & (z < at.L - 1))
        def _():
            run((z, at.L))

    def sent(self):
        at = self.at
        for zd in range(at.L):

            @pl.when(zd != at.z)
            def _():
                for half in (0, 1):
                    block = self.recv.at[zd, self.part(half), :]
                    remote(block, block, self.fwd_send.at[zd, half], self.recv_sem.at[zd, half], {"head": at.up}).wait_send()


class SlotGather:
    def __init__(self, at, own, out, sems):
        self.at, self.own, self.out = at, own, out
        self.line_recv, self.up_send, self.down_send, self.sib_send, self.sib_recv, self.local = sems
        self.half = own.shape[0] // 2

    @staticmethod
    def sems(L):
        return [DMA((L, 2))] * 5 + [DMA]

    def block(self, index, half):
        return self.out.at[index, pl.ds(half * self.half, self.half), :]

    def mine(self, half):
        return self.own.at[pl.ds(half * self.half, self.half), :]

    def copy(self, z, way, zb, half):
        at = self.at
        dst = self.block(zb * 2 + at.c, half)
        src = self.mine(half) if zb == z else dst
        send = (self.up_send if way > 0 else self.down_send).at[zb, half]
        return remote(src, dst, send, self.line_recv.at[zb, half], {"head": at.up if way > 0 else at.down})

    def landed(self, z, way, zb, half):
        at = self.at
        dst = self.block(zb * 2 + at.c, half)
        return remote(dst, dst, self.up_send.at[zb, half], self.line_recv.at[zb, half], {"head": at.down if way > 0 else at.up})

    def share(self, zb, half, src=None):
        at = self.at
        dst = self.block(zb * 2 + at.c, half)
        return remote(dst if src is None else src, dst, self.sib_send.at[zb, half], self.sib_recv.at[zb, half], {"head": at.sib})

    def keep(self):
        return pltpu.make_async_copy(self.own, self.out.at[self.at.h], self.local)

    def begin(self):
        for half in (0, 1):
            self.share(self.at.z, half, self.mine(half)).start()
        self.keep().start()

    def finish(self):
        at = self.at
        self.keep().wait()
        for zb in range(at.L):
            for half in (0, 1):
                self.share(zb, half).wait_send()
                other = self.block(zb * 2 + 1 - at.c, half)
                remote(other, other, self.sib_send.at[zb, half], self.sib_recv.at[zb, half], {"head": at.sib}).wait_recv()

            @pl.when((zb <= at.z) & (at.z < at.L - 1))
            def _():
                for half in (0, 1):
                    self.copy(-1, 1, zb, half).wait_send()

            @pl.when((zb >= at.z) & (at.z > 0))
            def _():
                for half in (0, 1):
                    self.copy(-1, -1, zb, half).wait_send()


def norm_back_part(values, gain, grad):
    inv_root = inv_root_of(values)
    unit = values * inv_root
    weighted = grad * gain
    back = inv_root * (weighted - unit * jnp.mean(weighted * unit, axis=-1, keepdims=True))
    return back, jnp.sum(grad * unit, axis=0, keepdims=True)


def attention_in(n, H, tokens, cotangent, gains, weights, cosine, sine, starts):
    rows, T, D = tokens.shape
    R, W = weights[0].shape
    ff = weights[4].shape[1]
    L = H // 2
    S = H * T
    heads = W // HEAD_DIM
    mix = ("mix", 0)
    rank = [("x", r) for r in range(rows)] + [("ct", 0), mix]
    tasks = []
    for r in range(rows):
        tasks += [((kind, r, 0), (("x", r),), (), 0, 1) for kind in ("qkv", "low", "high")]
        if r == 0:
            tasks += [(("send", 0, i), (), (mix,), i, 1) for i in range(L)]
        else:
            tasks.append((("terms", r, 0), (), (), 0, 1))
    plan = Plan(L, rank, [mix], {}, {}, {j: 0 for j in rank if j != mix}, tasks)
    names = Names()
    z_at = [names.add(SlotGather.sems(L)) for _ in range(rows + 1)]
    w_at = [names.add(BatchGather.sems(n)) for _ in range(6)]
    g_at = names.add([DMA((n,)), DMA((n,)), DMA])
    m_at = names.add(SlotReduce.bufs(L, T, D))
    ms_at = names.add(SlotReduce.sems(L))
    rest = names.add(
        [
            pltpu.VMEM((rows, T, D), BF16),
            pltpu.VMEM((2, 2, T, D), BF16),
            pltpu.VMEM((2, 2, T, D), BF16),
            pltpu.VMEM((D, 3 * W), BF16),
            pltpu.VMEM((D, W), BF16),
            DMA((2,)),
            DMA((2,)),
            DMA((2,)),
        ]
    )
    wide = min(512, D)

    def kernel(
        tok,
        ct,
        gain,
        cos,
        sin,
        st,
        wq,
        wk,
        wv,
        wo,
        wg,
        wu,
        attn_in,
        ct_first,
        w_qkv,
        w_o,
        w_gu,
        terms,
        gains_full,
        qkv,
        lse,
        attended,
        mixed,
        mid,
        *scratch,
    ):
        at = Place(n, H)
        normed, xb, stage, wqkv, wout, x_sem, o_sem, w_sem = scratch[rest]
        gsend, grecv, glocal = scratch[g_at]
        at.greet()

        def gain_dst(b):
            return gains_full.at[:, pl.ds(pl.multiple_of(b * R, R), R)]

        mine = pltpu.make_async_copy(gain, gain_dst(at.b), glocal)
        mine.start()
        if at.square:
            first = remote(gain, gain_dst(at.b), gsend.at[0], grecv.at[0], {"batch": at.xn})
            own_y = remote(gain, gain_dst(at.b), gsend.at[1], grecv.at[1], {"batch": at.yn})
            first.start()
            own_y.start()
            got = gain_dst(at.xn)
            remote(got, got, gsend.at[0], grecv.at[0], {"batch": at.xn}).wait_recv()
            fwd = remote(got, got, gsend.at[2], grecv.at[2], {"batch": at.yn})
            fwd.start()
            got = gain_dst(at.yn)
            remote(got, got, gsend.at[1], grecv.at[1], {"batch": at.yn}).wait_recv()
            got = gain_dst(at.dg)
            remote(got, got, gsend.at[2], grecv.at[2], {"batch": at.yn}).wait_recv()
            for job in (first, own_y, fwd):
                job.wait_send()
        else:
            for o in range(1, n):
                remote(gain, gain_dst(at.b), gsend.at[o], grecv.at[o], {"batch": (at.b + o) % n}).start()
            for o in range(1, n):
                got = gain_dst((at.b + n - o) % n)
                remote(got, got, gsend.at[o], grecv.at[o], {"batch": (at.b + o) % n}).wait()
        mine.wait()

        gathers = {("x", r): SlotGather(at, normed.at[r], attn_in.at[r], scratch[z_at[r]]) for r in range(rows)}
        gathers[("ct", 0)] = SlotGather(at, ct.at[0], ct_first, scratch[z_at[rows]])
        total = SlotReduce(at, *scratch[m_at], scratch[ms_at])

        def norm(r):
            def one(part):
                values = tok[r, part, :].astype(F32)
                normed[r, part, :] = (values * inv_root_of(values) * gains_full[0:1, :]).astype(BF16)

            chunk_loop(T, 32, one)
            gathers[("x", r)].begin()

        outs = []
        for src, dst, col, width in (
            (wq, w_qkv, 0, W),
            (wk, w_qkv, W, W),
            (wv, w_qkv, 2 * W, W),
            (wo, w_o, 0, W),
            (wg, w_gu, 0, ff),
            (wu, w_gu, ff, ff),
        ):
            outs.append((src, lambda b, part, dst=dst, col=col, width=width: dst.at[b, part, pl.ds(col, width)]))
        shards = [BatchGather(at, src, out, scratch[w_at[i]]) for i, (src, out) in enumerate(outs)]
        for job in shards[:4]:
            job.start()
        for r in range(rows):
            norm(r)
        gathers[("ct", 0)].begin()

        def weight_loads():
            return [
                pltpu.make_async_copy(w_qkv.at[b], wqkv.at[pl.ds(b * R, R), :], w_sem.at[0]) for b in range(n)
            ] + [pltpu.make_async_copy(w_o.at[b], wout.at[pl.ds(b * R, R), :], w_sem.at[1]) for b in range(n)]

        def x_load(r, b):
            return pltpu.make_async_copy(attn_in.at[r, pl.ds(2 * b, 2)], xb.at[b % 2], x_sem.at[b % 2])

        def make_qkv(r):
            gathers[("x", r)].finish()
            x_load(r, 0).start()
            x_load(r, 1).start()
            if r == 0:
                pltpu.make_async_copy(wqkv, wqkv, w_sem.at[0]).wait()
                pltpu.make_async_copy(wout, wout, w_sem.at[1]).wait()
            for b in range(L):
                x_load(r, b).wait()
                part = pl.ds(b * 2 * T, 2 * T)
                lin = jnp.dot(xb[b % 2].reshape(2 * T, D), wqkv[...], preferred_element_type=F32)
                if b + 2 < L:
                    x_load(r, b + 2).start()
                c, s = cos[r, part, :], sin[r, part, :]
                qkv[r, part, 0:W] = rotate(lin[:, :W], c, s).astype(BF16)
                qkv[r, part, W : 2 * W] = rotate(lin[:, W : 2 * W], c, s).astype(BF16)
                qkv[r, part, 2 * W : 3 * W] = lin[:, 2 * W :].astype(BF16)

        def head(r, h):
            attend(qkv.at[r], st.at[r], lse.at[r], attended.at[r], h, W)

        def store(r, b):
            return pltpu.make_async_copy(stage.at[b % 2], terms.at[r - 1, pl.ds(2 * b, 2)], o_sem.at[b % 2])

        def make_terms(r):
            for b in range(L):
                if b >= 2:
                    store(r, b - 2).wait()
                for j in range(D // wide):
                    cols = pl.ds(j * wide, wide)
                    value = cols_dot(attended[r, pl.ds(b * 2 * T, 2 * T), :], wout[cols, :]).astype(BF16)
                    stage[b % 2, 0, :, cols] = value[:T]
                    stage[b % 2, 1, :, cols] = value[T:]
                store(r, b).start()
            for b in (L - 2, L - 1):
                store(r, b).wait()

        def make_send(i):
            zd = plan.block(at.z, i)
            part = pl.ds(pl.multiple_of(zd * 2 * T, 2 * T), 2 * T)
            for j in range(D // wide):
                cols = pl.ds(j * wide, wide)
                value = cols_dot(attended[0, part, :], wout[cols, :]).astype(BF16)
                stage[i % 2, 0, :, cols] = value[:T]
                stage[i % 2, 1, :, cols] = value[T:]
            total.exchange(zd, stage.at[i % 2, 1 - at.c]).start()

        def combine(i):
            zd = plan.block(at.z, i)
            total.exchange(zd, stage.at[i % 2, 1 - at.c]).wait()
            total.combine(zd, stage.at[i % 2, at.c])

        def finish(j):
            def put(part, value):
                value = value + tok[0, part, :].astype(F32)
                mixed[part, :] = value
                mid[part, :] = (value * inv_root_of(value) * gains_full[1:2, :]).astype(BF16)

            total.final(put)
            total.sent()

        def task(name):
            kind, r, i = name
            if kind == "qkv":
                make_qkv(r)
            elif kind == "low":
                pl.loop(0, heads // 2)(lambda h: head(r, h))
            elif kind == "high":
                pl.loop(heads // 2, heads)(lambda h: head(r, h))
            elif kind == "send":
                make_send(i)
            else:
                make_terms(r)

        def after(s):
            name = plan.tasks[s - 1][0] if s - 1 in plan.tasks else None
            if name and name[0] == "send":
                combine(name[2])
            if s == 3:
                for job in shards[:4]:
                    job.forward()
                for job in shards[4:]:
                    job.start()
            if s == 6:
                for job in shards[:4]:
                    job.finish()
                for job in weight_loads():
                    job.start()
            if s == 11:
                shards[4].forward()
            if s == 15:
                shards[5].forward()

        run_plan(plan, at, {**gathers, mix: total}, task, after, finish)
        gathers[("ct", 0)].finish()
        for job in shards[4:]:
            job.finish()

    return pl.pallas_call(
        kernel,
        out_shape=(
            jax.ShapeDtypeStruct((rows, H, T, D), BF16),
            jax.ShapeDtypeStruct((H, T, D), BF16),
            jax.ShapeDtypeStruct((n, R, 3 * W), BF16),
            jax.ShapeDtypeStruct((n, R, W), BF16),
            jax.ShapeDtypeStruct((n, R, 2 * ff), BF16),
            jax.ShapeDtypeStruct((rows - 1, H, T, D), BF16),
            jax.ShapeDtypeStruct((8, D), F32),
            jax.ShapeDtypeStruct((rows, S, 3 * W), BF16),
            jax.ShapeDtypeStruct((rows, 8, S), F32),
            jax.ShapeDtypeStruct((rows, S, W), BF16),
            jax.ShapeDtypeStruct((T, D), F32),
            jax.ShapeDtypeStruct((T, D), BF16),
        ),
        in_specs=[VMEM, ANY] + [VMEM] * 4 + [ANY] * 6,
        out_specs=(ANY,) * 6 + (VMEM,) * 6,
        scratch_shapes=names.shapes,
        compiler_params=pltpu.CompilerParams(collective_id=1, has_side_effects=True, vmem_limit_bytes=VMEM_LIMIT),
        name="attention_in",
    )(tokens, cotangent, gains, cosine, sine, starts, *weights)


def feed_forward(n, H, terms, ct_first, mixed_first, mid_first, tokens, cotangent, gains, w_gu, w_d):
    rows, T, D = tokens.shape
    L = H // 2
    ff = w_d.shape[1]
    S = H * T
    R = w_d.shape[0]
    U = R // 2
    square = n == 4
    rank = []
    for kinds in (("mix", "in"), ("sum", "att"), ("out",)):
        rank += [(kind, r) for r in range(rows) for kind in kinds if (kind, r) != ("mix", 0)]
        if kinds[0] == "mix":
            rank[2:2] = [("ct", r) for r in range(1, rows)]
    tasks = []
    for r in range(rows):
        for i in range(L):
            needs = (("in", r),) + ((("ct", r),) if r else ())
            made = (("sum", r), ("out", r))
            if r and i < L // 2:
                tasks.append((("both", r, i), needs, made, i, 1))
            else:
                tasks.append((("first", r, i), needs, (), i, 1))
                tasks.append((("second", r, i), (), made, i, 1))
    tasks += [(("grad", k, 0), (), (), 0, 1) for k in range(2 * n)]
    plan = Plan(
        L,
        rank,
        [j for j in rank if j[0] in ("mix", "sum", "out")],
        {("mix", r): [(r - 1) * L + i for i in range(L)] for r in range(1, rows)},
        {(a, r): (b, r) for a, b in (("mix", "in"), ("sum", "att")) for r in range(rows)},
        {("in", 0): 0, **{("ct", r): 0 for r in range(1, rows)}},
        tasks,
    )
    names = Names()
    n_bufs = [names.add(SlotReduce.bufs(L, T, D)) for _ in range(2 * rows)]
    n_sems = [names.add(SlotReduce.sems(L)) for _ in range(2 * rows)]
    n_gsem = [names.add(SlotGather.sems(L)) for _ in range(2 * rows)]
    n_wsem = names.add(BatchGather.sems(n))
    rest = names.add(
        [
            pltpu.VMEM((rows, T, D), BF16),
            pltpu.VMEM((rows, T, D), BF16),
            pltpu.VMEM((rows, T, D), F32),
            pltpu.VMEM((2, 2, T, D), BF16),
            pltpu.VMEM((2, 2, T, D), BF16),
            pltpu.VMEM((max(D, rows * S), 2 * ff), BF16),
            pltpu.VMEM((max(D, rows * S), ff), BF16),
            pltpu.VMEM((2, 2, T, D), BF16),
            pltpu.VMEM((2, 2, T, D), BF16),
            pltpu.VMEM((2, max(2 * T, U), ff), BF16),
            pltpu.VMEM((2, max(2 * T, U), 2 * ff), BF16),
            pltpu.VMEM((2, rows, H, T, U), BF16),
            pltpu.VMEM((2, rows, H, T, U), BF16),
            DMA((6,)),
            DMA((2, 4)),
            DMA((2, 4)),
            DMA((2,)),
            DMA((2,)),
            DMA((rows, L)),
            DMA((2,)),
            DMA((2,)),
            DMA((2,)),
            DMA((2,)),
        ]
    )
    tile = min(512, ff)
    wide = min(512, D)

    def kernel(
        src,
        ct_row,
        mixed_row,
        mid_row,
        tok,
        ct,
        gain,
        wgu_hbm,
        wd_own,
        ctf,
        mlp_in,
        g_att,
        hid_hbm,
        ggu_hbm,
        grad_gu,
        grad_d,
        first_gu,
        first_d,
        g_mixed,
        layer_out,
        gain_sum,
        *scratch,
    ):
        at = Place(n, H)
        z = at.z
        (
            normed,
            att,
            mixed,
            stage_g,
            stage_o,
            wgu,
            wd,
            xb,
            cb,
            hb,
            gb,
            xt,
            ct_t,
            t_sem,
            gsend,
            grecv,
            w_sem,
            row_sem,
            own_sem,
            x_sem,
            c_sem,
            h_sem,
            g_sem,
        ) = scratch[rest]
        loads = [pltpu.make_async_copy(wgu_hbm, wgu.at[pl.ds(0, D), :], w_sem.at[0])]
        down = BatchGather(
            at,
            wd_own,
            lambda b, part: wd.at[pl.ds(pl.multiple_of(b * R + part.start, U), part.size), :],
            scratch[n_wsem],
        )
        row_loads = [
            pltpu.make_async_copy(mixed_row, mixed.at[0], row_sem.at[0]),
            pltpu.make_async_copy(mid_row, normed.at[0], row_sem.at[1]),
        ]
        for job in row_loads:
            job.start()
        red, gat = {}, {}
        for r in range(rows):
            for kind in ("mix", "sum"):
                red[(kind, r)] = SlotReduce(at, *scratch[n_bufs[r]], scratch[n_sems[r]])
            red[("out", r)] = SlotReduce(at, *scratch[n_bufs[rows + r]], scratch[n_sems[rows + r]])
            gat[("in", r)] = SlotGather(at, normed.at[r], mlp_in.at[r], scratch[n_gsem[r]])
            gat[("att", r)] = SlotGather(at, att.at[r], g_att.at[r], scratch[n_gsem[r]])
            if r:
                gat[("ct", r)] = SlotGather(at, ct.at[r], ctf.at[r - 1], scratch[n_gsem[rows + r]])
        both = {**red, **gat}
        at.greet()
        down.start()

        def mine_of(r, zd):
            return red[("out", r)].recv.at[zd]

        def own_load(r, zd):
            return pltpu.make_async_copy(src.at[r - 1, zd * 2 + at.c], mine_of(r, zd), own_sem.at[r, zd])

        def exchange(r, zd):
            return red[("mix", r)].exchange(zd, src.at[r - 1, zd * 2 + 1 - at.c])

        for job in row_loads:
            job.wait()
        gat[("in", 0)].begin()
        for r in range(1, rows):
            for i in range(L):
                zd = plan.block(z, i)
                exchange(r, zd).start()
                own_load(r, zd).start()
        for r in range(1, rows):
            gat[("ct", r)].begin()
        for job in loads:
            job.start()
        gain_sum[...] = jnp.zeros_like(gain_sum)

        def combine_mix(r, i):
            zd = plan.block(z, i)
            own_load(r, zd).wait()
            exchange(r, zd).wait()
            red[("mix", r)].combine(zd, mine_of(r, zd))

        def combine_terms(r, i):
            zd = plan.block(z, i)
            for kind, stage in (("sum", stage_g), ("out", stage_o)):
                job = red[(kind, r)]
                job.exchange(zd, stage.at[i % 2, 1 - at.c]).wait()
                job.combine(zd, stage.at[i % 2, at.c])

        def x_load(r, i):
            blk = plan.block(z, i)
            return (
                pltpu.make_async_copy(mlp_in.at[r, pl.ds(2 * blk, 2)], xb.at[i % 2], x_sem.at[i % 2]),
                pltpu.make_async_copy(
                    (ctf.at[r - 1] if r else ct_row).at[pl.ds(2 * blk, 2)], cb.at[i % 2], c_sem.at[i % 2]
                ),
            )

        def act_store(r, i):
            blk = plan.block(z, i)
            at_row = pl.ds(pl.multiple_of(r * S + blk * 2 * T, 2 * T), 2 * T)
            return (
                pltpu.make_async_copy(hb.at[i % 2, pl.ds(0, 2 * T), :], hid_hbm.at[at_row, :], h_sem.at[i % 2]),
                pltpu.make_async_copy(gb.at[i % 2, pl.ds(0, 2 * T), :], ggu_hbm.at[at_row, :], g_sem.at[i % 2]),
            )

        def first_part(r, i):
            if i == 0:
                gat[("in", r)].finish()
                if r:
                    gat[("ct", r)].finish()
                for job in x_load(r, 0):
                    job.start()
                if r == 0:
                    down.finish()
                    for job in loads:
                        job.wait()
            for job in x_load(r, i):
                job.wait()
            if i + 1 < L:
                for job in x_load(r, i + 1):
                    job.start()
            if r * L + i >= 2:
                before = (r, i - 2) if i >= 2 else (r - 1, L + i - 2)
                for job in act_store(*before):
                    job.wait()
            k = i % 2

            @pl.loop(0, ff // tile)
            def _(j):
                cols = pl.ds(pl.multiple_of(j * tile, tile), tile)
                up_cols = pl.ds(pl.multiple_of(ff + j * tile, tile), tile)
                x = xb[k].reshape(2 * T, D)
                gate = jnp.dot(x, wgu[0:D, cols], preferred_element_type=F32)
                up = jnp.dot(x, wgu[0:D, up_cols], preferred_element_type=F32)
                back = jnp.dot(cb[k].reshape(2 * T, D), wd[0:D, cols], preferred_element_type=F32)
                sig = 1.0 / (1.0 + jnp.exp(-gate))
                silu = gate * sig
                hb[k, 0 : 2 * T, cols] = (silu * up).astype(BF16)
                gb[k, 0 : 2 * T, cols] = (back * up * (sig * (1.0 + gate * (1.0 - sig)))).astype(BF16)
                gb[k, 0 : 2 * T, up_cols] = (back * silu).astype(BF16)

            for job in act_store(r, i):
                job.start()

        def second_part(r, i):
            k = i % 2

            @pl.loop(0, D // wide)
            def _(j):
                cols = pl.ds(pl.multiple_of(j * wide, wide), wide)
                back = cols_dot(gb[k, 0 : 2 * T, :], wgu[cols, :]).astype(BF16)
                stage_g[k, 0, :, cols] = back[:T]
                stage_g[k, 1, :, cols] = back[T:]
                out = cols_dot(hb[k, 0 : 2 * T, :], wd[cols, :]).astype(BF16)
                stage_o[k, 0, :, cols] = out[:T]
                stage_o[k, 1, :, cols] = out[T:]

            zd = plan.block(z, i)
            for kind, stage in (("sum", stage_g), ("out", stage_o)):
                red[(kind, r)].exchange(zd, stage.at[k, 1 - at.c]).start()

        def finish_mix(r):
            def put(part, value):
                value = value + tok[r, part, :].astype(F32)
                mixed[r, part, :] = value
                normed[r, part, :] = (value * inv_root_of(value) * gain[1:2, :]).astype(BF16)

            red[("mix", r)].final(put)
            red[("mix", r)].sent()
            gat[("in", r)].begin()

        def finish_sum(r):
            def put(part, value):
                back, gain_part = norm_back_part(mixed[r, part, :], gain[1:2, :], value)
                total = ct[r, part, :].astype(F32) + back
                g_mixed[r, part, :] = total
                att[r, part, :] = total.astype(BF16)
                gain_sum[1:2, :] += gain_part

            red[("sum", r)].final(put)
            red[("sum", r)].sent()
            gat[("att", r)].begin()

        def finish_out(r):
            def put(part, value):
                layer_out[r, part, :] = (mixed[r, part, :] + value).astype(BF16)

            red[("out", r)].final(put)
            red[("out", r)].sent()

        units = send_units(at, square, n)
        again = [
            pltpu.make_async_copy(ggu_hbm, wgu.at[pl.ds(0, rows * S), :], w_sem.at[0]),
            pltpu.make_async_copy(hid_hbm, wd.at[pl.ds(0, rows * S), :], w_sem.at[1]),
        ]

        def columns(k):
            cols = pl.ds(pl.multiple_of((units[k][0] * 2 + units[k][1]) * U, U), U)
            return [
                pltpu.make_async_copy(mlp_in.at[:, :, :, cols], xt.at[k % 2], t_sem.at[k % 2]),
                pltpu.make_async_copy(ct_row.at[:, :, cols], ct_t.at[k % 2, 0], t_sem.at[2 + k % 2]),
                pltpu.make_async_copy(
                    ctf.at[:, :, :, cols], ct_t.at[k % 2, pl.ds(1, rows - 1)], t_sem.at[4 + k % 2]
                ),
            ]

        def grad_store(k):
            b, half = units[k][:2]
            part = pl.ds(half * U, U)
            return [
                pltpu.make_async_copy(hb.at[k % 2, pl.ds(0, U), :], grad_d.at[b, part, :], h_sem.at[k % 2]),
                pltpu.make_async_copy(gb.at[k % 2, pl.ds(0, U), :], grad_gu.at[b, part, :], g_sem.at[k % 2]),
            ]

        def grad_sends(k):
            b, half, slot, to = units[k]
            part = pl.ds(half * U, U)
            return [
                remote(src.at[b, part, :], dst.at[slot], gsend.at[a, k], grecv.at[a, slot], {"batch": to})
                for a, (src, dst) in enumerate(((grad_d, first_d), (grad_gu, first_gu)))
            ]

        def prepare_grads():
            for i in (L - 2, L - 1):
                for job in act_store(rows - 1, i):
                    job.wait()
            for job in again + columns(0):
                job.start()

        def grad(k):
            if k == 0:
                for job in again:
                    job.wait()
            for job in columns(k):
                job.wait()
            if k + 1 < 2 * n:
                for job in columns(k + 1):
                    job.start()
            ring = k % 2

            @pl.loop(0, 2 * ff // tile)
            def _(j):
                cols = pl.ds(pl.multiple_of(j * tile, tile), tile)
                x = xt[ring].reshape(rows * S, U)
                gb[ring, 0:U, cols] = rows_dot(x, wgu[0 : rows * S, cols]).astype(BF16)

            @pl.loop(0, ff // tile)
            def _(j):
                cols = pl.ds(pl.multiple_of(j * tile, tile), tile)
                x = ct_t[ring].reshape(rows * S, U)
                hb[ring, 0:U, cols] = rows_dot(x, wd[0 : rows * S, cols]).astype(BF16)

            for job in grad_store(k):
                job.start()

        def task(name):
            kind, r, i = name
            if kind == "first":
                first_part(r, i)
            elif kind in ("second", "both"):
                if kind == "both":
                    first_part(r, i)
                second_part(r, i)
                if (r, i) == (rows - 1, L - 1):
                    prepare_grads()
            else:
                grad(r)

        def after(s):
            if s == 4:
                down.forward()
            if s + 1 < (rows - 1) * L:
                combine_mix(1 + (s + 1) // L, (s + 1) % L)
            name = plan.tasks[s - 1][0] if s - 1 in plan.tasks else None
            if name and name[0] in ("second", "both"):
                combine_terms(*name[1:])
            if name and name[0] == "grad":
                for job in grad_store(name[1]):
                    job.wait()
                if units[name[1]][3] is not None:
                    for job in grad_sends(name[1]):
                        job.start()

        def finish(j):
            {"mix": finish_mix, "sum": finish_sum, "out": finish_out}[j[0]](j[1])

        combine_mix(1, 0)
        run_plan(plan, at, both, task, after, finish)
        if square:
            for k in range(4):
                for job in grad_sends(k):
                    job.wait()
        for r in range(rows):
            gat[("att", r)].finish()

    return pl.pallas_call(
        kernel,
        out_shape=(
            jax.ShapeDtypeStruct((rows - 1, H, T, D), BF16),
            jax.ShapeDtypeStruct((rows, H, T, D), BF16),
            jax.ShapeDtypeStruct((rows, H, T, D), BF16),
            jax.ShapeDtypeStruct((rows * S, ff), BF16),
            jax.ShapeDtypeStruct((rows * S, 2 * ff), BF16),
            jax.ShapeDtypeStruct((n, 2 * U, 2 * ff), BF16),
            jax.ShapeDtypeStruct((n, 2 * U, ff), BF16),
            jax.ShapeDtypeStruct((4, U, 2 * ff), BF16),
            jax.ShapeDtypeStruct((4, U, ff), BF16),
            jax.ShapeDtypeStruct((rows, T, D), F32),
            jax.ShapeDtypeStruct((rows, T, D), BF16),
            jax.ShapeDtypeStruct((8, D), F32),
        ),
        in_specs=[ANY, ANY, ANY, ANY, VMEM, VMEM, VMEM, ANY, ANY],
        out_specs=(ANY,) * 9 + (VMEM, VMEM, VMEM),
        scratch_shapes=names.shapes,
        compiler_params=pltpu.CompilerParams(collective_id=2, has_side_effects=True, vmem_limit_bytes=VMEM_LIMIT),
        name="feed_forward",
    )(terms, ct_first, mixed_first, mid_first, tokens, cotangent, gains, w_gu, w_d)


class LateReduce:
    def __init__(self, at, src, first, bufs, sems):
        self.at, self.src, self.first = at, src, first
        self.mine, self.came, self.second = bufs
        self.load, self.send, self.recv = sems
        self.U = first.shape[1]

    @staticmethod
    def bufs(U, K):
        return [pltpu.VMEM((2, U, K), BF16)] * 3

    @staticmethod
    def sems():
        return [DMA((4,)), DMA((2,)), DMA((2,))]

    def loads(self, j, own):
        at, U = self.at, self.U
        if j == 0:
            y = at.y if own else 1 - at.y
            b, slot = y * 2 + at.x, y
        else:
            x = at.x if own else 1 - at.x
            b, slot = at.y * 2 + x, 2 + x
        return [
            pltpu.make_async_copy(self.src.at[b, pl.ds(j * U, U), :], self.mine.at[j], self.load.at[2 * j]),
            pltpu.make_async_copy(self.first.at[slot], self.came.at[j], self.load.at[2 * j + 1]),
        ]

    def pass_on(self, j):
        to = {"batch": self.at.xn if j else self.at.yn}
        return remote(self.mine.at[j], self.second.at[j], self.send.at[j], self.recv.at[j], to)

    def start(self):
        for j in (0, 1):
            for job in self.loads(j, False):
                job.start()

    def second_step(self):
        for j in (0, 1):
            for job in self.loads(j, False):
                job.wait()

            def add(rows, j=j):
                self.mine[j, rows, :] = (self.mine[j, rows, :].astype(F32) + self.came[j, rows, :].astype(F32)).astype(BF16)

            chunk_loop(self.U, 16, add)
            self.pass_on(j).start()

    def reload(self):
        for j in (0, 1):
            self.pass_on(j).wait()
            for job in self.loads(j, True):
                job.start()

    def final(self, j, step, put):
        for job in self.loads(j, True):
            job.wait()

        @pl.loop(0, self.U // step)
        def _(i):
            rows = pl.ds(pl.multiple_of(i * step, step), step)
            put(
                i,
                self.mine[j, rows, :].astype(F32) + self.came[j, rows, :].astype(F32) + self.second[j, rows, :].astype(F32),
            )


def send_units(at, square, n):
    if not square:
        return [(k // 2, k % 2, None, None) for k in range(2 * n)]
    return [
        ((1 - at.y) * 2 + 1 - at.x, 0, 1 - at.y, at.xn),
        ((1 - at.y) * 2 + 1 - at.x, 1, 3 - at.x, at.yn),
        (at.y * 2 + 1 - at.x, 0, at.y, at.xn),
        ((1 - at.y) * 2 + at.x, 1, 2 + at.x, at.yn),
        ((1 - at.y) * 2 + at.x, 0, None, None),
        (at.y * 2 + 1 - at.x, 1, None, None),
        (at.b, 0, None, None),
        (at.b, 1, None, None),
    ]


def attention_back(
    n,
    H,
    g_att,
    attended,
    qkv,
    lse,
    attn_in,
    w_qkv,
    w_o,
    cosine,
    sine,
    starts,
    tokens,
    g_mixed,
    gains,
    gain_sum,
    g_gu,
    g_d,
    first_gu,
    first_d,
):
    rows, T, D = tokens.shape
    L = H // 2
    S = H * T
    R, ff = g_d.shape[1], g_d.shape[2]
    W = w_o.shape[1]
    heads = W // HEAD_DIM
    U = R // 2
    square = n == 4
    step = min(256, S)
    wide = min(512, D)
    blocks = S // step
    rank = [("in", r) for r in range(rows)]
    tasks = []
    for r in range(rows):
        tasks.append((("prob", r, 0), (), (), 0, 1))
        if r == 0:
            tasks.append((("heads", r, 0), (), (), 0, 1))
        else:
            tasks += [(("head", r, h), (), (), 0, 1) for h in range(heads)]
        tasks += [(("terms", r, i), (), (("in", r),), i, 1) for i in range(L)]
    tasks += [(("grad", k, 0), (), (), 0, 1) for k in range(n)]
    plan = Plan(L, rank, rank, {}, {}, {}, tasks)
    names = Names()
    r_bufs = [names.add(SlotReduce.bufs(L, T, D)) for _ in range(rows)]
    r_sems = [names.add(SlotReduce.sems(L)) for _ in range(rows)]
    if square:
        m_bufs = [names.add(LateReduce.bufs(U, K)) for K in (ff, 2 * ff)]
        m_sems = [names.add(LateReduce.sems()) for _ in range(2)]
        a_bufs = names.add([pltpu.VMEM((4, U, 4 * W), BF16), pltpu.VMEM((2, U, 4 * W), BF16)])
        a_sems = names.add([DMA((6,)), DMA((6,))])
    else:
        m_bufs = [names.add(BatchReduce.bufs(n, R, K)) for K in (ff, 2 * ff)]
        m_sems = [names.add(BatchReduce.sems(n)) for _ in range(2)]
        a_bufs = names.add([pltpu.VMEM((n, 2, U, 4 * W), BF16)])
        a_sems = names.add([DMA((n,)), DMA((n,))])
    s_at = names.add(
        [pltpu.VMEM((8, D), F32), pltpu.VMEM((n, 8, R), F32), pltpu.VMEM((H, 8, R), F32)]
        + [DMA((n,)), DMA((n,)), DMA((H,)), DMA((H,)), DMA]
    )
    rest = names.add(
        [
            pltpu.VMEM((2, step, D), BF16),
            pltpu.VMEM((S, W), BF16),
            pltpu.VMEM((S, W), F32),
            pltpu.VMEM((S, W), F32),
            pltpu.VMEM((S, W), F32),
            pltpu.VMEM((rows * S, 3 * W), BF16),
            pltpu.VMEM((2, 2, T, D), BF16),
            pltpu.VMEM((2, rows * S, U), BF16),
            pltpu.VMEM((2, rows * S, U), BF16),
            pltpu.VMEM((2 * n, U, 4 * W), BF16),
            pltpu.VMEM((4, 32, 2 * ff), F32),
            DMA((2,)),
            DMA((4,)),
            DMA((4, 2)),
            DMA,
        ]
    )

    def kernel(
        ga,
        att,
        qkv,
        ls,
        x_hbm,
        wq,
        wo,
        cos,
        sin,
        st,
        tok,
        gmix,
        gain,
        gain_in,
        ggu,
        gd,
        fgu,
        fd,
        grad_in,
        out_q,
        out_k,
        out_v,
        out_o,
        ggate,
        gup,
        gdown,
        gain_out,
        *scratch,
    ):
        at = Place(n, H)
        z = at.z
        small, over_batch, over_head, bsend, brecv, hsend, hrecv, local = scratch[s_at]
        gab, gat, gq, gk, gv, gqkv, stage, xt, gt, units_buf, out_buf, ga_sem, t_sem, o_sem, mix_sem = scratch[rest]
        sums = {("in", r): SlotReduce(at, *scratch[r_bufs[r]], scratch[r_sems[r]]) for r in range(rows)}
        asend, arecv = scratch[a_sems]
        units = send_units(at, square, n)
        take_mix = pltpu.make_async_copy(gmix, grad_in, mix_sem)
        take_mix.start()

        def ga_load(g):
            return pltpu.make_async_copy(
                ga.at[g // blocks, pl.ds(g % blocks * step, step), :], gab.at[g % 2], ga_sem.at[g % 2]
            )

        ga_load(0).start()
        ga_load(1).start()
        at.greet(all_heads=True)
        if square:
            mlp = [
                LateReduce(at, src, first, scratch[m_bufs[i]], scratch[m_sems[i]])
                for i, (src, first) in enumerate(((gd, fd), (ggu, fgu)))
            ]
        else:
            mlp = [BatchReduce(at, src, scratch[m_bufs[i]], scratch[m_sems[i]]) for i, src in enumerate((gd, ggu))]
        for job in mlp:
            job.start()
        small[...] = gain_in[...]
        for job in mlp:
            job.second_step()

        def prob(r):
            gq[...] = jnp.zeros_like(gq)
            gk[...] = jnp.zeros_like(gk)
            gv[...] = jnp.zeros_like(gv)
            for b in range(blocks):
                g = r * blocks + b
                ga_load(g).wait()
                gat[b * step : (b + 1) * step, :] = jnp.dot(gab[g % 2], wo[...], preferred_element_type=F32).astype(BF16)
                if g + 2 < rows * blocks:
                    ga_load(g + 2).start()

        def head(r, h):
            attend_back(qkv.at[r], st.at[r], ls.at[r], gat, gq, gk, gv, h, W)

        def terms(r, i):
            zd = plan.block(z, i)
            k = i % 2
            part = pl.ds(pl.multiple_of(zd * 2 * T, 2 * T), 2 * T)
            c, s = cos[r, part, :], -sin[r, part, :]
            keep = pl.ds(pl.multiple_of(r * S + zd * 2 * T, 2 * T), 2 * T)
            gqkv[keep, 0:W] = rotate(gq[part, :], c, s).astype(BF16)
            gqkv[keep, W : 2 * W] = rotate(gk[part, :], c, s).astype(BF16)
            gqkv[keep, 2 * W : 3 * W] = gv[part, :].astype(BF16)

            @pl.loop(0, D // wide)
            def _(j):
                cols = pl.ds(pl.multiple_of(j * wide, wide), wide)
                back = cols_dot(gqkv[keep, :], wq[cols, :]).astype(BF16)
                stage[k, 0, :, cols] = back[:T]
                stage[k, 1, :, cols] = back[T:]

            sums[("in", r)].exchange(zd, stage.at[k, 1 - at.c]).start()

        def combine_terms(r, i):
            zd = plan.block(z, i)
            job = sums[("in", r)]
            job.exchange(zd, stage.at[i % 2, 1 - at.c]).wait()
            job.combine(zd, stage.at[i % 2, at.c])

        def columns(k):
            cols = pl.ds(pl.multiple_of((units[k][0] * 2 + units[k][1]) * U, U), U)
            return [pltpu.make_async_copy(x_hbm.at[:, cols], xt.at[k % 2], t_sem.at[k % 2])] + [
                pltpu.make_async_copy(
                    ga.at[r, :, cols], gt.at[k % 2, pl.ds(r * S, S), :], t_sem.at[2 + k % 2]
                )
                for r in range(rows)
            ]

        def columns_wait(k):
            pltpu.make_async_copy(xt.at[k % 2], xt.at[k % 2], t_sem.at[k % 2]).wait()
            pltpu.make_async_copy(gt.at[k % 2], gt.at[k % 2], t_sem.at[2 + k % 2]).wait()

        def grad(k):
            if k == 0:
                for job in columns(0):
                    job.start()
            columns_wait(k)
            if k + 1 < 2 * n:
                for job in columns(k + 1):
                    job.start()
            units_buf[k, :, 0 : 3 * W] = rows_dot(xt[k % 2], gqkv[...]).astype(BF16)
            units_buf[k, :, 3 * W : 4 * W] = rows_dot(gt[k % 2], att[...].reshape(rows * S, W)).astype(BF16)
            if units[k][3] is not None:
                unit_send(k).start()

        if square:
            a_first, a_second = scratch[a_bufs]

            def unit_send(k):
                _, _, slot, to = units[k]
                return remote(units_buf.at[k], a_first.at[slot], asend.at[k], arecv.at[slot], {"batch": to})

            def unit_pass(j):
                to = at.xn if j else at.yn
                return remote(units_buf.at[4 + j], a_second.at[j], asend.at[4 + j], arecv.at[4 + j], {"batch": to})

            def unit_second():
                for j, k, slot in ((0, 0, 1 - at.y), (1, 1, 3 - at.x)):
                    unit_send(k).wait_recv()

                    def add(part, j=j, slot=slot):
                        units_buf[4 + j, part, :] = (
                            units_buf[4 + j, part, :].astype(F32) + a_first[slot, part, :].astype(F32)
                        ).astype(BF16)

                    chunk_loop(U, 16, add)
                    unit_pass(j).start()

            def unit_final(put):
                for j, k, slot in ((0, 2, at.y), (1, 3, 2 + at.x)):
                    unit_send(k).wait_recv()
                    unit_pass(j).wait_recv()

                    @pl.loop(0, U // 16)
                    def _(i, j=j, slot=slot):
                        r = pl.multiple_of(i * 16, 16)
                        part = pl.ds(r, 16)
                        put(
                            pl.ds(r + j * U, 16),
                            units_buf[6 + j, part, :].astype(F32)
                            + a_first[slot, part, :].astype(F32)
                            + a_second[j, part, :].astype(F32),
                        )

                for k in range(4):
                    unit_send(k).wait_send()
                for j in (0, 1):
                    unit_pass(j).wait_send()

        else:
            (a_slots,) = scratch[a_bufs]

            def unit_direct(off):
                to = (at.b + off) % n
                return remote(
                    units_buf.at[pl.ds(2 * to, 2)], a_slots.at[off], asend.at[off], arecv.at[off], {"batch": to}
                )

            def unit_second():
                for off in range(1, n):
                    unit_direct(off).start()

            def unit_final(put):
                for off in range(1, n):
                    unit_direct(off).wait()
                for j in (0, 1):

                    @pl.loop(0, U // 16)
                    def _(i, j=j):
                        r = pl.multiple_of(i * 16, 16)
                        part = pl.ds(r, 16)
                        total = units_buf[2 * at.b + j, part, :].astype(F32)
                        for off in range(1, n):
                            total = total + a_slots[off, j, part, :].astype(F32)
                        put(pl.ds(r + j * U, 16), total)

        def finish(j):
            r = j[1]

            def put(part, value):
                back, gain_part = norm_back_part(tok[r, part, :].astype(F32), gain[0:1, :], value)
                grad_in[r, part, :] += back
                small[0:1, :] += gain_part

            sums[j].final(put)
            sums[j].sent()

        def task(name):
            kind, r, i = name
            if kind == "prob":
                prob(r)
                if r == 0:
                    take_mix.wait()
            elif kind == "heads":
                pl.loop(0, heads)(lambda h: head(r, h))
            elif kind == "head":
                head(r, i)
            elif kind == "terms":
                terms(r, i)
            else:
                grad(2 * r)
                grad(2 * r + 1)

        def out_copies(outs, r, ring, step):
            return [
                pltpu.make_async_copy(
                    out_buf.at[ring, pl.ds(0, step), pl.ds(a * ff, ff)], dst.at[pl.ds(r, step), :], o_sem.at[ring, a]
                )
                for a, dst in enumerate(outs)
            ]

        mlp_outs = ((gdown,), (ggate, gup))

        def mlp_half(a, j):
            step = min(32, U)
            count = U // step
            outs = mlp_outs[a]

            def put(i, value):
                ring = i % 4

                @pl.when(i >= 4)
                def _():
                    for copy in out_copies(outs, j * U, ring, step):
                        copy.wait()

                out_buf[ring, 0:step, 0 : len(outs) * ff] = value
                for copy in out_copies(outs, pl.multiple_of(j * U + i * step, step), ring, step):
                    copy.start()

            mlp[a].final(j, step, put)
            for ring in range(min(4, count)):
                for copy in out_copies(outs, j * U, ring, step):
                    copy.wait()

        def mlp_whole(a):
            outs = mlp_outs[a]

            def put(part, value):
                out_buf[0, 0:16, 0 : len(outs) * ff] = value
                for copy in out_copies(outs, part.start, 0, 16):
                    copy.start()
                for copy in out_copies(outs, part.start, 0, 16):
                    copy.wait()

            mlp[a].final(put)
            mlp[a].finish()

        grads_at = min(s for s, task in plan.tasks.items() if task[0][0] == "grad")

        def after(s):
            name = plan.tasks[s - 1][0] if s - 1 in plan.tasks else None
            if name and name[0] == "terms":
                combine_terms(*name[1:])
            if square:
                if s == grads_at + 1:
                    for job in mlp:
                        job.reload()
                if s == grads_at + 2:
                    mlp_half(0, 0)
                    mlp_half(0, 1)
                if s == grads_at + 4:
                    mlp_half(1, 0)
            if s == grads_at + n - 1:
                unit_second()

        run_plan(plan, at, sums, task, after, finish)

        def slice_of(b):
            return small.at[:, pl.ds(pl.multiple_of(b * R, R), R)]

        def batch_job(off):
            to = (at.b + off) % n
            return remote(slice_of(to), over_batch.at[off], bsend.at[off], brecv.at[off], {"batch": to})

        for off in range(1, n):
            batch_job(off).start()
        mine = pltpu.make_async_copy(slice_of(at.b), over_batch.at[0], local)
        mine.start()
        if square:
            mlp_half(1, 1)
        else:
            mlp_whole(0)
            mlp_whole(1)
        mine.wait()
        total = over_batch[0]
        for off in range(1, n):
            batch_job(off).wait_recv()
            total = total + over_batch[off]
        over_head[at.h] = total

        def head_job(off, block):
            to = (at.h + off) % H
            return remote(over_head.at[block], over_head.at[block], hsend.at[off], hrecv.at[off], {"head": to})

        for off in range(1, H):
            head_job(off, at.h).start()

        def put_units(part, value):
            out_q[part, :] = value[:, :W]
            out_k[part, :] = value[:, W : 2 * W]
            out_v[part, :] = value[:, 2 * W : 3 * W]
            out_o[part, :] = value[:, 3 * W :]

        unit_final(put_units)
        for off in range(1, H):
            head_job(off, (at.h + H - off) % H).wait_recv()
        total = over_head[0]
        for h in range(1, H):
            total = total + over_head[h]
        gain_out[...] = total
        for off in range(1, n):
            batch_job(off).wait_send()
        for off in range(1, H):
            head_job(off, at.h).wait_send()

    weight = jax.ShapeDtypeStruct((R, W), F32)
    wide_weight = jax.ShapeDtypeStruct((R, ff), F32)
    return pl.pallas_call(
        kernel,
        out_shape=(
            jax.ShapeDtypeStruct((rows, T, D), F32),
            weight,
            weight,
            weight,
            weight,
            wide_weight,
            wide_weight,
            wide_weight,
            jax.ShapeDtypeStruct((8, R), F32),
        ),
        in_specs=[ANY, VMEM, VMEM, VMEM, ANY] + [VMEM] * 6 + [ANY, VMEM, VMEM] + [ANY] * 4,
        out_specs=(VMEM,) * 5 + (ANY,) * 3 + (VMEM,),
        scratch_shapes=names.shapes,
        compiler_params=pltpu.CompilerParams(collective_id=4, has_side_effects=True, vmem_limit_bytes=BACK_LIMIT),
        name="attention_back",
    )(
        g_att,
        attended,
        qkv,
        lse,
        attn_in,
        w_qkv,
        w_o,
        cosine,
        sine,
        starts,
        tokens,
        g_mixed,
        gains,
        gain_sum,
        g_gu,
        g_d,
        first_gu,
        first_d,
    )


def rows_dot(left, right):
    return lax.dot_general(left, right, (((0,), (0,)), ((), ())), preferred_element_type=F32)


def cols_dot(left, right):
    return lax.dot_general(left, right, (((1,), (1,)), ((), ())), preferred_element_type=F32)


QUERIES = 256


def rope_tables(positions):
    half_dim = HEAD_DIM // 2
    frequency = rope_base ** (-(jnp.arange(half_dim).astype(F32) * 2.0) / HEAD_DIM)
    angles = positions.astype(F32)[:, :, None] * frequency
    cosine, sine = jnp.cos(angles), jnp.sin(angles)
    return jnp.concatenate([cosine] * 4, axis=-1), jnp.concatenate([-sine, sine] * 2, axis=-1)


def rotate(values, cosine, sine):
    half_dim = HEAD_DIM // 2
    parts = []
    for g in range(values.shape[1] // 128):
        part = values[:, g * 128 : (g + 1) * 128]
        lane = lax.broadcasted_iota(jnp.int32, part.shape, 1)
        swapped = jnp.where(
            lane % HEAD_DIM < half_dim, pltpu.roll(part, 128 - half_dim, 1), pltpu.roll(part, half_dim, 1)
        )
        parts.append(part * cosine + swapped * sine)
    return jnp.concatenate(parts, axis=1) if len(parts) > 1 else parts[0]


def only_head(values, h):
    lane = lax.broadcasted_iota(jnp.int32, values.shape, 1)
    return jnp.where(lane // HEAD_DIM == h, values, jnp.zeros_like(values))


def masked_scores(keys, query, starts, first):
    scores = cols_dot(keys, query)
    key_index = lax.broadcasted_iota(jnp.int32, scores.shape, 0)
    query_index = lax.broadcasted_iota(jnp.int32, scores.shape, 1) + first
    return jnp.where((key_index >= starts) & (key_index <= query_index), scores, masked_value)


def attend(qkv, starts, lse, attended, h, W):
    S = qkv.shape[0]
    scale = HEAD_DIM**-0.5
    block = min(QUERIES, S)
    for i in range(S // block):
        rows = pl.ds(i * block, block)
        width = (i + 1) * block
        query = only_head(qkv[rows, 0:W], h) * jnp.asarray(scale, BF16)
        scores = masked_scores(qkv[0:width, W : 2 * W], query, starts[:, rows], i * block)
        top = jnp.max(scores, axis=0, keepdims=True)
        weights = jnp.exp(scores - top)
        total = jnp.sum(weights, axis=0, keepdims=True)
        lse[pl.ds(h, 1), rows] = top + jnp.log(total)
        probs = (weights * (1.0 / total)).astype(BF16)
        out = rows_dot(probs, qkv[0:width, 2 * W : 3 * W]).astype(BF16)
        lane = lax.broadcasted_iota(jnp.int32, out.shape, 1)
        attended[rows, :] = jnp.where(lane // HEAD_DIM == h, out, attended[rows, :])


def attend_back(qkv, starts, lse, grad, g_query, g_key, g_value, h, W):
    S = qkv.shape[0]
    scale = HEAD_DIM**-0.5
    block = min(QUERIES, S)
    for i in range(S // block):
        rows = pl.ds(i * block, block)
        width = (i + 1) * block
        query = only_head(qkv[rows, 0:W], h) * jnp.asarray(scale, BF16)
        keys = qkv[0:width, W : 2 * W]
        scores = masked_scores(keys, query, starts[:, rows], i * block)
        probs = jnp.exp(scores - lse[pl.ds(h, 1), rows])
        back = only_head(grad[rows, :], h)
        g_prob = cols_dot(qkv[0:width, 2 * W : 3 * W], back)
        delta = jnp.sum(probs * g_prob, axis=0, keepdims=True)
        g_score = (probs * (g_prob - delta)).astype(BF16)
        g_value[0:width, :] += jnp.dot(probs.astype(BF16), back, preferred_element_type=F32)
        g_key[0:width, :] += jnp.dot(g_score, query, preferred_element_type=F32)
        g_query[rows, :] += only_head(rows_dot(g_score, keys) * scale, h)


def hand_out(arrays):
    count = len(arrays)

    def kernel(*refs):
        sem = refs[-1]
        jobs = [pltpu.make_async_copy(refs[i], refs[count + i], sem.at[i]) for i in range(count)]
        for job in jobs:
            job.start()
        for job in jobs:
            job.wait()

    return pl.pallas_call(
        kernel,
        out_shape=tuple(jax.ShapeDtypeStruct(a.shape, a.dtype) for a in arrays),
        in_specs=[ANY] * count,
        out_specs=(ANY,) * count,
        scratch_shapes=[DMA((count,))],
        name="hand_out",
    )(*arrays)


def per_device(
    n,
    H,
    tokens,
    segment_ids,
    position_ids,
    w_query,
    w_key,
    w_value,
    w_output,
    w_gate,
    w_up,
    w_down,
    attn_gain,
    mlp_gain,
    cotangent,
):
    rows, T, D = tokens.shape
    S = T * H
    R, hw = w_query.shape
    ff = w_gate.shape[1]
    shard_gains = jnp.concatenate(
        [attn_gain.astype(F32)[None], mlp_gain.astype(F32)[None], jnp.zeros((6, R), F32)], axis=0
    )
    cosine, sine = rope_tables(position_ids)
    starts = (jnp.arange(S, dtype=jnp.int32)[None, :] - position_ids)[:, None, :]
    attn_in, ct_first, w_qkv, w_o, w_gu, terms, gains, qkv, lse, attended, mixed_first, mid_first = attention_in(
        n, H, tokens, cotangent, shard_gains, (w_query, w_key, w_value, w_output, w_gate, w_up), cosine, sine, starts
    )
    w_qkv = w_qkv.reshape(D, 3 * hw)
    w_o = w_o.reshape(D, hw)
    w_gu = w_gu.reshape(D, 2 * ff)
    _, _, g_att, _, _, grad_gu, grad_d, first_gu, first_d, g_mixed, layer_out, gain_sum = feed_forward(
        n, H, terms, ct_first, mixed_first, mid_first, tokens, cotangent, gains, w_gu, w_down
    )
    grad_input, grad_q, grad_k, grad_v, grad_out, grad_gate, grad_up, grad_down, gain_grads = attention_back(
        n,
        H,
        g_att.reshape(rows, S, D),
        attended,
        qkv,
        lse,
        attn_in.reshape(rows * S, D),
        w_qkv,
        w_o,
        cosine,
        sine,
        starts,
        tokens,
        g_mixed,
        gains,
        gain_sum,
        grad_gu,
        grad_d,
        first_gu,
        first_d,
    )
    results = hand_out(
        (layer_out, grad_input, grad_q, grad_k, grad_v, grad_out, grad_gate, grad_up, grad_down)
    )
    return (*results, gain_grads[0], gain_grads[1])


def solution(mesh):
    row = P("batch", "head", None)
    ids = P("batch", None)
    weight = P("batch", "head")
    gain = P("batch")
    return jax.shard_map(
        functools.partial(per_device, mesh.shape["batch"], mesh.shape["head"]),
        mesh=mesh,
        in_specs=(row, ids, ids) + (weight,) * 7 + (gain, gain, row),
        out_specs=(row, row) + (weight,) * 7 + (gain, gain),
        check_vma=False,
    )
```

```python
import functools

import jax
import jax.numpy as jnp
import numpy as np
from jax import lax
from jax.experimental import pallas as pl
from jax.experimental.pallas import tpu as pltpu
from jax.sharding import PartitionSpec as P

HEAD_DIM = 64
epsilon = 1e-05
rope_base = 130000.0
masked_value = -1000000000.0
MESH = pl.DeviceIdType.MESH
F32 = jnp.float32
BF16 = jnp.bfloat16
DMA = pltpu.SemaphoreType.DMA
ANY = pl.BlockSpec(memory_space=pl.ANY)
VMEM = pl.BlockSpec(memory_space=pltpu.VMEM)
VMEM_LIMIT = 60 * 2**20
BACK_LIMIT = 63 * 2**20


class Place:
    def __init__(self, batch, head):
        self.n, self.H = batch, head
        self.L = head // 2
        self.b = lax.axis_index("batch")
        self.h = lax.axis_index("head")
        self.z = self.h // 2
        self.c = self.h % 2
        self.sib = self.z * 2 + (1 - self.c)
        self.up = self.h + 2
        self.down = self.h - 2
        self.x, self.y = self.b % 2, self.b // 2
        self.xn = self.y * 2 + (1 - self.x)
        self.yn = (1 - self.y) * 2 + self.x
        self.dg = (1 - self.y) * 2 + (1 - self.x)
        self.square = batch == 4

    def greet(self, line=True, batch=True, all_heads=False, all_batch=False):
        barrier = pltpu.get_barrier_semaphore()
        me, L = self, self.L

        def hello(device):
            pl.semaphore_signal(barrier, inc=1, device_id=device, device_id_type=MESH)

        count = 0
        if all_heads:
            for off in range(1, self.H):
                hello({"head": (me.h + off) % self.H})
                count += 1
        elif line:
            hello({"head": me.sib})
            count += 1

            @pl.when(me.z > 0)
            def _():
                hello({"head": me.down})

            @pl.when(me.z < L - 1)
            def _():
                hello({"head": me.up})

        if batch:
            if self.square and not all_heads and not all_batch:
                hello({"batch": me.xn})
                hello({"batch": me.yn})
                count += 2
            else:
                for off in range(1, self.n):
                    hello({"batch": (me.b + off) % self.n})
                    count += 1
        if line and not all_heads:
            count = count + jnp.minimum(me.z, 1) + jnp.minimum(L - 1 - me.z, 1)
        pl.semaphore_wait(barrier, count)


def remote(src, dst, ssem, rsem, device):
    return pltpu.make_async_remote_copy(
        src_ref=src, dst_ref=dst, send_sem=ssem, recv_sem=rsem, device_id=device, device_id_type=MESH
    )


class Gather:
    def __init__(self, at, own, out, sems):
        self.at, self.own, self.out = at, own, out
        self.line_recv, self.sib_recv, self.up_send, self.down_send, self.sib_send, self.local = sems

    @staticmethod
    def sems(at_L):
        return [DMA((at_L,))] * 5 + [DMA]

    def _up(self, zb, src):
        at = self.at
        return remote(src, self.out.at[zb * 2 + at.c], self.up_send.at[zb], self.line_recv.at[zb], {"head": at.up})

    def _down(self, zb, src):
        at = self.at
        return remote(src, self.out.at[zb * 2 + at.c], self.down_send.at[zb], self.line_recv.at[zb], {"head": at.down})

    def _sib(self, zb, src):
        at = self.at
        return remote(src, self.out.at[zb * 2 + at.c], self.sib_send.at[zb], self.sib_recv.at[zb], {"head": at.sib})

    def _mine(self):
        return pltpu.make_async_copy(self.own, self.out.at[self.at.h], self.local)

    def start(self):
        at = self.at

        @pl.when(at.z < at.L - 1)
        def _():
            self._up(at.z, self.own).start()

        @pl.when(at.z > 0)
        def _():
            self._down(at.z, self.own).start()

        self._sib(at.z, self.own).start()
        self._mine().start()

    def step(self, k):
        at = self.at
        below, above = at.z - k, at.z + k

        @pl.when(below >= 0)
        def _():
            block = self.out.at[below * 2 + at.c]
            self._up(below, block).wait_recv()

            @pl.when(at.z < at.L - 1)
            def _():
                self._up(below, block).start()

            self._sib(below, block).start()

        @pl.when(above <= at.L - 1)
        def _():
            block = self.out.at[above * 2 + at.c]
            self._down(above, block).wait_recv()

            @pl.when(at.z > 0)
            def _():
                self._down(above, block).start()

            self._sib(above, block).start()

    def finish(self):
        at = self.at
        self._mine().wait()
        for zb in range(at.L):
            block = self.out.at[zb * 2 + at.c]
            self._sib(zb, block).wait_send()
            other = self.out.at[zb * 2 + 1 - at.c]
            remote(other, other, self.sib_send.at[zb], self.sib_recv.at[zb], {"head": at.sib}).wait_recv()

            @pl.when((zb <= at.z) & (at.z < at.L - 1))
            def _():
                self._up(zb, block).wait_send()

            @pl.when((zb >= at.z) & (at.z > 0))
            def _():
                self._down(zb, block).wait_send()


class Reduce:
    def __init__(self, at, src, own, sib, recv, sems):
        self.at, self.src, self.own, self.sib, self.recv = at, src, own, sib, recv
        self.load, self.sib_send, self.sib_recv, self.fwd_send, self.recv_sem = sems

    @staticmethod
    def sems(L):
        return [DMA((L,)), DMA((L,)), DMA((L,)), DMA((L,)), DMA((L + 1,))]

    @staticmethod
    def bufs(L, T, D):
        return [pltpu.VMEM((L, T, D), BF16), pltpu.VMEM((L, T, D), BF16), pltpu.VMEM((L + 1, T, D), BF16)]

    def _load(self, zd):
        return pltpu.make_async_copy(self.src.at[zd * 2 + self.at.c], self.own.at[zd], self.load.at[zd])

    def _sib(self, zd):
        at = self.at
        return remote(
            self.src.at[zd * 2 + 1 - at.c], self.sib.at[zd], self.sib_send.at[zd], self.sib_recv.at[zd], {"head": at.sib}
        )

    def _fwd(self, zd, slot, device):
        return remote(self.recv.at[zd], self.recv.at[slot], self.fwd_send.at[zd], self.recv_sem.at[slot], {"head": device})

    def start(self):
        at, L = self.at, self.at.L
        order = []
        for k in range((L + 1) // 2):
            order += [L - 1 - k] + ([k] if k != L - 1 - k else [])
        for zd in order:
            self._sib(zd).start()
            self._load(zd).start()

    def _chunks(self, fn):
        T = self.own.shape[1]
        step = 32 if T % 32 == 0 else T

        @pl.loop(0, T // step)
        def _(i):
            fn(pl.ds(pl.multiple_of(i * step, step), step))

    def _hop(self, zd, first, slot, device, which):
        @pl.when(first)
        def _():
            if which in ("first", "both"):
                self._load(zd).wait()
                self._sib(zd).wait_recv()

                def add(rows):
                    self.recv[zd, rows, :] = (self.own[zd, rows, :].astype(F32) + self.sib[zd, rows, :].astype(F32)).astype(
                        BF16
                    )

                self._chunks(add)
                self._fwd(zd, slot, device).start()

        @pl.when(jnp.logical_not(first))
        def _():
            if which in ("mid", "both"):
                self._load(zd).wait()
                self._sib(zd).wait_recv()
                self._fwd(zd, zd, device).wait_recv()

                def add(rows):
                    self.recv[zd, rows, :] = (
                        self.own[zd, rows, :].astype(F32)
                        + self.sib[zd, rows, :].astype(F32)
                        + self.recv[zd, rows, :].astype(F32)
                    ).astype(BF16)

                self._chunks(add)
                self._fwd(zd, slot, device).start()

    def hops(self, k, which="both"):
        at, L = self.at, self.at.L
        far, near = L - 1 - k, k

        @pl.when(far > at.z)
        def _():
            self._hop(far, at.z == 0, far, at.up, which)

        @pl.when(near < at.z)
        def _():
            self._hop(near, at.z == L - 1, jnp.where(at.z - 1 == near, L, near), at.down, which)

    def final(self, add):
        at, L = self.at, self.at.L
        z = at.z
        self._load(z).wait()
        self._sib(z).wait_recv()

        @pl.when(z > 0)
        def _():
            self._fwd(z, z, at.up).wait_recv()

        @pl.when(z < L - 1)
        def _():
            self._fwd(z, L, at.down).wait_recv()

        def base(rows):
            return self.own[z, rows, :].astype(F32) + self.sib[z, rows, :].astype(F32)

        @pl.when(z == 0)
        def _():
            self._chunks(lambda rows: add(rows, base(rows) + self.recv[L, rows, :].astype(F32)))

        @pl.when(z == L - 1)
        def _():
            self._chunks(lambda rows: add(rows, base(rows) + self.recv[z, rows, :].astype(F32)))

        @pl.when((z > 0) & (z < L - 1))
        def _():
            self._chunks(
                lambda rows: add(
                    rows, base(rows) + self.recv[z, rows, :].astype(F32) + self.recv[L, rows, :].astype(F32)
                )
            )

    def finish(self):
        at = self.at
        for zd in range(at.L):
            self._sib(zd).wait_send()

            @pl.when(zd != at.z)
            def _():
                self._fwd(zd, zd, at.up).wait_send()


class BatchGather:
    def __init__(self, at, own, out, sems):
        self.at, self.own, self.out = at, own, out
        self.send, self.recv, self.local = sems

    @staticmethod
    def sems(n):
        m = 4 if n == 4 else n
        return [DMA((m,)), DMA((m,)), DMA]

    def _half(self, b, i):
        half = self.own.shape[0] // 2
        return self.out(b, pl.ds(i * half, half))

    def _all(self, b):
        return self.out(b, pl.ds(0, self.own.shape[0]))

    def _direct(self, i, device):
        at = self.at
        return remote(self.own, self._all(at.b), self.send.at[i], self.recv.at[i], {"batch": device})

    def start(self):
        at = self.at
        pltpu.make_async_copy(self.own, self._all(at.b), self.local).start()
        if at.square:
            self._direct(0, at.xn).start()
            self._direct(1, at.yn).start()
        else:
            for off in range(1, at.n):
                remote(
                    self.own, self._all(at.b), self.send.at[off], self.recv.at[off], {"batch": (at.b + off) % at.n}
                ).start()

    def forward(self):
        at = self.at
        if at.square:
            block = self._all(at.xn)
            remote(block, block, self.send.at[0], self.recv.at[0], {"batch": at.xn}).wait_recv()
            half = self._half(at.xn, 0)
            remote(half, half, self.send.at[2], self.recv.at[2], {"batch": at.yn}).start()
            block = self._all(at.yn)
            remote(block, block, self.send.at[1], self.recv.at[1], {"batch": at.yn}).wait_recv()
            half = self._half(at.yn, 1)
            remote(half, half, self.send.at[3], self.recv.at[3], {"batch": at.xn}).start()

    def finish(self):
        at = self.at
        pltpu.make_async_copy(self.own, self._all(at.b), self.local).wait()
        if at.square:
            self._direct(0, at.xn).wait_send()
            self._direct(1, at.yn).wait_send()
            half = self._half(at.dg, 0)
            remote(half, half, self.send.at[2], self.recv.at[2], {"batch": at.yn}).wait()
            half = self._half(at.dg, 1)
            remote(half, half, self.send.at[3], self.recv.at[3], {"batch": at.xn}).wait()
        else:
            for off in range(1, at.n):
                block = self._all((at.b + at.n - off) % at.n)
                remote(block, block, self.send.at[off], self.recv.at[off], {"batch": (at.b + off) % at.n}).wait()


class BatchReduce:
    def __init__(self, at, src, bufs, sems, before=None):
        self.at, self.src, self.before = at, src, before
        if at.square:
            self.first, self.mine, self.second = bufs
        else:
            (self.slots,) = bufs
        self.send, self.recv, self.load = sems

    @staticmethod
    def sems(n):
        m = 6 if n == 4 else n
        return [DMA((m,)), DMA((m,)), DMA((4,))]

    @staticmethod
    def bufs(n, R, K):
        if n == 4:
            return [
                pltpu.VMEM((4, R // 2, K), BF16),
                pltpu.VMEM((4, R // 2, K), BF16),
                pltpu.VMEM((2, R // 2, K), BF16),
            ]
        return [pltpu.VMEM((n, R, K), BF16)]

    def _first(self, i):
        at, half = self.at, self.src.shape[1] // 2
        if i < 2:
            src = self.src.at[i * 2 + 1 - at.x, pl.ds(0, half), :]
            device = {"batch": at.xn}
        else:
            src = self.src.at[(1 - at.y) * 2 + i - 2, pl.ds(half, half), :]
            device = {"batch": at.yn}
        return remote(src, self.first.at[i], self.send.at[i], self.recv.at[i], device)

    def _taken(self, i):
        if self.before is None:
            return self._first(i)
        return pltpu.make_async_copy(self.before.at[i], self.first.at[i], self.recv.at[i])

    def _load(self, i):
        at, half = self.at, self.src.shape[1] // 2
        if i < 2:
            src = self.src.at[i * 2 + at.x, pl.ds(0, half), :]
        else:
            src = self.src.at[at.y * 2 + i - 2, pl.ds(half, half), :]
        return pltpu.make_async_copy(src, self.mine.at[i], self.load.at[i])

    def _second(self, j):
        at = self.at
        if j == 0:
            return remote(
                self.mine.at[1 - at.y], self.second.at[0], self.send.at[4], self.recv.at[4], {"batch": at.yn}
            )
        return remote(self.mine.at[3 - at.x], self.second.at[1], self.send.at[5], self.recv.at[5], {"batch": at.xn})

    def _direct(self, off):
        at = self.at
        to = (at.b + off) % at.n
        return remote(self.src.at[to], self.slots.at[off], self.send.at[off], self.recv.at[off], {"batch": to})

    def start(self):
        at = self.at
        if at.square:
            for i in (0, 2, 1, 3):
                self._taken(i).start()
                self._load(i).start()
        else:
            for off in range(1, at.n):
                self._direct(off).start()
            pltpu.make_async_copy(self.src.at[at.b], self.slots.at[0], self.load.at[0]).start()

    def _chunks(self, R, fn):
        step = 16

        @pl.loop(0, R // step)
        def _(i):
            fn(pl.multiple_of(i * step, step), step)

    def second_step(self):
        at = self.at
        if at.square:
            for i in range(4):
                self._load(i).wait()
                if self.before is None:
                    self._first(i).wait_recv()
                else:
                    self._taken(i).wait()
            for j, i in ((0, 1 - at.y), (1, 3 - at.x)):

                def add(r, step, i=i):
                    rows = pl.ds(r, step)
                    self.mine[i, rows, :] = (
                        self.mine[i, rows, :].astype(F32) + self.first[i, rows, :].astype(F32)
                    ).astype(BF16)

                self._chunks(self.mine.shape[1], add)
                self._second(j).start()

    def final(self, put):
        at = self.at
        if at.square:
            half = self.src.shape[1] // 2
            for j, i in ((0, at.y), (1, 2 + at.x)):
                self._second(j).wait_recv()

                def add(r, step, i=i, j=j):
                    rows = pl.ds(r, step)
                    put(
                        pl.ds(r + j * half, step),
                        self.mine[i, rows, :].astype(F32)
                        + self.first[i, rows, :].astype(F32)
                        + self.second[j, rows, :].astype(F32),
                    )

                self._chunks(half, add)
        else:
            pltpu.make_async_copy(self.src.at[at.b], self.slots.at[0], self.load.at[0]).wait()
            for off in range(1, at.n):
                self._direct(off).wait_recv()

            def add(r, step):
                rows = pl.ds(r, step)
                total = self.slots[0, rows, :].astype(F32)
                for off in range(1, at.n):
                    total = total + self.slots[off, rows, :].astype(F32)
                put(rows, total)

            self._chunks(self.src.shape[1], add)

    def finish(self):
        at = self.at
        if at.square:
            for i in range(4 if self.before is None else 0):
                self._first(i).wait_send()
            self._second(0).wait_send()
            self._second(1).wait_send()
        else:
            for off in range(1, at.n):
                self._direct(off).wait_send()


class Names:
    def __init__(self):
        self.shapes = []

    def add(self, shapes):
        start = len(self.shapes)
        self.shapes += list(shapes)
        return slice(start, len(self.shapes))


def chunk_loop(rows, step, fn):
    step = min(step, rows)

    @pl.loop(0, rows // step)
    def _(i):
        fn(pl.ds(pl.multiple_of(i * step, step), step))


def inv_root_of(values):
    return lax.rsqrt(jnp.mean(values * values, axis=-1, keepdims=True) + epsilon)


def far_first(L, z):
    return sorted(range(L), key=lambda zd: (-abs(zd - z), -zd))


class Plan:
    def __init__(self, L, rank, reduces, early, follow, begin, tasks):
        self.L = L
        order = [far_first(L, z) for z in range(L)]
        never = 10**6
        jobs = list(rank)
        ready = {j: [[never] * L for _ in range(L)] for j in reduces}
        own = {j: begin.get(j, never) for j in jobs if j not in reduces}
        arrive = {j: {} for j in jobs}
        sent = {j: set() for j in jobs}
        for j, when in early.items():
            for z in range(L):
                for i in range(L):
                    ready[j][z][order[z][i]] = when[i]
        self.final, self.complete, self.tasks, self.sends = {}, {}, {}, []
        todo = list(tasks)
        total = L * (L - 1) * 2
        last = {j: -1 for j in jobs}
        s = free = 0

        def close():
            for j in jobs:
                if len(sent[j]) == total:
                    if j in reduces and j not in self.final:
                        self.final[j] = max(last[j] + 1, max(ready[j][z][z] for z in range(L)) - 1, s - 1)
                        if j in follow:
                            own[follow[j]] = self.final[j] + 1
                    if j in own and j not in self.complete:
                        self.complete[j] = last[j] + 2

        while any(len(sent[j]) < total for j in jobs) or todo:
            close()
            now = {}
            for z in range(L):
                for way in (1, -1):
                    if not 0 <= z + way < L:
                        continue
                    for j in jobs:
                        best = []
                        for block in range(L):
                            for half in (0, 1):
                                if (z, way, block, half) in sent[j]:
                                    continue
                                came = arrive[j].get((z, way, block, half), never)
                                if j in reduces:
                                    first = not 0 <= z - way < L
                                    if (block - z) * way > 0 and ready[j][z][block] <= s and (first or came + 2 <= s):
                                        best.append((-abs(block - z), half, block))
                                elif (z - block) * way >= 0 and (own[j] <= s if block == z else came + 2 <= s):
                                    best.append((abs(block - z), half, block))
                        if best:
                            _, half, block = min(best)
                            now[(z, way)] = (j, block, half)
                            break
            for (z, way), (j, block, half) in now.items():
                sent[j].add((z, way, block, half))
                arrive[j][(z + way, way, block, half)] = s
                last[j] = s
            self.sends.append(now)
            if todo and s >= free:
                name, needs, makes, i, length = todo[0]
                if all(self.complete.get(j, never) <= s for j in needs):
                    self.tasks[s] = todo.pop(0)
                    free = s + length
                    for j in makes:
                        for z in range(L):
                            ready[j][z][order[z][i]] = s + 2
            s += 1
        close()
        self.jobs, self.reduces, self.order = jobs, reduces, order
        self.ready, self.arrive, self.own = ready, arrive, own
        self.slots = 1 + max(list(self.final.values()) + list(self.complete.values()) + [s + 1 for s in self.tasks])

    def block(self, z, i):
        return pick(z, [self.order[q][i] for q in range(self.L)])


def run_plan(plan, at, jobs, task, after, finish):
    z, L = at.z, at.L
    for s in range(plan.slots):
        now = plan.sends[s] if s < len(plan.sends) else {}
        for q in range(L):
            mine = [(way, now[(q, way)]) for way in (1, -1) if (q, way) in now]
            if mine:

                @pl.when(z == q)
                def _():
                    for way, (j, block, half) in mine:
                        jobs[j].copy(q, way, block, half).start()

        if s in plan.tasks:
            task(plan.tasks[s][0])
        after(s)
        past = plan.sends[s - 1] if 0 <= s - 1 < len(plan.sends) else {}
        for q in range(L):
            came = [(way, past[(q - way, way)]) for way in (1, -1) if (q - way, way) in past]
            adds = []
            for j in plan.reduces:
                for (zq, way, block, half), when in plan.arrive[j].items():
                    if zq == q and block != q and max(when + 1, plan.ready[j][q][block] - 1) == s:
                        adds.append((j, block, half))
            if came or adds:

                @pl.when(z == q)
                def _():
                    for way, (j, block, half) in came:
                        jobs[j].landed(q, way, block, half).wait_recv()
                        if j not in plan.reduces:
                            jobs[j].share(block, half).start()
                    for j, block, half in adds:
                        jobs[j].add(block, half)

        for j, when in plan.final.items():
            if when == s:
                finish(j)


def pick(z, values):
    if len(set(values)) == 1:
        return values[0]
    out = jnp.int32(values[0])
    for i, v in enumerate(values[1:], 1):
        out = jnp.where(z == i, v, out)
    return out


class SlotReduce:
    def __init__(self, at, sib, recv, sems):
        self.at, self.sib, self.recv = at, sib, recv
        self.sib_send, self.sib_recv, self.fwd_send, self.recv_sem = sems
        self.half = sib.shape[1] // 2

    @staticmethod
    def sems(L):
        return [DMA((L,)), DMA((L,)), DMA((L, 2)), DMA((L + 1, 2))]

    @staticmethod
    def bufs(L, T, D):
        return [pltpu.VMEM((L, T, D), BF16), pltpu.VMEM((L + 1, T, D), BF16)]

    def part(self, half):
        return pl.ds(half * self.half, self.half)

    def slot(self, z, way, zd):
        return self.at.L if way < 0 and z == zd else zd

    def copy(self, z, way, zd, half):
        at, part = self.at, self.part(half)
        first = not 0 <= z - way < at.L
        src = (self.sib if first else self.recv).at[zd, part, :]
        slot = self.slot(z + way, way, zd)
        device = {"head": at.up if way > 0 else at.down}
        return remote(src, self.recv.at[slot, part, :], self.fwd_send.at[zd, half], self.recv_sem.at[slot, half], device)

    def landed(self, z, way, zd, half):
        at, part = self.at, self.part(half)
        slot = self.slot(z, way, zd)
        block = self.recv.at[slot, part, :]
        device = {"head": at.down if way > 0 else at.up}
        return remote(block, block, self.fwd_send.at[zd, half], self.recv_sem.at[slot, half], device)

    def exchange(self, zd, src):
        return remote(src, self.sib.at[zd], self.sib_send.at[zd], self.sib_recv.at[zd], {"head": self.at.sib})

    def combine(self, zd, mine):
        def add(rows):
            self.sib[zd, rows, :] = (self.sib[zd, rows, :].astype(F32) + mine[rows, :].astype(F32)).astype(BF16)

        chunk_loop(self.sib.shape[1], 32, add)

    def add(self, zd, half):
        def one(rows):
            self.recv[zd, rows, :] = (self.recv[zd, rows, :].astype(F32) + self.sib[zd, rows, :].astype(F32)).astype(BF16)

        step = min(32, self.half)

        @pl.loop(0, self.half // step)
        def _(i):
            one(pl.ds(pl.multiple_of(half * self.half + i * step, step), step))

    def final(self, put):
        at, z = self.at, self.at.z

        def run(extra):
            def part(rows):
                value = self.sib[z, rows, :].astype(F32)
                for slot in extra:
                    value = value + self.recv[slot, rows, :].astype(F32)
                put(rows, value)

            chunk_loop(self.sib.shape[1], 32, part)

        @pl.when(z == 0)
        def _():
            run((at.L,))

        @pl.when(z == at.L - 1)
        def _():
            run((z,))

        @pl.when((z > 0) & (z < at.L - 1))
        def _():
            run((z, at.L))

    def sent(self):
        at = self.at
        for zd in range(at.L):

            @pl.when(zd != at.z)
            def _():
                for half in (0, 1):
                    block = self.recv.at[zd, self.part(half), :]
                    remote(block, block, self.fwd_send.at[zd, half], self.recv_sem.at[zd, half], {"head": at.up}).wait_send()


class SlotGather:
    def __init__(self, at, own, out, sems):
        self.at, self.own, self.out = at, own, out
        self.line_recv, self.up_send, self.down_send, self.sib_send, self.sib_recv, self.local = sems
        self.half = own.shape[0] // 2

    @staticmethod
    def sems(L):
        return [DMA((L, 2))] * 5 + [DMA]

    def block(self, index, half):
        return self.out.at[index, pl.ds(half * self.half, self.half), :]

    def mine(self, half):
        return self.own.at[pl.ds(half * self.half, self.half), :]

    def copy(self, z, way, zb, half):
        at = self.at
        dst = self.block(zb * 2 + at.c, half)
        src = self.mine(half) if zb == z else dst
        send = (self.up_send if way > 0 else self.down_send).at[zb, half]
        return remote(src, dst, send, self.line_recv.at[zb, half], {"head": at.up if way > 0 else at.down})

    def landed(self, z, way, zb, half):
        at = self.at
        dst = self.block(zb * 2 + at.c, half)
        return remote(dst, dst, self.up_send.at[zb, half], self.line_recv.at[zb, half], {"head": at.down if way > 0 else at.up})

    def share(self, zb, half, src=None):
        at = self.at
        dst = self.block(zb * 2 + at.c, half)
        return remote(dst if src is None else src, dst, self.sib_send.at[zb, half], self.sib_recv.at[zb, half], {"head": at.sib})

    def keep(self):
        return pltpu.make_async_copy(self.own, self.out.at[self.at.h], self.local)

    def begin(self):
        for half in (0, 1):
            self.share(self.at.z, half, self.mine(half)).start()
        self.keep().start()

    def finish(self):
        at = self.at
        self.keep().wait()
        for zb in range(at.L):
            for half in (0, 1):
                self.share(zb, half).wait_send()
                other = self.block(zb * 2 + 1 - at.c, half)
                remote(other, other, self.sib_send.at[zb, half], self.sib_recv.at[zb, half], {"head": at.sib}).wait_recv()

            @pl.when((zb <= at.z) & (at.z < at.L - 1))
            def _():
                for half in (0, 1):
                    self.copy(-1, 1, zb, half).wait_send()

            @pl.when((zb >= at.z) & (at.z > 0))
            def _():
                for half in (0, 1):
                    self.copy(-1, -1, zb, half).wait_send()


def norm_back_part(values, gain, grad):
    inv_root = inv_root_of(values)
    unit = values * inv_root
    weighted = grad * gain
    back = inv_root * (weighted - unit * jnp.mean(weighted * unit, axis=-1, keepdims=True))
    return back, jnp.sum(grad * unit, axis=0, keepdims=True)


def attention_in(n, H, tokens, cotangent, gains, weights, positions, frequencies):
    rows, T, D = tokens.shape
    R, W = weights[0].shape
    ff = weights[4].shape[1]
    L = H // 2
    S = H * T
    heads = W // HEAD_DIM
    mix = ("mix", 0)
    rank = [("x", r) for r in range(rows)] + [("ct", 0), mix]
    tasks = []
    for r in range(rows):
        tasks += [((kind, r, 0), (("x", r),), (), 0, 1) for kind in ("qkv", "low", "high")]
        if r == 0:
            tasks += [(("send", 0, i), (), (mix,), i, 1) for i in range(L)]
        else:
            tasks.append((("terms", r, 0), (), (), 0, 1))
    plan = Plan(L, rank, [mix], {}, {}, {j: 0 if j[0] == "ct" else 2 for j in rank if j != mix}, tasks)
    names = Names()
    z_at = [names.add(SlotGather.sems(L)) for _ in range(rows + 1)]
    w_at = [names.add(BatchGather.sems(n)) for _ in range(6)]
    g_at = names.add([DMA((n,)), DMA((n,)), DMA])
    m_at = names.add(SlotReduce.bufs(L, T, D))
    ms_at = names.add(SlotReduce.sems(L))
    rest = names.add(
        [
            pltpu.VMEM((rows, T, D), BF16),
            pltpu.VMEM((2, 2, T, D), BF16),
            pltpu.VMEM((2, 2, T, D), BF16),
            pltpu.VMEM((D, 3 * W), BF16),
            pltpu.VMEM((D, W), BF16),
            DMA((2,)),
            DMA((2,)),
            DMA((2,)),
        ]
    )
    wide = min(512, D)

    def kernel(
        tok,
        ct,
        gain,
        pos,
        freq,
        wq,
        wk,
        wv,
        wo,
        wg,
        wu,
        attn_in,
        ct_first,
        w_qkv,
        w_o,
        w_gu,
        terms,
        gains_full,
        qkv,
        lse,
        attended,
        mixed,
        mid,
        cos,
        sin,
        st,
        *scratch,
    ):
        at = Place(n, H)
        normed, xb, stage, wqkv, wout, x_sem, o_sem, w_sem = scratch[rest]
        gsend, grecv, glocal = scratch[g_at]
        at.greet(all_batch=True)

        def gain_dst(b):
            return gains_full.at[:, pl.ds(pl.multiple_of(b * R, R), R)]

        def gain_send(off):
            return remote(gain, gain_dst(at.b), gsend.at[off], grecv.at[off], {"batch": (at.b + off) % n})

        own_gain = pltpu.make_async_copy(gain, gain_dst(at.b), glocal)
        own_gain.start()
        for off in range(1, n):
            gain_send(off).start()

        gathers = {("x", r): SlotGather(at, normed.at[r], attn_in.at[r], scratch[z_at[r]]) for r in range(rows)}
        gathers[("ct", 0)] = SlotGather(at, ct.at[0], ct_first, scratch[z_at[rows]])
        total = SlotReduce(at, *scratch[m_at], scratch[ms_at])

        def norm(r):
            def one(part):
                values = tok[r, part, :].astype(F32)
                normed[r, part, :] = (values * inv_root_of(values) * gains_full[0:1, :]).astype(BF16)

            chunk_loop(T, 32, one)
            gathers[("x", r)].begin()

        outs = []
        for src, dst, col, width in (
            (wq, w_qkv, 0, W),
            (wk, w_qkv, W, W),
            (wv, w_qkv, 2 * W, W),
            (wo, w_o, 0, W),
            (wg, w_gu, 0, ff),
            (wu, w_gu, ff, ff),
        ):
            outs.append((src, lambda b, part, dst=dst, col=col, width=width: dst.at[b, part, pl.ds(col, width)]))
        shards = [BatchGather(at, src, out, scratch[w_at[i]]) for i, (src, out) in enumerate(outs)]
        gathers[("ct", 0)].begin()
        for job in shards[:4]:
            job.start()

        def norms():
            own_gain.wait()
            for off in range(1, n):
                got = gain_dst((at.b + n - off) % n)
                remote(got, got, gsend.at[off], grecv.at[off], {"batch": (at.b + off) % n}).wait()
            for r in range(rows):
                norm(r)

        def tables(r):
            step = 128
            for i in range(S // step):
                places = pos[r : r + 1, i * step : (i + 1) * step]
                index = lax.broadcasted_iota(jnp.int32, places.shape, 1) + i * step
                st[r, 0:1, i * step : (i + 1) * step] = index - places

            @pl.loop(0, S // step)
            def _(i):
                part = pl.ds(pl.multiple_of(i * step, step), step)
                down = jnp.broadcast_to(pos[r : r + 1, part].astype(F32), (step, step)).T
                angles = down * freq[...]
                lane = lax.broadcasted_iota(jnp.int32, angles.shape, 1)
                cos[r, part, :] = jnp.cos(angles)
                sine = jnp.sin(angles)
                sin[r, part, :] = jnp.where(lane % HEAD_DIM < HEAD_DIM // 2, -sine, sine)

        def weight_loads():
            return [
                pltpu.make_async_copy(w_qkv.at[b], wqkv.at[pl.ds(b * R, R), :], w_sem.at[0]) for b in range(n)
            ] + [pltpu.make_async_copy(w_o.at[b], wout.at[pl.ds(b * R, R), :], w_sem.at[1]) for b in range(n)]

        def x_load(r, b):
            return pltpu.make_async_copy(attn_in.at[r, pl.ds(2 * b, 2)], xb.at[b % 2], x_sem.at[b % 2])

        def make_qkv(r):
            gathers[("x", r)].finish()
            x_load(r, 0).start()
            x_load(r, 1).start()
            if r == 0:
                pltpu.make_async_copy(wqkv, wqkv, w_sem.at[0]).wait()
                pltpu.make_async_copy(wout, wout, w_sem.at[1]).wait()
            for b in range(L):
                x_load(r, b).wait()
                part = pl.ds(b * 2 * T, 2 * T)
                lin = jnp.dot(xb[b % 2].reshape(2 * T, D), wqkv[...], preferred_element_type=F32)
                if b + 2 < L:
                    x_load(r, b + 2).start()
                c, s = cos[r, part, :], sin[r, part, :]
                qkv[r, part, 0:W] = rotate(lin[:, :W], c, s).astype(BF16)
                qkv[r, part, W : 2 * W] = rotate(lin[:, W : 2 * W], c, s).astype(BF16)
                qkv[r, part, 2 * W : 3 * W] = lin[:, 2 * W :].astype(BF16)

        def head(r, h):
            attend(qkv.at[r], st.at[r], lse.at[r], attended.at[r], h, W)

        def store(r, b):
            return pltpu.make_async_copy(stage.at[b % 2], terms.at[r - 1, pl.ds(2 * b, 2)], o_sem.at[b % 2])

        def make_terms(r):
            for b in range(L):
                if b >= 2:
                    store(r, b - 2).wait()
                for j in range(D // wide):
                    cols = pl.ds(j * wide, wide)
                    value = cols_dot(attended[r, pl.ds(b * 2 * T, 2 * T), :], wout[cols, :]).astype(BF16)
                    stage[b % 2, 0, :, cols] = value[:T]
                    stage[b % 2, 1, :, cols] = value[T:]
                store(r, b).start()
            for b in (L - 2, L - 1):
                store(r, b).wait()

        def make_send(i):
            zd = plan.block(at.z, i)
            part = pl.ds(pl.multiple_of(zd * 2 * T, 2 * T), 2 * T)
            for j in range(D // wide):
                cols = pl.ds(j * wide, wide)
                value = cols_dot(attended[0, part, :], wout[cols, :]).astype(BF16)
                stage[i % 2, 0, :, cols] = value[:T]
                stage[i % 2, 1, :, cols] = value[T:]
            total.exchange(zd, stage.at[i % 2, 1 - at.c]).start()

        def combine(i):
            zd = plan.block(at.z, i)
            total.exchange(zd, stage.at[i % 2, 1 - at.c]).wait()
            total.combine(zd, stage.at[i % 2, at.c])

        def finish(j):
            def put(part, value):
                value = value + tok[0, part, :].astype(F32)
                mixed[part, :] = value
                mid[part, :] = (value * inv_root_of(value) * gains_full[1:2, :]).astype(BF16)

            total.final(put)
            total.sent()

        def task(name):
            kind, r, i = name
            if kind == "qkv":
                make_qkv(r)
            elif kind == "low":
                pl.loop(0, heads // 2)(lambda h: head(r, h))
            elif kind == "high":
                pl.loop(heads // 2, heads)(lambda h: head(r, h))
            elif kind == "send":
                make_send(i)
            else:
                make_terms(r)

        def after(s):
            name = plan.tasks[s - 1][0] if s - 1 in plan.tasks else None
            if name and name[0] == "send":
                combine(name[2])
            if s == 1:
                norms()
            if s - 4 in range(rows):
                tables(s - 4)
            if s == 3:
                for job in shards[:4]:
                    job.forward()
                for job in shards[4:]:
                    job.start()
            if s == 6:
                for job in shards[:4]:
                    job.finish()
                for job in weight_loads():
                    job.start()
            if s == 11:
                shards[4].forward()
            if s == 15:
                shards[5].forward()

        run_plan(plan, at, {**gathers, mix: total}, task, after, finish)
        gathers[("ct", 0)].finish()
        for job in shards[4:]:
            job.finish()

    return pl.pallas_call(
        kernel,
        out_shape=(
            jax.ShapeDtypeStruct((rows, H, T, D), BF16),
            jax.ShapeDtypeStruct((H, T, D), BF16),
            jax.ShapeDtypeStruct((n, R, 3 * W), BF16),
            jax.ShapeDtypeStruct((n, R, W), BF16),
            jax.ShapeDtypeStruct((n, R, 2 * ff), BF16),
            jax.ShapeDtypeStruct((rows - 1, H, T, D), BF16),
            jax.ShapeDtypeStruct((8, D), F32),
            jax.ShapeDtypeStruct((rows, S, 3 * W), BF16),
            jax.ShapeDtypeStruct((rows, 8, S), F32),
            jax.ShapeDtypeStruct((rows, S, W), BF16),
            jax.ShapeDtypeStruct((T, D), F32),
            jax.ShapeDtypeStruct((T, D), BF16),
            jax.ShapeDtypeStruct((rows, S, 128), F32),
            jax.ShapeDtypeStruct((rows, S, 128), F32),
            jax.ShapeDtypeStruct((rows, 1, S), jnp.int32),
        ),
        in_specs=[VMEM, VMEM] + [VMEM] * 3 + [ANY] * 6,
        out_specs=(ANY,) * 6 + (VMEM,) * 9,
        scratch_shapes=names.shapes,
        compiler_params=pltpu.CompilerParams(collective_id=1, has_side_effects=True, vmem_limit_bytes=VMEM_LIMIT),
        name="attention_in",
    )(tokens, cotangent, gains, positions, frequencies, *weights)


def feed_forward(n, H, terms, ct_first, mixed_first, mid_first, tokens, cotangent, gains, w_gu, w_d):
    rows, T, D = tokens.shape
    L = H // 2
    ff = w_d.shape[1]
    S = H * T
    R = w_d.shape[0]
    U = R // 2
    square = n == 4
    rank = []
    for kinds in (("mix", "in"), ("sum", "att"), ("out",)):
        rank += [(kind, r) for r in range(rows) for kind in kinds if (kind, r) != ("mix", 0)]
        if kinds[0] == "mix":
            rank[2:2] = [("ct", r) for r in range(1, rows)]
    tasks = []
    for r in range(rows):
        for i in range(L):
            needs = (("in", r),) + ((("ct", r),) if r else ())
            made = (("sum", r), ("out", r))
            if r and i < L // 2:
                tasks.append((("both", r, i), needs, made, i, 1))
            else:
                tasks.append((("first", r, i), needs, (), i, 1))
                tasks.append((("second", r, i), (), made, i, 1))
    tasks += [(("grad", k, 0), (), (), 0, 1) for k in range(2 * n)]
    plan = Plan(
        L,
        rank,
        [j for j in rank if j[0] in ("mix", "sum", "out")],
        {("mix", r): [(r - 1) * L + i for i in range(L)] for r in range(1, rows)},
        {(a, r): (b, r) for a, b in (("mix", "in"), ("sum", "att")) for r in range(rows)},
        {("in", 0): 0, **{("ct", r): 0 for r in range(1, rows)}},
        tasks,
    )
    names = Names()
    n_bufs = [names.add(SlotReduce.bufs(L, T, D)) for _ in range(2 * rows)]
    n_sems = [names.add(SlotReduce.sems(L)) for _ in range(2 * rows)]
    n_gsem = [names.add(SlotGather.sems(L)) for _ in range(2 * rows)]
    n_wsem = names.add(BatchGather.sems(n))
    rest = names.add(
        [
            pltpu.VMEM((rows, T, D), BF16),
            pltpu.VMEM((rows, T, D), BF16),
            pltpu.VMEM((rows, T, D), F32),
            pltpu.VMEM((2, 2, T, D), BF16),
            pltpu.VMEM((2, 2, T, D), BF16),
            pltpu.VMEM((max(D, rows * S), 2 * ff), BF16),
            pltpu.VMEM((max(D, rows * S), ff), BF16),
            pltpu.VMEM((2, 2, T, D), BF16),
            pltpu.VMEM((2, 2, T, D), BF16),
            pltpu.VMEM((2, max(2 * T, U), ff), BF16),
            pltpu.VMEM((2, max(2 * T, U), 2 * ff), BF16),
            pltpu.VMEM((2, rows, H, T, U), BF16),
            pltpu.VMEM((2, rows, H, T, U), BF16),
            DMA((6,)),
            DMA((2, 4)),
            DMA((2, 4)),
            DMA((2,)),
            DMA((2,)),
            DMA((rows, L)),
            DMA((2,)),
            DMA((2,)),
            DMA((2,)),
            DMA((2,)),
        ]
    )
    tile = min(512, ff)
    wide = min(512, D)

    def kernel(
        src,
        ct_row,
        mixed_row,
        mid_row,
        tok,
        ct,
        gain,
        wgu_hbm,
        wd_own,
        ctf,
        mlp_in,
        g_att,
        hid_hbm,
        ggu_hbm,
        grad_gu,
        grad_d,
        first_gu,
        first_d,
        g_mixed,
        layer_out,
        gain_sum,
        *scratch,
    ):
        at = Place(n, H)
        z = at.z
        (
            normed,
            att,
            mixed,
            stage_g,
            stage_o,
            wgu,
            wd,
            xb,
            cb,
            hb,
            gb,
            xt,
            ct_t,
            t_sem,
            gsend,
            grecv,
            w_sem,
            row_sem,
            own_sem,
            x_sem,
            c_sem,
            h_sem,
            g_sem,
        ) = scratch[rest]
        loads = [pltpu.make_async_copy(wgu_hbm, wgu.at[pl.ds(0, D), :], w_sem.at[0])]
        down = BatchGather(
            at,
            wd_own,
            lambda b, part: wd.at[pl.ds(pl.multiple_of(b * R + part.start, U), part.size), :],
            scratch[n_wsem],
        )
        row_loads = [
            pltpu.make_async_copy(mixed_row, mixed.at[0], row_sem.at[0]),
            pltpu.make_async_copy(mid_row, normed.at[0], row_sem.at[1]),
        ]
        for job in row_loads:
            job.start()
        red, gat = {}, {}
        for r in range(rows):
            for kind in ("mix", "sum"):
                red[(kind, r)] = SlotReduce(at, *scratch[n_bufs[r]], scratch[n_sems[r]])
            red[("out", r)] = SlotReduce(at, *scratch[n_bufs[rows + r]], scratch[n_sems[rows + r]])
            gat[("in", r)] = SlotGather(at, normed.at[r], mlp_in.at[r], scratch[n_gsem[r]])
            gat[("att", r)] = SlotGather(at, att.at[r], g_att.at[r], scratch[n_gsem[r]])
            if r:
                gat[("ct", r)] = SlotGather(at, ct.at[r], ctf.at[r - 1], scratch[n_gsem[rows + r]])
        both = {**red, **gat}
        at.greet()
        down.start()

        def mine_of(r, zd):
            return red[("out", r)].recv.at[zd]

        def own_load(r, zd):
            return pltpu.make_async_copy(src.at[r - 1, zd * 2 + at.c], mine_of(r, zd), own_sem.at[r, zd])

        def exchange(r, zd):
            return red[("mix", r)].exchange(zd, src.at[r - 1, zd * 2 + 1 - at.c])

        for job in row_loads:
            job.wait()
        gat[("in", 0)].begin()
        for r in range(1, rows):
            for i in range(L):
                zd = plan.block(z, i)
                exchange(r, zd).start()
                own_load(r, zd).start()
        for r in range(1, rows):
            gat[("ct", r)].begin()
        for job in loads:
            job.start()
        gain_sum[...] = jnp.zeros_like(gain_sum)

        def combine_mix(r, i):
            zd = plan.block(z, i)
            own_load(r, zd).wait()
            exchange(r, zd).wait()
            red[("mix", r)].combine(zd, mine_of(r, zd))

        def combine_terms(r, i):
            zd = plan.block(z, i)
            for kind, stage in (("sum", stage_g), ("out", stage_o)):
                job = red[(kind, r)]
                job.exchange(zd, stage.at[i % 2, 1 - at.c]).wait()
                job.combine(zd, stage.at[i % 2, at.c])

        def x_load(r, i):
            blk = plan.block(z, i)
            return (
                pltpu.make_async_copy(mlp_in.at[r, pl.ds(2 * blk, 2)], xb.at[i % 2], x_sem.at[i % 2]),
                pltpu.make_async_copy(
                    (ctf.at[r - 1] if r else ct_row).at[pl.ds(2 * blk, 2)], cb.at[i % 2], c_sem.at[i % 2]
                ),
            )

        def act_store(r, i):
            blk = plan.block(z, i)
            at_row = pl.ds(pl.multiple_of(r * S + blk * 2 * T, 2 * T), 2 * T)
            return (
                pltpu.make_async_copy(hb.at[i % 2, pl.ds(0, 2 * T), :], hid_hbm.at[at_row, :], h_sem.at[i % 2]),
                pltpu.make_async_copy(gb.at[i % 2, pl.ds(0, 2 * T), :], ggu_hbm.at[at_row, :], g_sem.at[i % 2]),
            )

        def first_part(r, i):
            if i == 0:
                gat[("in", r)].finish()
                if r:
                    gat[("ct", r)].finish()
                for job in x_load(r, 0):
                    job.start()
                if r == 0:
                    down.finish()
                    for job in loads:
                        job.wait()
            for job in x_load(r, i):
                job.wait()
            if i + 1 < L:
                for job in x_load(r, i + 1):
                    job.start()
            if r * L + i >= 2:
                before = (r, i - 2) if i >= 2 else (r - 1, L + i - 2)
                for job in act_store(*before):
                    job.wait()
            k = i % 2

            @pl.loop(0, ff // tile)
            def _(j):
                cols = pl.ds(pl.multiple_of(j * tile, tile), tile)
                up_cols = pl.ds(pl.multiple_of(ff + j * tile, tile), tile)
                x = xb[k].reshape(2 * T, D)
                gate = jnp.dot(x, wgu[0:D, cols], preferred_element_type=F32)
                up = jnp.dot(x, wgu[0:D, up_cols], preferred_element_type=F32)
                back = jnp.dot(cb[k].reshape(2 * T, D), wd[0:D, cols], preferred_element_type=F32)
                sig = 1.0 / (1.0 + jnp.exp(-gate))
                silu = gate * sig
                hb[k, 0 : 2 * T, cols] = (silu * up).astype(BF16)
                gb[k, 0 : 2 * T, cols] = (back * up * (sig * (1.0 + gate * (1.0 - sig)))).astype(BF16)
                gb[k, 0 : 2 * T, up_cols] = (back * silu).astype(BF16)

            for job in act_store(r, i):
                job.start()

        def second_part(r, i):
            k = i % 2

            @pl.loop(0, D // wide)
            def _(j):
                cols = pl.ds(pl.multiple_of(j * wide, wide), wide)
                back = cols_dot(gb[k, 0 : 2 * T, :], wgu[cols, :]).astype(BF16)
                stage_g[k, 0, :, cols] = back[:T]
                stage_g[k, 1, :, cols] = back[T:]
                out = cols_dot(hb[k, 0 : 2 * T, :], wd[cols, :]).astype(BF16)
                stage_o[k, 0, :, cols] = out[:T]
                stage_o[k, 1, :, cols] = out[T:]

            zd = plan.block(z, i)
            for kind, stage in (("sum", stage_g), ("out", stage_o)):
                red[(kind, r)].exchange(zd, stage.at[k, 1 - at.c]).start()

        def finish_mix(r):
            def put(part, value):
                value = value + tok[r, part, :].astype(F32)
                mixed[r, part, :] = value
                normed[r, part, :] = (value * inv_root_of(value) * gain[1:2, :]).astype(BF16)

            red[("mix", r)].final(put)
            red[("mix", r)].sent()
            gat[("in", r)].begin()

        def finish_sum(r):
            def put(part, value):
                back, gain_part = norm_back_part(mixed[r, part, :], gain[1:2, :], value)
                total = ct[r, part, :].astype(F32) + back
                g_mixed[r, part, :] = total
                att[r, part, :] = total.astype(BF16)
                gain_sum[1:2, :] += gain_part

            red[("sum", r)].final(put)
            red[("sum", r)].sent()
            gat[("att", r)].begin()

        def finish_out(r):
            def put(part, value):
                layer_out[r, part, :] = (mixed[r, part, :] + value).astype(BF16)

            red[("out", r)].final(put)
            red[("out", r)].sent()

        units = send_units(at, square, n)
        again = [
            pltpu.make_async_copy(ggu_hbm, wgu.at[pl.ds(0, rows * S), :], w_sem.at[0]),
            pltpu.make_async_copy(hid_hbm, wd.at[pl.ds(0, rows * S), :], w_sem.at[1]),
        ]

        def columns(k):
            cols = pl.ds(pl.multiple_of((units[k][0] * 2 + units[k][1]) * U, U), U)
            return [
                pltpu.make_async_copy(mlp_in.at[:, :, :, cols], xt.at[k % 2], t_sem.at[k % 2]),
                pltpu.make_async_copy(ct_row.at[:, :, cols], ct_t.at[k % 2, 0], t_sem.at[2 + k % 2]),
                pltpu.make_async_copy(
                    ctf.at[:, :, :, cols], ct_t.at[k % 2, pl.ds(1, rows - 1)], t_sem.at[4 + k % 2]
                ),
            ]

        def grad_store(k):
            b, half = units[k][:2]
            part = pl.ds(half * U, U)
            return [
                pltpu.make_async_copy(hb.at[k % 2, pl.ds(0, U), :], grad_d.at[b, part, :], h_sem.at[k % 2]),
                pltpu.make_async_copy(gb.at[k % 2, pl.ds(0, U), :], grad_gu.at[b, part, :], g_sem.at[k % 2]),
            ]

        def grad_sends(k):
            b, half, slot, to = units[k]
            part = pl.ds(half * U, U)
            return [
                remote(src.at[b, part, :], dst.at[slot], gsend.at[a, k], grecv.at[a, slot], {"batch": to})
                for a, (src, dst) in enumerate(((grad_d, first_d), (grad_gu, first_gu)))
            ]

        def prepare_grads():
            for i in (L - 2, L - 1):
                for job in act_store(rows - 1, i):
                    job.wait()
            for job in again + columns(0):
                job.start()

        def grad(k):
            if k == 0:
                for job in again:
                    job.wait()
            for job in columns(k):
                job.wait()
            if k + 1 < 2 * n:
                for job in columns(k + 1):
                    job.start()
            ring = k % 2

            @pl.loop(0, 2 * ff // tile)
            def _(j):
                cols = pl.ds(pl.multiple_of(j * tile, tile), tile)
                x = xt[ring].reshape(rows * S, U)
                gb[ring, 0:U, cols] = rows_dot(x, wgu[0 : rows * S, cols]).astype(BF16)

            @pl.loop(0, ff // tile)
            def _(j):
                cols = pl.ds(pl.multiple_of(j * tile, tile), tile)
                x = ct_t[ring].reshape(rows * S, U)
                hb[ring, 0:U, cols] = rows_dot(x, wd[0 : rows * S, cols]).astype(BF16)

            for job in grad_store(k):
                job.start()

        def task(name):
            kind, r, i = name
            if kind == "first":
                first_part(r, i)
            elif kind in ("second", "both"):
                if kind == "both":
                    first_part(r, i)
                second_part(r, i)
                if (r, i) == (rows - 1, L - 1):
                    prepare_grads()
            else:
                grad(r)

        def after(s):
            if s == 4:
                down.forward()
            if s + 1 < (rows - 1) * L:
                combine_mix(1 + (s + 1) // L, (s + 1) % L)
            name = plan.tasks[s - 1][0] if s - 1 in plan.tasks else None
            if name and name[0] in ("second", "both"):
                combine_terms(*name[1:])
            if name and name[0] == "grad":
                for job in grad_store(name[1]):
                    job.wait()
                if units[name[1]][3] is not None:
                    for job in grad_sends(name[1]):
                        job.start()

        def finish(j):
            {"mix": finish_mix, "sum": finish_sum, "out": finish_out}[j[0]](j[1])

        combine_mix(1, 0)
        run_plan(plan, at, both, task, after, finish)
        if square:
            for k in range(4):
                for job in grad_sends(k):
                    job.wait()
        for r in range(rows):
            gat[("att", r)].finish()

    return pl.pallas_call(
        kernel,
        out_shape=(
            jax.ShapeDtypeStruct((rows - 1, H, T, D), BF16),
            jax.ShapeDtypeStruct((rows, H, T, D), BF16),
            jax.ShapeDtypeStruct((rows, H, T, D), BF16),
            jax.ShapeDtypeStruct((rows * S, ff), BF16),
            jax.ShapeDtypeStruct((rows * S, 2 * ff), BF16),
            jax.ShapeDtypeStruct((n, 2 * U, 2 * ff), BF16),
            jax.ShapeDtypeStruct((n, 2 * U, ff), BF16),
            jax.ShapeDtypeStruct((4, U, 2 * ff), BF16),
            jax.ShapeDtypeStruct((4, U, ff), BF16),
            jax.ShapeDtypeStruct((rows, T, D), F32),
            jax.ShapeDtypeStruct((rows, T, D), BF16),
            jax.ShapeDtypeStruct((8, D), F32),
        ),
        in_specs=[ANY, ANY, ANY, ANY, VMEM, VMEM, VMEM, ANY, ANY],
        out_specs=(ANY,) * 9 + (VMEM, VMEM, VMEM),
        scratch_shapes=names.shapes,
        compiler_params=pltpu.CompilerParams(collective_id=2, has_side_effects=True, vmem_limit_bytes=VMEM_LIMIT),
        name="feed_forward",
    )(terms, ct_first, mixed_first, mid_first, tokens, cotangent, gains, w_gu, w_d)


class LateReduce:
    def __init__(self, at, src, first, bufs, sems):
        self.at, self.src, self.first = at, src, first
        self.mine, self.came, self.second = bufs
        self.load, self.send, self.recv = sems
        self.U = first.shape[1]

    @staticmethod
    def bufs(U, K):
        return [pltpu.VMEM((2, U, K), BF16)] * 3

    @staticmethod
    def sems():
        return [DMA((4,)), DMA((2,)), DMA((2,))]

    def loads(self, j, own):
        at, U = self.at, self.U
        if j == 0:
            y = at.y if own else 1 - at.y
            b, slot = y * 2 + at.x, y
        else:
            x = at.x if own else 1 - at.x
            b, slot = at.y * 2 + x, 2 + x
        return [
            pltpu.make_async_copy(self.src.at[b, pl.ds(j * U, U), :], self.mine.at[j], self.load.at[2 * j]),
            pltpu.make_async_copy(self.first.at[slot], self.came.at[j], self.load.at[2 * j + 1]),
        ]

    def pass_on(self, j):
        to = {"batch": self.at.xn if j else self.at.yn}
        return remote(self.mine.at[j], self.second.at[j], self.send.at[j], self.recv.at[j], to)

    def start(self):
        for j in (0, 1):
            for job in self.loads(j, False):
                job.start()

    def second_step(self):
        for j in (0, 1):
            for job in self.loads(j, False):
                job.wait()

            def add(rows, j=j):
                self.mine[j, rows, :] = (self.mine[j, rows, :].astype(F32) + self.came[j, rows, :].astype(F32)).astype(BF16)

            chunk_loop(self.U, 16, add)
            self.pass_on(j).start()

    def reload(self):
        for j in (0, 1):
            self.pass_on(j).wait()
            for job in self.loads(j, True):
                job.start()

    def final(self, j, step, put):
        for job in self.loads(j, True):
            job.wait()

        @pl.loop(0, self.U // step)
        def _(i):
            rows = pl.ds(pl.multiple_of(i * step, step), step)
            put(
                i,
                self.mine[j, rows, :].astype(F32) + self.came[j, rows, :].astype(F32) + self.second[j, rows, :].astype(F32),
            )


def send_units(at, square, n):
    if not square:
        return [(k // 2, k % 2, None, None) for k in range(2 * n)]
    return [
        ((1 - at.y) * 2 + 1 - at.x, 0, 1 - at.y, at.xn),
        ((1 - at.y) * 2 + 1 - at.x, 1, 3 - at.x, at.yn),
        (at.y * 2 + 1 - at.x, 0, at.y, at.xn),
        ((1 - at.y) * 2 + at.x, 1, 2 + at.x, at.yn),
        ((1 - at.y) * 2 + at.x, 0, None, None),
        (at.y * 2 + 1 - at.x, 1, None, None),
        (at.b, 0, None, None),
        (at.b, 1, None, None),
    ]


def attention_back(
    n,
    H,
    g_att,
    attended,
    qkv,
    lse,
    attn_in,
    w_qkv,
    w_o,
    cosine,
    sine,
    starts,
    tokens,
    g_mixed,
    gains,
    gain_sum,
    g_gu,
    g_d,
    first_gu,
    first_d,
):
    rows, T, D = tokens.shape
    L = H // 2
    S = H * T
    R, ff = g_d.shape[1], g_d.shape[2]
    W = w_o.shape[1]
    heads = W // HEAD_DIM
    U = R // 2
    square = n == 4
    step = min(256, S)
    wide = min(512, D)
    blocks = S // step
    rank = [("in", r) for r in range(rows)]
    tasks = []
    for r in range(rows):
        tasks.append((("prob", r, 0), (), (), 0, 1))
        if r == 0:
            tasks.append((("heads", r, 0), (), (), 0, 1))
        else:
            tasks += [(("head", r, h), (), (), 0, 1) for h in range(heads)]
        tasks += [(("terms", r, i), (), (("in", r),), i, 1) for i in range(L)]
    tasks += [(("grad", k, 0), (), (), 0, 1) for k in range(n)]
    plan = Plan(L, rank, rank, {}, {}, {}, tasks)
    names = Names()
    r_bufs = [names.add(SlotReduce.bufs(L, T, D)) for _ in range(rows)]
    r_sems = [names.add(SlotReduce.sems(L)) for _ in range(rows)]
    if square:
        m_bufs = [names.add(LateReduce.bufs(U, K)) for K in (ff, 2 * ff)]
        m_sems = [names.add(LateReduce.sems()) for _ in range(2)]
        a_bufs = names.add([pltpu.VMEM((4, U, 4 * W), BF16), pltpu.VMEM((2, U, 4 * W), BF16)])
        a_sems = names.add([DMA((6,)), DMA((6,))])
    else:
        m_bufs = [names.add(BatchReduce.bufs(n, R, K)) for K in (ff, 2 * ff)]
        m_sems = [names.add(BatchReduce.sems(n)) for _ in range(2)]
        a_bufs = names.add([pltpu.VMEM((n, 2, U, 4 * W), BF16)])
        a_sems = names.add([DMA((n,)), DMA((n,))])
    s_at = names.add(
        [pltpu.VMEM((8, D), F32), pltpu.VMEM((n, 8, R), F32), pltpu.VMEM((H, 8, R), F32)]
        + [DMA((n,)), DMA((n,)), DMA((H,)), DMA((H,)), DMA]
    )
    rest = names.add(
        [
            pltpu.VMEM((2, step, D), BF16),
            pltpu.VMEM((S, W), BF16),
            pltpu.VMEM((S, W), F32),
            pltpu.VMEM((S, W), F32),
            pltpu.VMEM((S, W), F32),
            pltpu.VMEM((rows * S, 3 * W), BF16),
            pltpu.VMEM((2, 2, T, D), BF16),
            pltpu.VMEM((2, rows * S, U), BF16),
            pltpu.VMEM((2, rows * S, U), BF16),
            pltpu.VMEM((2 * n, U, 4 * W), BF16),
            pltpu.VMEM((4, 32, 2 * ff), F32),
            DMA((2,)),
            DMA((4,)),
            DMA((4, 2)),
            DMA,
        ]
    )

    def kernel(
        ga,
        att,
        qkv,
        ls,
        x_hbm,
        wq,
        wo,
        cos,
        sin,
        st,
        tok,
        gmix,
        gain,
        gain_in,
        ggu,
        gd,
        fgu,
        fd,
        grad_in,
        out_q,
        out_k,
        out_v,
        out_o,
        ggate,
        gup,
        gdown,
        gain_out,
        *scratch,
    ):
        at = Place(n, H)
        z = at.z
        small, over_batch, over_head, bsend, brecv, hsend, hrecv, local = scratch[s_at]
        gab, gat, gq, gk, gv, gqkv, stage, xt, gt, units_buf, out_buf, ga_sem, t_sem, o_sem, mix_sem = scratch[rest]
        sums = {("in", r): SlotReduce(at, *scratch[r_bufs[r]], scratch[r_sems[r]]) for r in range(rows)}
        asend, arecv = scratch[a_sems]
        units = send_units(at, square, n)
        take_mix = pltpu.make_async_copy(gmix, grad_in, mix_sem)
        take_mix.start()

        def ga_load(g):
            return pltpu.make_async_copy(
                ga.at[g // blocks, pl.ds(g % blocks * step, step), :], gab.at[g % 2], ga_sem.at[g % 2]
            )

        ga_load(0).start()
        ga_load(1).start()
        at.greet(all_heads=True)
        if square:
            mlp = [
                LateReduce(at, src, first, scratch[m_bufs[i]], scratch[m_sems[i]])
                for i, (src, first) in enumerate(((gd, fd), (ggu, fgu)))
            ]
        else:
            mlp = [BatchReduce(at, src, scratch[m_bufs[i]], scratch[m_sems[i]]) for i, src in enumerate((gd, ggu))]
        for job in mlp:
            job.start()
        small[...] = gain_in[...]
        for job in mlp:
            job.second_step()

        def prob(r):
            gq[...] = jnp.zeros_like(gq)
            gk[...] = jnp.zeros_like(gk)
            gv[...] = jnp.zeros_like(gv)
            for b in range(blocks):
                g = r * blocks + b
                ga_load(g).wait()
                gat[b * step : (b + 1) * step, :] = jnp.dot(gab[g % 2], wo[...], preferred_element_type=F32).astype(BF16)
                if g + 2 < rows * blocks:
                    ga_load(g + 2).start()

        def head(r, h):
            attend_back(qkv.at[r], st.at[r], ls.at[r], gat, gq, gk, gv, h, W)

        def terms(r, i):
            zd = plan.block(z, i)
            k = i % 2
            part = pl.ds(pl.multiple_of(zd * 2 * T, 2 * T), 2 * T)
            c, s = cos[r, part, :], -sin[r, part, :]
            keep = pl.ds(pl.multiple_of(r * S + zd * 2 * T, 2 * T), 2 * T)
            gqkv[keep, 0:W] = rotate(gq[part, :], c, s).astype(BF16)
            gqkv[keep, W : 2 * W] = rotate(gk[part, :], c, s).astype(BF16)
            gqkv[keep, 2 * W : 3 * W] = gv[part, :].astype(BF16)

            @pl.loop(0, D // wide)
            def _(j):
                cols = pl.ds(pl.multiple_of(j * wide, wide), wide)
                back = cols_dot(gqkv[keep, :], wq[cols, :]).astype(BF16)
                stage[k, 0, :, cols] = back[:T]
                stage[k, 1, :, cols] = back[T:]

            sums[("in", r)].exchange(zd, stage.at[k, 1 - at.c]).start()

        def combine_terms(r, i):
            zd = plan.block(z, i)
            job = sums[("in", r)]
            job.exchange(zd, stage.at[i % 2, 1 - at.c]).wait()
            job.combine(zd, stage.at[i % 2, at.c])

        def columns(k):
            cols = pl.ds(pl.multiple_of((units[k][0] * 2 + units[k][1]) * U, U), U)
            return [pltpu.make_async_copy(x_hbm.at[:, cols], xt.at[k % 2], t_sem.at[k % 2])] + [
                pltpu.make_async_copy(
                    ga.at[r, :, cols], gt.at[k % 2, pl.ds(r * S, S), :], t_sem.at[2 + k % 2]
                )
                for r in range(rows)
            ]

        def columns_wait(k):
            pltpu.make_async_copy(xt.at[k % 2], xt.at[k % 2], t_sem.at[k % 2]).wait()
            pltpu.make_async_copy(gt.at[k % 2], gt.at[k % 2], t_sem.at[2 + k % 2]).wait()

        def grad(k):
            if k == 0:
                for job in columns(0):
                    job.start()
            columns_wait(k)
            if k + 1 < 2 * n:
                for job in columns(k + 1):
                    job.start()
            units_buf[k, :, 0 : 3 * W] = rows_dot(xt[k % 2], gqkv[...]).astype(BF16)
            units_buf[k, :, 3 * W : 4 * W] = rows_dot(gt[k % 2], att[...].reshape(rows * S, W)).astype(BF16)
            if units[k][3] is not None:
                unit_send(k).start()

        if square:
            a_first, a_second = scratch[a_bufs]

            def unit_send(k):
                _, _, slot, to = units[k]
                return remote(units_buf.at[k], a_first.at[slot], asend.at[k], arecv.at[slot], {"batch": to})

            def unit_pass(j):
                to = at.xn if j else at.yn
                return remote(units_buf.at[4 + j], a_second.at[j], asend.at[4 + j], arecv.at[4 + j], {"batch": to})

            def unit_second():
                for j, k, slot in ((0, 0, 1 - at.y), (1, 1, 3 - at.x)):
                    unit_send(k).wait_recv()

                    def add(part, j=j, slot=slot):
                        units_buf[4 + j, part, :] = (
                            units_buf[4 + j, part, :].astype(F32) + a_first[slot, part, :].astype(F32)
                        ).astype(BF16)

                    chunk_loop(U, 16, add)
                    unit_pass(j).start()

            def unit_final(put):
                for j, k, slot in ((0, 2, at.y), (1, 3, 2 + at.x)):
                    unit_send(k).wait_recv()
                    unit_pass(j).wait_recv()

                    @pl.loop(0, U // 16)
                    def _(i, j=j, slot=slot):
                        r = pl.multiple_of(i * 16, 16)
                        part = pl.ds(r, 16)
                        put(
                            pl.ds(r + j * U, 16),
                            units_buf[6 + j, part, :].astype(F32)
                            + a_first[slot, part, :].astype(F32)
                            + a_second[j, part, :].astype(F32),
                        )

                for k in range(4):
                    unit_send(k).wait_send()
                for j in (0, 1):
                    unit_pass(j).wait_send()

        else:
            (a_slots,) = scratch[a_bufs]

            def unit_direct(off):
                to = (at.b + off) % n
                return remote(
                    units_buf.at[pl.ds(2 * to, 2)], a_slots.at[off], asend.at[off], arecv.at[off], {"batch": to}
                )

            def unit_second():
                for off in range(1, n):
                    unit_direct(off).start()

            def unit_final(put):
                for off in range(1, n):
                    unit_direct(off).wait()
                for j in (0, 1):

                    @pl.loop(0, U // 16)
                    def _(i, j=j):
                        r = pl.multiple_of(i * 16, 16)
                        part = pl.ds(r, 16)
                        total = units_buf[2 * at.b + j, part, :].astype(F32)
                        for off in range(1, n):
                            total = total + a_slots[off, j, part, :].astype(F32)
                        put(pl.ds(r + j * U, 16), total)

        def finish(j):
            r = j[1]

            def put(part, value):
                back, gain_part = norm_back_part(tok[r, part, :].astype(F32), gain[0:1, :], value)
                grad_in[r, part, :] += back
                small[0:1, :] += gain_part

            sums[j].final(put)
            sums[j].sent()

        def task(name):
            kind, r, i = name
            if kind == "prob":
                prob(r)
                if r == 0:
                    take_mix.wait()
            elif kind == "heads":
                pl.loop(0, heads)(lambda h: head(r, h))
            elif kind == "head":
                head(r, i)
            elif kind == "terms":
                terms(r, i)
            else:
                grad(2 * r)
                grad(2 * r + 1)

        def out_copies(outs, r, ring, step):
            return [
                pltpu.make_async_copy(
                    out_buf.at[ring, pl.ds(0, step), pl.ds(a * ff, ff)], dst.at[pl.ds(r, step), :], o_sem.at[ring, a]
                )
                for a, dst in enumerate(outs)
            ]

        mlp_outs = ((gdown,), (ggate, gup))

        def mlp_half(a, j):
            step = min(32, U)
            count = U // step
            outs = mlp_outs[a]

            def put(i, value):
                ring = i % 4

                @pl.when(i >= 4)
                def _():
                    for copy in out_copies(outs, j * U, ring, step):
                        copy.wait()

                out_buf[ring, 0:step, 0 : len(outs) * ff] = value
                for copy in out_copies(outs, pl.multiple_of(j * U + i * step, step), ring, step):
                    copy.start()

            mlp[a].final(j, step, put)
            for ring in range(min(4, count)):
                for copy in out_copies(outs, j * U, ring, step):
                    copy.wait()

        def mlp_whole(a):
            outs = mlp_outs[a]

            def put(part, value):
                out_buf[0, 0:16, 0 : len(outs) * ff] = value
                for copy in out_copies(outs, part.start, 0, 16):
                    copy.start()
                for copy in out_copies(outs, part.start, 0, 16):
                    copy.wait()

            mlp[a].final(put)
            mlp[a].finish()

        grads_at = min(s for s, task in plan.tasks.items() if task[0][0] == "grad")

        def after(s):
            name = plan.tasks[s - 1][0] if s - 1 in plan.tasks else None
            if name and name[0] == "terms":
                combine_terms(*name[1:])
            if square:
                if s == grads_at + 1:
                    for job in mlp:
                        job.reload()
                if s == grads_at + 2:
                    mlp_half(0, 0)
                    mlp_half(0, 1)
                if s == grads_at + 4:
                    mlp_half(1, 0)
            if s == grads_at + n - 1:
                unit_second()

        run_plan(plan, at, sums, task, after, finish)

        def slice_of(b):
            return small.at[:, pl.ds(pl.multiple_of(b * R, R), R)]

        def batch_job(off):
            to = (at.b + off) % n
            return remote(slice_of(to), over_batch.at[off], bsend.at[off], brecv.at[off], {"batch": to})

        for off in range(1, n):
            batch_job(off).start()
        mine = pltpu.make_async_copy(slice_of(at.b), over_batch.at[0], local)
        mine.start()
        if square:
            mlp_half(1, 1)
        else:
            mlp_whole(0)
            mlp_whole(1)
        mine.wait()
        total = over_batch[0]
        for off in range(1, n):
            batch_job(off).wait_recv()
            total = total + over_batch[off]
        over_head[at.h] = total

        def head_job(off, block):
            to = (at.h + off) % H
            return remote(over_head.at[block], over_head.at[block], hsend.at[off], hrecv.at[off], {"head": to})

        for off in range(1, H):
            head_job(off, at.h).start()

        def put_units(part, value):
            out_q[part, :] = value[:, :W]
            out_k[part, :] = value[:, W : 2 * W]
            out_v[part, :] = value[:, 2 * W : 3 * W]
            out_o[part, :] = value[:, 3 * W :]

        unit_final(put_units)
        for off in range(1, H):
            head_job(off, (at.h + H - off) % H).wait_recv()
        total = over_head[0]
        for h in range(1, H):
            total = total + over_head[h]
        gain_out[...] = total
        for off in range(1, n):
            batch_job(off).wait_send()
        for off in range(1, H):
            head_job(off, at.h).wait_send()

    weight = jax.ShapeDtypeStruct((R, W), F32)
    wide_weight = jax.ShapeDtypeStruct((R, ff), F32)
    return pl.pallas_call(
        kernel,
        out_shape=(
            jax.ShapeDtypeStruct((rows, T, D), F32),
            weight,
            weight,
            weight,
            weight,
            wide_weight,
            wide_weight,
            wide_weight,
            jax.ShapeDtypeStruct((8, R), F32),
        ),
        in_specs=[ANY, VMEM, VMEM, VMEM, ANY] + [VMEM] * 6 + [ANY, VMEM, VMEM] + [ANY] * 4,
        out_specs=(VMEM,) * 5 + (ANY,) * 3 + (VMEM,),
        scratch_shapes=names.shapes,
        compiler_params=pltpu.CompilerParams(collective_id=4, has_side_effects=True, vmem_limit_bytes=BACK_LIMIT),
        name="attention_back",
    )(
        g_att,
        attended,
        qkv,
        lse,
        attn_in,
        w_qkv,
        w_o,
        cosine,
        sine,
        starts,
        tokens,
        g_mixed,
        gains,
        gain_sum,
        g_gu,
        g_d,
        first_gu,
        first_d,
    )


def rows_dot(left, right):
    return lax.dot_general(left, right, (((0,), (0,)), ((), ())), preferred_element_type=F32)


def cols_dot(left, right):
    return lax.dot_general(left, right, (((1,), (1,)), ((), ())), preferred_element_type=F32)


QUERIES = 256


def rotate(values, cosine, sine):
    half_dim = HEAD_DIM // 2
    parts = []
    for g in range(values.shape[1] // 128):
        part = values[:, g * 128 : (g + 1) * 128]
        lane = lax.broadcasted_iota(jnp.int32, part.shape, 1)
        swapped = jnp.where(
            lane % HEAD_DIM < half_dim, pltpu.roll(part, 128 - half_dim, 1), pltpu.roll(part, half_dim, 1)
        )
        parts.append(part * cosine + swapped * sine)
    return jnp.concatenate(parts, axis=1) if len(parts) > 1 else parts[0]


def only_head(values, h):
    lane = lax.broadcasted_iota(jnp.int32, values.shape, 1)
    return jnp.where(lane // HEAD_DIM == h, values, jnp.zeros_like(values))


def masked_scores(keys, query, starts, first):
    scores = cols_dot(keys, query)
    key_index = lax.broadcasted_iota(jnp.int32, scores.shape, 0)
    query_index = lax.broadcasted_iota(jnp.int32, scores.shape, 1) + first
    return jnp.where((key_index >= starts) & (key_index <= query_index), scores, masked_value)


def attend(qkv, starts, lse, attended, h, W):
    S = qkv.shape[0]
    scale = HEAD_DIM**-0.5
    block = min(QUERIES, S)
    for i in range(S // block):
        rows = pl.ds(i * block, block)
        width = (i + 1) * block
        query = only_head(qkv[rows, 0:W], h) * jnp.asarray(scale, BF16)
        scores = masked_scores(qkv[0:width, W : 2 * W], query, starts[:, rows], i * block)
        top = jnp.max(scores, axis=0, keepdims=True)
        weights = jnp.exp(scores - top)
        total = jnp.sum(weights, axis=0, keepdims=True)
        lse[pl.ds(h, 1), rows] = top + jnp.log(total)
        probs = (weights * (1.0 / total)).astype(BF16)
        out = rows_dot(probs, qkv[0:width, 2 * W : 3 * W]).astype(BF16)
        lane = lax.broadcasted_iota(jnp.int32, out.shape, 1)
        attended[rows, :] = jnp.where(lane // HEAD_DIM == h, out, attended[rows, :])


def attend_back(qkv, starts, lse, grad, g_query, g_key, g_value, h, W):
    S = qkv.shape[0]
    scale = HEAD_DIM**-0.5
    block = min(QUERIES, S)
    for i in range(S // block):
        rows = pl.ds(i * block, block)
        width = (i + 1) * block
        query = only_head(qkv[rows, 0:W], h) * jnp.asarray(scale, BF16)
        keys = qkv[0:width, W : 2 * W]
        scores = masked_scores(keys, query, starts[:, rows], i * block)
        probs = jnp.exp(scores - lse[pl.ds(h, 1), rows])
        back = only_head(grad[rows, :], h)
        g_prob = cols_dot(qkv[0:width, 2 * W : 3 * W], back)
        delta = jnp.sum(probs * g_prob, axis=0, keepdims=True)
        g_score = (probs * (g_prob - delta)).astype(BF16)
        g_value[0:width, :] += jnp.dot(probs.astype(BF16), back, preferred_element_type=F32)
        g_key[0:width, :] += jnp.dot(g_score, query, preferred_element_type=F32)
        g_query[rows, :] += only_head(rows_dot(g_score, keys) * scale, h)


def hand_out(arrays):
    count = len(arrays)

    def kernel(*refs):
        held, sem_in, sem_out = refs[2 * count : 3 * count], refs[-2], refs[-1]
        take = [pltpu.make_async_copy(refs[i], held[i], sem_in.at[i]) for i in range(count)]
        give = [pltpu.make_async_copy(held[i], refs[count + i], sem_out.at[i]) for i in range(count)]
        for job in take:
            job.start()
        for i in range(count):
            take[i].wait()
            give[i].start()
        for job in give:
            job.wait()

    return pl.pallas_call(
        kernel,
        out_shape=tuple(jax.ShapeDtypeStruct(a.shape, a.dtype) for a in arrays),
        in_specs=[ANY] * count,
        out_specs=(ANY,) * count,
        scratch_shapes=[pltpu.VMEM(a.shape, a.dtype) for a in arrays] + [DMA((count,))] * 2,
        compiler_params=pltpu.CompilerParams(vmem_limit_bytes=VMEM_LIMIT),
        name="hand_out",
    )(*arrays)


def per_device(
    n,
    H,
    tokens,
    segment_ids,
    position_ids,
    w_query,
    w_key,
    w_value,
    w_output,
    w_gate,
    w_up,
    w_down,
    attn_gain,
    mlp_gain,
    cotangent,
):
    rows, T, D = tokens.shape
    S = T * H
    R, hw = w_query.shape
    ff = w_gate.shape[1]
    shard_gains = jnp.concatenate(
        [attn_gain.astype(F32)[None], mlp_gain.astype(F32)[None], jnp.zeros((6, R), F32)], axis=0
    )
    half_dim = HEAD_DIM // 2
    frequencies = jnp.asarray(
        np.tile(rope_base ** (-(np.arange(half_dim) * 2.0) / HEAD_DIM), 4).astype(np.float32)[None]
    )
    (
        attn_in,
        ct_first,
        w_qkv,
        w_o,
        w_gu,
        terms,
        gains,
        qkv,
        lse,
        attended,
        mixed_first,
        mid_first,
        cosine,
        sine,
        starts,
    ) = attention_in(
        n,
        H,
        tokens,
        cotangent,
        shard_gains,
        (w_query, w_key, w_value, w_output, w_gate, w_up),
        position_ids,
        frequencies,
    )
    w_qkv = w_qkv.reshape(D, 3 * hw)
    w_o = w_o.reshape(D, hw)
    w_gu = w_gu.reshape(D, 2 * ff)
    _, _, g_att, _, _, grad_gu, grad_d, first_gu, first_d, g_mixed, layer_out, gain_sum = feed_forward(
        n, H, terms, ct_first, mixed_first, mid_first, tokens, cotangent, gains, w_gu, w_down
    )
    grad_input, grad_q, grad_k, grad_v, grad_out, grad_gate, grad_up, grad_down, gain_grads = attention_back(
        n,
        H,
        g_att.reshape(rows, S, D),
        attended,
        qkv,
        lse,
        attn_in.reshape(rows * S, D),
        w_qkv,
        w_o,
        cosine,
        sine,
        starts,
        tokens,
        g_mixed,
        gains,
        gain_sum,
        grad_gu,
        grad_d,
        first_gu,
        first_d,
    )
    results = hand_out(
        (layer_out, grad_input, grad_q, grad_k, grad_v, grad_out, grad_gate, grad_up, grad_down)
    )
    return (*results, gain_grads[0], gain_grads[1])


def solution(mesh):
    row = P("batch", "head", None)
    ids = P("batch", None)
    weight = P("batch", "head")
    gain = P("batch")
    return jax.shard_map(
        functools.partial(per_device, mesh.shape["batch"], mesh.shape["head"]),
        mesh=mesh,
        in_specs=(row, ids, ids) + (weight,) * 7 + (gain, gain, row),
        out_specs=(row, row) + (weight,) * 7 + (gain, gain),
        check_vma=False,
    )
```

```python
import functools

import jax
import jax.numpy as jnp
import numpy as np
from jax import lax
from jax.experimental import pallas as pl
from jax.experimental.pallas import tpu as pltpu
from jax.sharding import PartitionSpec as P

HEAD_DIM = 64
epsilon = 1e-05
rope_base = 130000.0
masked_value = -1000000000.0
MESH = pl.DeviceIdType.MESH
F32 = jnp.float32
BF16 = jnp.bfloat16
DMA = pltpu.SemaphoreType.DMA
ANY = pl.BlockSpec(memory_space=pl.ANY)
VMEM = pl.BlockSpec(memory_space=pltpu.VMEM)
VMEM_LIMIT = 60 * 2**20
BACK_LIMIT = 63 * 2**20


class Place:
    def __init__(self, batch, head):
        self.n, self.H = batch, head
        self.L = head // 2
        self.b = lax.axis_index("batch")
        self.h = lax.axis_index("head")
        self.z = self.h // 2
        self.c = self.h % 2
        self.sib = self.z * 2 + (1 - self.c)
        self.up = self.h + 2
        self.down = self.h - 2
        self.x, self.y = self.b % 2, self.b // 2
        self.xn = self.y * 2 + (1 - self.x)
        self.yn = (1 - self.y) * 2 + self.x
        self.dg = (1 - self.y) * 2 + (1 - self.x)
        self.square = batch == 4

    def greet(self, line=True, batch=True, all_heads=False, all_batch=False):
        barrier = pltpu.get_barrier_semaphore()
        me, L = self, self.L

        def hello(device):
            pl.semaphore_signal(barrier, inc=1, device_id=device, device_id_type=MESH)

        count = 0
        if all_heads:
            for off in range(1, self.H):
                hello({"head": (me.h + off) % self.H})
                count += 1
        elif line:
            hello({"head": me.sib})
            count += 1

            @pl.when(me.z > 0)
            def _():
                hello({"head": me.down})

            @pl.when(me.z < L - 1)
            def _():
                hello({"head": me.up})

        if batch:
            if self.square and not all_heads and not all_batch:
                hello({"batch": me.xn})
                hello({"batch": me.yn})
                count += 2
            else:
                for off in range(1, self.n):
                    hello({"batch": (me.b + off) % self.n})
                    count += 1
        if line and not all_heads:
            count = count + jnp.minimum(me.z, 1) + jnp.minimum(L - 1 - me.z, 1)
        pl.semaphore_wait(barrier, count)


def remote(src, dst, ssem, rsem, device):
    return pltpu.make_async_remote_copy(
        src_ref=src, dst_ref=dst, send_sem=ssem, recv_sem=rsem, device_id=device, device_id_type=MESH
    )


class Gather:
    def __init__(self, at, own, out, sems):
        self.at, self.own, self.out = at, own, out
        self.line_recv, self.sib_recv, self.up_send, self.down_send, self.sib_send, self.local = sems

    @staticmethod
    def sems(at_L):
        return [DMA((at_L,))] * 5 + [DMA]

    def _up(self, zb, src):
        at = self.at
        return remote(src, self.out.at[zb * 2 + at.c], self.up_send.at[zb], self.line_recv.at[zb], {"head": at.up})

    def _down(self, zb, src):
        at = self.at
        return remote(src, self.out.at[zb * 2 + at.c], self.down_send.at[zb], self.line_recv.at[zb], {"head": at.down})

    def _sib(self, zb, src):
        at = self.at
        return remote(src, self.out.at[zb * 2 + at.c], self.sib_send.at[zb], self.sib_recv.at[zb], {"head": at.sib})

    def _mine(self):
        return pltpu.make_async_copy(self.own, self.out.at[self.at.h], self.local)

    def start(self):
        at = self.at

        @pl.when(at.z < at.L - 1)
        def _():
            self._up(at.z, self.own).start()

        @pl.when(at.z > 0)
        def _():
            self._down(at.z, self.own).start()

        self._sib(at.z, self.own).start()
        self._mine().start()

    def step(self, k):
        at = self.at
        below, above = at.z - k, at.z + k

        @pl.when(below >= 0)
        def _():
            block = self.out.at[below * 2 + at.c]
            self._up(below, block).wait_recv()

            @pl.when(at.z < at.L - 1)
            def _():
                self._up(below, block).start()

            self._sib(below, block).start()

        @pl.when(above <= at.L - 1)
        def _():
            block = self.out.at[above * 2 + at.c]
            self._down(above, block).wait_recv()

            @pl.when(at.z > 0)
            def _():
                self._down(above, block).start()

            self._sib(above, block).start()

    def finish(self):
        at = self.at
        self._mine().wait()
        for zb in range(at.L):
            block = self.out.at[zb * 2 + at.c]
            self._sib(zb, block).wait_send()
            other = self.out.at[zb * 2 + 1 - at.c]
            remote(other, other, self.sib_send.at[zb], self.sib_recv.at[zb], {"head": at.sib}).wait_recv()

            @pl.when((zb <= at.z) & (at.z < at.L - 1))
            def _():
                self._up(zb, block).wait_send()

            @pl.when((zb >= at.z) & (at.z > 0))
            def _():
                self._down(zb, block).wait_send()


class Reduce:
    def __init__(self, at, src, own, sib, recv, sems):
        self.at, self.src, self.own, self.sib, self.recv = at, src, own, sib, recv
        self.load, self.sib_send, self.sib_recv, self.fwd_send, self.recv_sem = sems

    @staticmethod
    def sems(L):
        return [DMA((L,)), DMA((L,)), DMA((L,)), DMA((L,)), DMA((L + 1,))]

    @staticmethod
    def bufs(L, T, D):
        return [pltpu.VMEM((L, T, D), BF16), pltpu.VMEM((L, T, D), BF16), pltpu.VMEM((L + 1, T, D), BF16)]

    def _load(self, zd):
        return pltpu.make_async_copy(self.src.at[zd * 2 + self.at.c], self.own.at[zd], self.load.at[zd])

    def _sib(self, zd):
        at = self.at
        return remote(
            self.src.at[zd * 2 + 1 - at.c], self.sib.at[zd], self.sib_send.at[zd], self.sib_recv.at[zd], {"head": at.sib}
        )

    def _fwd(self, zd, slot, device):
        return remote(self.recv.at[zd], self.recv.at[slot], self.fwd_send.at[zd], self.recv_sem.at[slot], {"head": device})

    def start(self):
        at, L = self.at, self.at.L
        order = []
        for k in range((L + 1) // 2):
            order += [L - 1 - k] + ([k] if k != L - 1 - k else [])
        for zd in order:
            self._sib(zd).start()
            self._load(zd).start()

    def _chunks(self, fn):
        T = self.own.shape[1]
        step = 32 if T % 32 == 0 else T

        @pl.loop(0, T // step)
        def _(i):
            fn(pl.ds(pl.multiple_of(i * step, step), step))

    def _hop(self, zd, first, slot, device, which):
        @pl.when(first)
        def _():
            if which in ("first", "both"):
                self._load(zd).wait()
                self._sib(zd).wait_recv()

                def add(rows):
                    self.recv[zd, rows, :] = (self.own[zd, rows, :].astype(F32) + self.sib[zd, rows, :].astype(F32)).astype(
                        BF16
                    )

                self._chunks(add)
                self._fwd(zd, slot, device).start()

        @pl.when(jnp.logical_not(first))
        def _():
            if which in ("mid", "both"):
                self._load(zd).wait()
                self._sib(zd).wait_recv()
                self._fwd(zd, zd, device).wait_recv()

                def add(rows):
                    self.recv[zd, rows, :] = (
                        self.own[zd, rows, :].astype(F32)
                        + self.sib[zd, rows, :].astype(F32)
                        + self.recv[zd, rows, :].astype(F32)
                    ).astype(BF16)

                self._chunks(add)
                self._fwd(zd, slot, device).start()

    def hops(self, k, which="both"):
        at, L = self.at, self.at.L
        far, near = L - 1 - k, k

        @pl.when(far > at.z)
        def _():
            self._hop(far, at.z == 0, far, at.up, which)

        @pl.when(near < at.z)
        def _():
            self._hop(near, at.z == L - 1, jnp.where(at.z - 1 == near, L, near), at.down, which)

    def final(self, add):
        at, L = self.at, self.at.L
        z = at.z
        self._load(z).wait()
        self._sib(z).wait_recv()

        @pl.when(z > 0)
        def _():
            self._fwd(z, z, at.up).wait_recv()

        @pl.when(z < L - 1)
        def _():
            self._fwd(z, L, at.down).wait_recv()

        def base(rows):
            return self.own[z, rows, :].astype(F32) + self.sib[z, rows, :].astype(F32)

        @pl.when(z == 0)
        def _():
            self._chunks(lambda rows: add(rows, base(rows) + self.recv[L, rows, :].astype(F32)))

        @pl.when(z == L - 1)
        def _():
            self._chunks(lambda rows: add(rows, base(rows) + self.recv[z, rows, :].astype(F32)))

        @pl.when((z > 0) & (z < L - 1))
        def _():
            self._chunks(
                lambda rows: add(
                    rows, base(rows) + self.recv[z, rows, :].astype(F32) + self.recv[L, rows, :].astype(F32)
                )
            )

    def finish(self):
        at = self.at
        for zd in range(at.L):
            self._sib(zd).wait_send()

            @pl.when(zd != at.z)
            def _():
                self._fwd(zd, zd, at.up).wait_send()


class BatchGather:
    def __init__(self, at, own, out, sems):
        self.at, self.own, self.out = at, own, out
        self.send, self.recv, self.local = sems

    @staticmethod
    def sems(n):
        m = 4 if n == 4 else n
        return [DMA((m,)), DMA((m,)), DMA]

    def _half(self, b, i):
        half = self.own.shape[0] // 2
        return self.out(b, pl.ds(i * half, half))

    def _all(self, b):
        return self.out(b, pl.ds(0, self.own.shape[0]))

    def _direct(self, i, device):
        at = self.at
        return remote(self.own, self._all(at.b), self.send.at[i], self.recv.at[i], {"batch": device})

    def start(self):
        at = self.at
        pltpu.make_async_copy(self.own, self._all(at.b), self.local).start()
        if at.square:
            self._direct(0, at.xn).start()
            self._direct(1, at.yn).start()
        else:
            for off in range(1, at.n):
                remote(
                    self.own, self._all(at.b), self.send.at[off], self.recv.at[off], {"batch": (at.b + off) % at.n}
                ).start()

    def forward(self):
        at = self.at
        if at.square:
            block = self._all(at.xn)
            remote(block, block, self.send.at[0], self.recv.at[0], {"batch": at.xn}).wait_recv()
            half = self._half(at.xn, 0)
            remote(half, half, self.send.at[2], self.recv.at[2], {"batch": at.yn}).start()
            block = self._all(at.yn)
            remote(block, block, self.send.at[1], self.recv.at[1], {"batch": at.yn}).wait_recv()
            half = self._half(at.yn, 1)
            remote(half, half, self.send.at[3], self.recv.at[3], {"batch": at.xn}).start()

    def finish(self):
        at = self.at
        pltpu.make_async_copy(self.own, self._all(at.b), self.local).wait()
        if at.square:
            self._direct(0, at.xn).wait_send()
            self._direct(1, at.yn).wait_send()
            half = self._half(at.dg, 0)
            remote(half, half, self.send.at[2], self.recv.at[2], {"batch": at.yn}).wait()
            half = self._half(at.dg, 1)
            remote(half, half, self.send.at[3], self.recv.at[3], {"batch": at.xn}).wait()
        else:
            for off in range(1, at.n):
                block = self._all((at.b + at.n - off) % at.n)
                remote(block, block, self.send.at[off], self.recv.at[off], {"batch": (at.b + off) % at.n}).wait()


class BatchReduce:
    def __init__(self, at, src, bufs, sems, before=None):
        self.at, self.src, self.before = at, src, before
        if at.square:
            self.first, self.mine, self.second = bufs
        else:
            (self.slots,) = bufs
        self.send, self.recv, self.load = sems

    @staticmethod
    def sems(n):
        m = 6 if n == 4 else n
        return [DMA((m,)), DMA((m,)), DMA((4,))]

    @staticmethod
    def bufs(n, R, K):
        if n == 4:
            return [
                pltpu.VMEM((4, R // 2, K), BF16),
                pltpu.VMEM((4, R // 2, K), BF16),
                pltpu.VMEM((2, R // 2, K), BF16),
            ]
        return [pltpu.VMEM((n, R, K), BF16)]

    def _first(self, i):
        at, half = self.at, self.src.shape[1] // 2
        if i < 2:
            src = self.src.at[i * 2 + 1 - at.x, pl.ds(0, half), :]
            device = {"batch": at.xn}
        else:
            src = self.src.at[(1 - at.y) * 2 + i - 2, pl.ds(half, half), :]
            device = {"batch": at.yn}
        return remote(src, self.first.at[i], self.send.at[i], self.recv.at[i], device)

    def _taken(self, i):
        if self.before is None:
            return self._first(i)
        return pltpu.make_async_copy(self.before.at[i], self.first.at[i], self.recv.at[i])

    def _load(self, i):
        at, half = self.at, self.src.shape[1] // 2
        if i < 2:
            src = self.src.at[i * 2 + at.x, pl.ds(0, half), :]
        else:
            src = self.src.at[at.y * 2 + i - 2, pl.ds(half, half), :]
        return pltpu.make_async_copy(src, self.mine.at[i], self.load.at[i])

    def _second(self, j):
        at = self.at
        if j == 0:
            return remote(
                self.mine.at[1 - at.y], self.second.at[0], self.send.at[4], self.recv.at[4], {"batch": at.yn}
            )
        return remote(self.mine.at[3 - at.x], self.second.at[1], self.send.at[5], self.recv.at[5], {"batch": at.xn})

    def _direct(self, off):
        at = self.at
        to = (at.b + off) % at.n
        return remote(self.src.at[to], self.slots.at[off], self.send.at[off], self.recv.at[off], {"batch": to})

    def start(self):
        at = self.at
        if at.square:
            for i in (0, 2, 1, 3):
                self._taken(i).start()
                self._load(i).start()
        else:
            for off in range(1, at.n):
                self._direct(off).start()
            pltpu.make_async_copy(self.src.at[at.b], self.slots.at[0], self.load.at[0]).start()

    def _chunks(self, R, fn):
        step = 16

        @pl.loop(0, R // step)
        def _(i):
            fn(pl.multiple_of(i * step, step), step)

    def second_step(self):
        at = self.at
        if at.square:
            for i in range(4):
                self._load(i).wait()
                if self.before is None:
                    self._first(i).wait_recv()
                else:
                    self._taken(i).wait()
            for j, i in ((0, 1 - at.y), (1, 3 - at.x)):

                def add(r, step, i=i):
                    rows = pl.ds(r, step)
                    self.mine[i, rows, :] = (
                        self.mine[i, rows, :].astype(F32) + self.first[i, rows, :].astype(F32)
                    ).astype(BF16)

                self._chunks(self.mine.shape[1], add)
                self._second(j).start()

    def final(self, put):
        at = self.at
        if at.square:
            half = self.src.shape[1] // 2
            for j, i in ((0, at.y), (1, 2 + at.x)):
                self._second(j).wait_recv()

                def add(r, step, i=i, j=j):
                    rows = pl.ds(r, step)
                    put(
                        pl.ds(r + j * half, step),
                        self.mine[i, rows, :].astype(F32)
                        + self.first[i, rows, :].astype(F32)
                        + self.second[j, rows, :].astype(F32),
                    )

                self._chunks(half, add)
        else:
            pltpu.make_async_copy(self.src.at[at.b], self.slots.at[0], self.load.at[0]).wait()
            for off in range(1, at.n):
                self._direct(off).wait_recv()

            def add(r, step):
                rows = pl.ds(r, step)
                total = self.slots[0, rows, :].astype(F32)
                for off in range(1, at.n):
                    total = total + self.slots[off, rows, :].astype(F32)
                put(rows, total)

            self._chunks(self.src.shape[1], add)

    def finish(self):
        at = self.at
        if at.square:
            for i in range(4 if self.before is None else 0):
                self._first(i).wait_send()
            self._second(0).wait_send()
            self._second(1).wait_send()
        else:
            for off in range(1, at.n):
                self._direct(off).wait_send()


class Names:
    def __init__(self):
        self.shapes = []

    def add(self, shapes):
        start = len(self.shapes)
        self.shapes += list(shapes)
        return slice(start, len(self.shapes))


def chunk_loop(rows, step, fn):
    step = min(step, rows)

    @pl.loop(0, rows // step)
    def _(i):
        fn(pl.ds(pl.multiple_of(i * step, step), step))


def inv_root_of(values):
    return lax.rsqrt(jnp.mean(values * values, axis=-1, keepdims=True) + epsilon)


def far_first(L, z):
    return sorted(range(L), key=lambda zd: (-abs(zd - z), -zd))


class Plan:
    def __init__(self, L, rank, reduces, early, follow, begin, tasks):
        self.L = L
        order = [far_first(L, z) for z in range(L)]
        never = 10**6
        jobs = list(rank)
        ready = {j: [[never] * L for _ in range(L)] for j in reduces}
        own = {j: begin.get(j, never) for j in jobs if j not in reduces}
        arrive = {j: {} for j in jobs}
        sent = {j: set() for j in jobs}
        for j, when in early.items():
            for z in range(L):
                for i in range(L):
                    ready[j][z][order[z][i]] = when[i]
        self.final, self.complete, self.tasks, self.sends = {}, {}, {}, []
        todo = list(tasks)
        total = L * (L - 1) * 2
        last = {j: -1 for j in jobs}
        s = free = 0

        def close():
            for j in jobs:
                if len(sent[j]) == total:
                    if j in reduces and j not in self.final:
                        self.final[j] = max(last[j] + 1, max(ready[j][z][z] for z in range(L)) - 1, s - 1)
                        if j in follow:
                            own[follow[j]] = self.final[j] + 1
                    if j in own and j not in self.complete:
                        self.complete[j] = last[j] + 2

        while any(len(sent[j]) < total for j in jobs) or todo:
            close()
            now = {}
            for z in range(L):
                for way in (1, -1):
                    if not 0 <= z + way < L:
                        continue
                    for j in jobs:
                        best = []
                        for block in range(L):
                            for half in (0, 1):
                                if (z, way, block, half) in sent[j]:
                                    continue
                                came = arrive[j].get((z, way, block, half), never)
                                if j in reduces:
                                    first = not 0 <= z - way < L
                                    if (block - z) * way > 0 and ready[j][z][block] <= s and (first or came + 2 <= s):
                                        best.append((-abs(block - z), half, block))
                                elif (z - block) * way >= 0 and (own[j] <= s if block == z else came + 2 <= s):
                                    best.append((abs(block - z), half, block))
                        if best:
                            _, half, block = min(best)
                            now[(z, way)] = (j, block, half)
                            break
            for (z, way), (j, block, half) in now.items():
                sent[j].add((z, way, block, half))
                arrive[j][(z + way, way, block, half)] = s
                last[j] = s
            self.sends.append(now)
            if todo and s >= free:
                name, needs, makes, i, length = todo[0]
                if all(self.complete.get(j, never) <= s for j in needs):
                    self.tasks[s] = todo.pop(0)
                    free = s + length
                    for j in makes:
                        for z in range(L):
                            ready[j][z][order[z][i]] = s + 2
            s += 1
        close()
        self.jobs, self.reduces, self.order = jobs, reduces, order
        self.ready, self.arrive, self.own = ready, arrive, own
        self.slots = 1 + max(list(self.final.values()) + list(self.complete.values()) + [s + 1 for s in self.tasks])

    def block(self, z, i):
        return pick(z, [self.order[q][i] for q in range(self.L)])


def run_plan(plan, at, jobs, task, after, finish):
    z, L = at.z, at.L
    for s in range(plan.slots):
        now = plan.sends[s] if s < len(plan.sends) else {}
        for q in range(L):
            mine = [(way, now[(q, way)]) for way in (1, -1) if (q, way) in now]
            if mine:

                @pl.when(z == q)
                def _():
                    for way, (j, block, half) in mine:
                        jobs[j].copy(q, way, block, half).start()

        if s in plan.tasks:
            task(plan.tasks[s][0])
        after(s)
        past = plan.sends[s - 1] if 0 <= s - 1 < len(plan.sends) else {}
        for q in range(L):
            came = [(way, past[(q - way, way)]) for way in (1, -1) if (q - way, way) in past]
            adds = []
            for j in plan.reduces:
                for (zq, way, block, half), when in plan.arrive[j].items():
                    if zq == q and block != q and max(when + 1, plan.ready[j][q][block] - 1) == s:
                        adds.append((j, block, half))
            if came or adds:

                @pl.when(z == q)
                def _():
                    for way, (j, block, half) in came:
                        jobs[j].landed(q, way, block, half).wait_recv()
                        if j not in plan.reduces:
                            jobs[j].share(block, half).start()
                    for j, block, half in adds:
                        jobs[j].add(block, half)

        for j, when in plan.final.items():
            if when == s:
                finish(j)


def pick(z, values):
    if len(set(values)) == 1:
        return values[0]
    out = jnp.int32(values[0])
    for i, v in enumerate(values[1:], 1):
        out = jnp.where(z == i, v, out)
    return out


class SlotReduce:
    def __init__(self, at, sib, recv, sems):
        self.at, self.sib, self.recv = at, sib, recv
        self.sib_send, self.sib_recv, self.fwd_send, self.recv_sem = sems
        self.half = sib.shape[1] // 2

    @staticmethod
    def sems(L):
        return [DMA((L,)), DMA((L,)), DMA((L, 2)), DMA((L + 1, 2))]

    @staticmethod
    def bufs(L, T, D):
        return [pltpu.VMEM((L, T, D), BF16), pltpu.VMEM((L + 1, T, D), BF16)]

    def part(self, half):
        return pl.ds(half * self.half, self.half)

    def slot(self, z, way, zd):
        return self.at.L if way < 0 and z == zd else zd

    def copy(self, z, way, zd, half):
        at, part = self.at, self.part(half)
        first = not 0 <= z - way < at.L
        src = (self.sib if first else self.recv).at[zd, part, :]
        slot = self.slot(z + way, way, zd)
        device = {"head": at.up if way > 0 else at.down}
        return remote(src, self.recv.at[slot, part, :], self.fwd_send.at[zd, half], self.recv_sem.at[slot, half], device)

    def landed(self, z, way, zd, half):
        at, part = self.at, self.part(half)
        slot = self.slot(z, way, zd)
        block = self.recv.at[slot, part, :]
        device = {"head": at.down if way > 0 else at.up}
        return remote(block, block, self.fwd_send.at[zd, half], self.recv_sem.at[slot, half], device)

    def exchange(self, zd, src):
        return remote(src, self.sib.at[zd], self.sib_send.at[zd], self.sib_recv.at[zd], {"head": self.at.sib})

    def combine(self, zd, mine):
        def add(rows):
            self.sib[zd, rows, :] = (self.sib[zd, rows, :].astype(F32) + mine[rows, :].astype(F32)).astype(BF16)

        chunk_loop(self.sib.shape[1], 32, add)

    def add(self, zd, half):
        def one(rows):
            self.recv[zd, rows, :] = (self.recv[zd, rows, :].astype(F32) + self.sib[zd, rows, :].astype(F32)).astype(BF16)

        step = min(32, self.half)

        @pl.loop(0, self.half // step)
        def _(i):
            one(pl.ds(pl.multiple_of(half * self.half + i * step, step), step))

    def final(self, put):
        at, z = self.at, self.at.z

        def run(extra):
            def part(rows):
                value = self.sib[z, rows, :].astype(F32)
                for slot in extra:
                    value = value + self.recv[slot, rows, :].astype(F32)
                put(rows, value)

            chunk_loop(self.sib.shape[1], 32, part)

        @pl.when(z == 0)
        def _():
            run((at.L,))

        @pl.when(z == at.L - 1)
        def _():
            run((z,))

        @pl.when((z > 0) & (z < at.L - 1))
        def _():
            run((z, at.L))

    def sent(self):
        at = self.at
        for zd in range(at.L):

            @pl.when(zd != at.z)
            def _():
                for half in (0, 1):
                    block = self.recv.at[zd, self.part(half), :]
                    remote(block, block, self.fwd_send.at[zd, half], self.recv_sem.at[zd, half], {"head": at.up}).wait_send()


class SlotGather:
    def __init__(self, at, own, out, sems):
        self.at, self.own, self.out = at, own, out
        self.line_recv, self.up_send, self.down_send, self.sib_send, self.sib_recv, self.local = sems
        self.half = own.shape[0] // 2

    @staticmethod
    def sems(L):
        return [DMA((L, 2))] * 5 + [DMA]

    def block(self, index, half):
        return self.out.at[index, pl.ds(half * self.half, self.half), :]

    def mine(self, half):
        return self.own.at[pl.ds(half * self.half, self.half), :]

    def copy(self, z, way, zb, half):
        at = self.at
        dst = self.block(zb * 2 + at.c, half)
        src = self.mine(half) if zb == z else dst
        send = (self.up_send if way > 0 else self.down_send).at[zb, half]
        return remote(src, dst, send, self.line_recv.at[zb, half], {"head": at.up if way > 0 else at.down})

    def landed(self, z, way, zb, half):
        at = self.at
        dst = self.block(zb * 2 + at.c, half)
        return remote(dst, dst, self.up_send.at[zb, half], self.line_recv.at[zb, half], {"head": at.down if way > 0 else at.up})

    def share(self, zb, half, src=None):
        at = self.at
        dst = self.block(zb * 2 + at.c, half)
        return remote(dst if src is None else src, dst, self.sib_send.at[zb, half], self.sib_recv.at[zb, half], {"head": at.sib})

    def keep(self):
        return pltpu.make_async_copy(self.own, self.out.at[self.at.h], self.local)

    def begin(self):
        for half in (0, 1):
            self.share(self.at.z, half, self.mine(half)).start()
        self.keep().start()

    def finish(self):
        at = self.at
        self.keep().wait()
        for zb in range(at.L):
            for half in (0, 1):
                self.share(zb, half).wait_send()
                other = self.block(zb * 2 + 1 - at.c, half)
                remote(other, other, self.sib_send.at[zb, half], self.sib_recv.at[zb, half], {"head": at.sib}).wait_recv()

            @pl.when((zb <= at.z) & (at.z < at.L - 1))
            def _():
                for half in (0, 1):
                    self.copy(-1, 1, zb, half).wait_send()

            @pl.when((zb >= at.z) & (at.z > 0))
            def _():
                for half in (0, 1):
                    self.copy(-1, -1, zb, half).wait_send()


def norm_back_part(values, gain, grad):
    inv_root = inv_root_of(values)
    unit = values * inv_root
    weighted = grad * gain
    back = inv_root * (weighted - unit * jnp.mean(weighted * unit, axis=-1, keepdims=True))
    return back, jnp.sum(grad * unit, axis=0, keepdims=True)


def attention_in(n, H, tokens, cotangent, gains, weights, positions, frequencies):
    rows, T, D = tokens.shape
    R, W = weights[0].shape
    ff = weights[4].shape[1]
    L = H // 2
    S = H * T
    heads = W // HEAD_DIM
    mix = ("mix", 0)
    rank = [("x", r) for r in range(rows)] + [("ct", 0), mix]
    tasks = []
    for r in range(rows):
        tasks += [((kind, r, 0), (("x", r),), (), 0, 1) for kind in ("qkv", "low", "high")]
        if r == 0:
            tasks += [(("send", 0, i), (), (mix,), i, 1) for i in range(L)]
        else:
            tasks.append((("terms", r, 0), (), (), 0, 1))
    plan = Plan(L, rank, [mix], {}, {}, {j: 0 if j[0] == "ct" else 2 for j in rank if j != mix}, tasks)
    names = Names()
    z_at = [names.add(SlotGather.sems(L)) for _ in range(rows + 1)]
    w_at = [names.add(BatchGather.sems(n)) for _ in range(6)]
    g_at = names.add([DMA((n,)), DMA((n,)), DMA])
    m_at = names.add(SlotReduce.bufs(L, T, D))
    ms_at = names.add(SlotReduce.sems(L))
    rest = names.add(
        [
            pltpu.VMEM((rows, T, D), BF16),
            pltpu.VMEM((2, 2, T, D), BF16),
            pltpu.VMEM((2, 2, T, D), BF16),
            pltpu.VMEM((D, 3 * W), BF16),
            pltpu.VMEM((D, W), BF16),
            DMA((2,)),
            DMA((2,)),
            DMA((2,)),
        ]
    )
    wide = min(512, D)

    def kernel(
        tok,
        ct,
        gain,
        pos,
        freq,
        wq,
        wk,
        wv,
        wo,
        wg,
        wu,
        attn_in,
        ct_first,
        w_qkv,
        w_o,
        w_gu,
        terms,
        gains_full,
        qkv,
        lse,
        attended,
        mixed,
        mid,
        cos,
        sin,
        st,
        *scratch,
    ):
        at = Place(n, H)
        normed, xb, stage, wqkv, wout, x_sem, o_sem, w_sem = scratch[rest]
        gsend, grecv, glocal = scratch[g_at]
        at.greet(all_batch=True)

        def gain_dst(b):
            return gains_full.at[:, pl.ds(pl.multiple_of(b * R, R), R)]

        def gain_send(off):
            return remote(gain, gain_dst(at.b), gsend.at[off], grecv.at[off], {"batch": (at.b + off) % n})

        own_gain = pltpu.make_async_copy(gain, gain_dst(at.b), glocal)
        own_gain.start()
        for off in range(1, n):
            gain_send(off).start()

        gathers = {("x", r): SlotGather(at, normed.at[r], attn_in.at[r], scratch[z_at[r]]) for r in range(rows)}
        gathers[("ct", 0)] = SlotGather(at, ct.at[0], ct_first, scratch[z_at[rows]])
        total = SlotReduce(at, *scratch[m_at], scratch[ms_at])

        def norm(r):
            def one(part):
                values = tok[r, part, :].astype(F32)
                normed[r, part, :] = (values * inv_root_of(values) * gains_full[0:1, :]).astype(BF16)

            chunk_loop(T, 32, one)
            gathers[("x", r)].begin()

        outs = []
        for src, dst, col, width in (
            (wq, w_qkv, 0, W),
            (wk, w_qkv, W, W),
            (wv, w_qkv, 2 * W, W),
            (wo, w_o, 0, W),
            (wg, w_gu, 0, ff),
            (wu, w_gu, ff, ff),
        ):
            outs.append((src, lambda b, part, dst=dst, col=col, width=width: dst.at[b, part, pl.ds(col, width)]))
        shards = [BatchGather(at, src, out, scratch[w_at[i]]) for i, (src, out) in enumerate(outs)]
        gathers[("ct", 0)].begin()
        for job in shards[:4]:
            job.start()

        def norms():
            own_gain.wait()
            for off in range(1, n):
                got = gain_dst((at.b + n - off) % n)
                remote(got, got, gsend.at[off], grecv.at[off], {"batch": (at.b + off) % n}).wait()
            for r in range(rows):
                norm(r)

        def tables(r):
            step = 128
            for i in range(S // step):
                places = pos[r : r + 1, i * step : (i + 1) * step]
                index = lax.broadcasted_iota(jnp.int32, places.shape, 1) + i * step
                st[r, 0:1, i * step : (i + 1) * step] = index - places

            @pl.loop(0, S // step)
            def _(i):
                part = pl.ds(pl.multiple_of(i * step, step), step)
                down = jnp.broadcast_to(pos[r : r + 1, part].astype(F32), (step, step)).T
                angles = down * freq[...]
                lane = lax.broadcasted_iota(jnp.int32, angles.shape, 1)
                cos[r, part, :] = jnp.cos(angles)
                sine = jnp.sin(angles)
                sin[r, part, :] = jnp.where(lane % HEAD_DIM < HEAD_DIM // 2, -sine, sine)

        def weight_loads():
            return [
                pltpu.make_async_copy(w_qkv.at[b], wqkv.at[pl.ds(b * R, R), :], w_sem.at[0]) for b in range(n)
            ] + [pltpu.make_async_copy(w_o.at[b], wout.at[pl.ds(b * R, R), :], w_sem.at[1]) for b in range(n)]

        def x_load(r, b):
            return pltpu.make_async_copy(attn_in.at[r, pl.ds(2 * b, 2)], xb.at[b % 2], x_sem.at[b % 2])

        def make_qkv(r):
            gathers[("x", r)].finish()
            x_load(r, 0).start()
            x_load(r, 1).start()
            if r == 0:
                pltpu.make_async_copy(wqkv, wqkv, w_sem.at[0]).wait()
                pltpu.make_async_copy(wout, wout, w_sem.at[1]).wait()
            for b in range(L):
                x_load(r, b).wait()
                part = pl.ds(b * 2 * T, 2 * T)
                lin = jnp.dot(xb[b % 2].reshape(2 * T, D), wqkv[...], preferred_element_type=F32)
                if b + 2 < L:
                    x_load(r, b + 2).start()
                c, s = cos[r, part, :], sin[r, part, :]
                qkv[r, part, 0:W] = rotate(lin[:, :W], c, s).astype(BF16)
                qkv[r, part, W : 2 * W] = rotate(lin[:, W : 2 * W], c, s).astype(BF16)
                qkv[r, part, 2 * W : 3 * W] = lin[:, 2 * W :].astype(BF16)

        def head(r, h):
            attend(qkv.at[r], st.at[r], lse.at[r], attended.at[r], h, W)

        def store(r, b):
            return pltpu.make_async_copy(stage.at[b % 2], terms.at[r - 1, pl.ds(2 * b, 2)], o_sem.at[b % 2])

        def make_terms(r):
            for b in range(L):
                if b >= 2:
                    store(r, b - 2).wait()
                for j in range(D // wide):
                    cols = pl.ds(j * wide, wide)
                    value = cols_dot(attended[r, pl.ds(b * 2 * T, 2 * T), :], wout[cols, :]).astype(BF16)
                    stage[b % 2, 0, :, cols] = value[:T]
                    stage[b % 2, 1, :, cols] = value[T:]
                store(r, b).start()
            for b in (L - 2, L - 1):
                store(r, b).wait()

        def make_send(i):
            zd = plan.block(at.z, i)
            part = pl.ds(pl.multiple_of(zd * 2 * T, 2 * T), 2 * T)
            for j in range(D // wide):
                cols = pl.ds(j * wide, wide)
                value = cols_dot(attended[0, part, :], wout[cols, :]).astype(BF16)
                stage[i % 2, 0, :, cols] = value[:T]
                stage[i % 2, 1, :, cols] = value[T:]
            total.exchange(zd, stage.at[i % 2, 1 - at.c]).start()

        def combine(i):
            zd = plan.block(at.z, i)
            total.exchange(zd, stage.at[i % 2, 1 - at.c]).wait()
            total.combine(zd, stage.at[i % 2, at.c])

        def finish(j):
            def put(part, value):
                value = value + tok[0, part, :].astype(F32)
                mixed[part, :] = value
                mid[part, :] = (value * inv_root_of(value) * gains_full[1:2, :]).astype(BF16)

            total.final(put)
            total.sent()

        def task(name):
            kind, r, i = name
            if kind == "qkv":
                make_qkv(r)
            elif kind == "low":
                pl.loop(0, heads // 2)(lambda h: head(r, h))
            elif kind == "high":
                pl.loop(heads // 2, heads)(lambda h: head(r, h))
            elif kind == "send":
                make_send(i)
            else:
                make_terms(r)

        def after(s):
            name = plan.tasks[s - 1][0] if s - 1 in plan.tasks else None
            if name and name[0] == "send":
                combine(name[2])
            if s == 1:
                norms()
            if s - 4 in range(rows):
                tables(s - 4)
            if s == 3:
                for job in shards[:4]:
                    job.forward()
                for job in shards[4:]:
                    job.start()
            if s == 6:
                for job in shards[:4]:
                    job.finish()
                for job in weight_loads():
                    job.start()
            if s == 11:
                shards[4].forward()
            if s == 15:
                shards[5].forward()

        run_plan(plan, at, {**gathers, mix: total}, task, after, finish)
        gathers[("ct", 0)].finish()
        for job in shards[4:]:
            job.finish()

    return pl.pallas_call(
        kernel,
        out_shape=(
            jax.ShapeDtypeStruct((rows, H, T, D), BF16),
            jax.ShapeDtypeStruct((H, T, D), BF16),
            jax.ShapeDtypeStruct((n, R, 3 * W), BF16),
            jax.ShapeDtypeStruct((n, R, W), BF16),
            jax.ShapeDtypeStruct((n, R, 2 * ff), BF16),
            jax.ShapeDtypeStruct((rows - 1, H, T, D), BF16),
            jax.ShapeDtypeStruct((8, D), F32),
            jax.ShapeDtypeStruct((rows, S, 3 * W), BF16),
            jax.ShapeDtypeStruct((rows, 8, S), F32),
            jax.ShapeDtypeStruct((rows, S, W), BF16),
            jax.ShapeDtypeStruct((T, D), F32),
            jax.ShapeDtypeStruct((T, D), BF16),
            jax.ShapeDtypeStruct((rows, S, 128), F32),
            jax.ShapeDtypeStruct((rows, S, 128), F32),
            jax.ShapeDtypeStruct((rows, 1, S), jnp.int32),
        ),
        in_specs=[VMEM, VMEM] + [VMEM] * 3 + [ANY] * 6,
        out_specs=(ANY,) * 6 + (VMEM,) * 9,
        scratch_shapes=names.shapes,
        compiler_params=pltpu.CompilerParams(collective_id=1, has_side_effects=True, vmem_limit_bytes=VMEM_LIMIT),
        name="attention_in",
    )(tokens, cotangent, gains, positions, frequencies, *weights)


def feed_forward(n, H, terms, ct_first, mixed_first, mid_first, tokens, cotangent, gains, w_gu, w_d):
    rows, T, D = tokens.shape
    L = H // 2
    ff = w_d.shape[1]
    S = H * T
    R = w_d.shape[0]
    U = R // 2
    square = n == 4
    rank = []
    for kinds in (("mix", "in"), ("sum", "att"), ("out",)):
        rank += [
            (kind, r)
            for r in range(rows)
            for kind in kinds
            if (kind, r) not in (("mix", 0), ("att", rows - 1), ("out", rows - 1))
        ]
        if kinds[0] == "mix":
            rank[2:2] = [("ct", r) for r in range(1, rows)]
    tasks = []
    for r in range(rows):
        for i in range(L):
            needs = (("in", r),) + ((("ct", r),) if r else ())
            made = (("sum", r), ("out", r)) if r + 1 < rows else (("sum", r),)
            if r and i < L // 2:
                tasks.append((("both", r, i), needs, made, i, 1))
            else:
                tasks.append((("first", r, i), needs, (), i, 1))
                tasks.append((("second", r, i), (), made, i, 1))
    tasks += [(("grad", k, 0), (), (), 0, 1) for k in range(2 * n)]
    plan = Plan(
        L,
        rank,
        [j for j in rank if j[0] in ("mix", "sum", "out")],
        {("mix", r): [(r - 1) * L + i for i in range(L)] for r in range(1, rows)},
        {**{("mix", r): ("in", r) for r in range(1, rows)}, **{("sum", r): ("att", r) for r in range(rows - 1)}},
        {("in", 0): 0, **{("ct", r): 0 for r in range(1, rows)}},
        tasks,
    )
    names = Names()
    n_bufs = [names.add(SlotReduce.bufs(L, T, D)) for _ in range(2 * rows - 1)]
    n_sems = [names.add(SlotReduce.sems(L)) for _ in range(2 * rows - 1)]
    n_gsem = [names.add(SlotGather.sems(L)) for _ in range(2 * rows)]
    n_wsem = names.add(BatchGather.sems(n))
    rest = names.add(
        [
            pltpu.VMEM((rows, T, D), BF16),
            pltpu.VMEM((rows - 1, T, D), BF16),
            pltpu.VMEM((rows - 1, L, T, D), BF16),
            pltpu.VMEM((rows, T, D), F32),
            pltpu.VMEM((2, 2, T, D), BF16),
            pltpu.VMEM((2, 2, T, D), BF16),
            pltpu.VMEM((max(D, rows * S), 2 * ff), BF16),
            pltpu.VMEM((max(D, rows * S), ff), BF16),
            pltpu.VMEM((2, 2, T, D), BF16),
            pltpu.VMEM((2, 2, T, D), BF16),
            pltpu.VMEM((2, max(2 * T, U), ff), BF16),
            pltpu.VMEM((2, max(2 * T, U), 2 * ff), BF16),
            pltpu.VMEM((2, rows, H, T, U), BF16),
            pltpu.VMEM((2, rows, H, T, U), BF16),
            DMA((6,)),
            DMA((2, 2)),
            DMA((2, 2)),
            DMA((2,)),
            DMA((2,)),
            DMA((2,)),
            DMA((rows, L)),
            DMA((2,)),
            DMA((2,)),
            DMA((2,)),
            DMA((2,)),
        ]
    )
    tile = min(512, ff)
    wide = min(512, D)

    def kernel(
        src,
        ct_row,
        mixed_row,
        mid_row,
        tok,
        ct,
        gain,
        wgu_hbm,
        wd_own,
        ctf,
        mlp_in,
        g_att,
        hid_hbm,
        ggu_hbm,
        grad_gu,
        grad_d,
        first_gu,
        first_d,
        out_terms,
        g_mixed,
        layer_out,
        mixed_last,
        att_last,
        gain_sum,
        *scratch,
    ):
        at = Place(n, H)
        z = at.z
        (
            normed,
            att,
            own_terms,
            mixed,
            stage_g,
            stage_o,
            wgu,
            wd,
            xb,
            cb,
            hb,
            gb,
            xt,
            ct_t,
            t_sem,
            gsend,
            grecv,
            last_sem,
            w_sem,
            row_sem,
            own_sem,
            x_sem,
            c_sem,
            h_sem,
            g_sem,
        ) = scratch[rest]
        loads = [pltpu.make_async_copy(wgu_hbm, wgu.at[pl.ds(0, D), :], w_sem.at[0])]
        down = BatchGather(
            at,
            wd_own,
            lambda b, part: wd.at[pl.ds(pl.multiple_of(b * R + part.start, U), part.size), :],
            scratch[n_wsem],
        )
        row_loads = [
            pltpu.make_async_copy(mixed_row, mixed.at[0], row_sem.at[0]),
            pltpu.make_async_copy(mid_row, normed.at[0], row_sem.at[1]),
        ]
        for job in row_loads:
            job.start()
        red, gat = {}, {}
        for r in range(rows):
            for kind in ("mix", "sum"):
                red[(kind, r)] = SlotReduce(at, *scratch[n_bufs[r]], scratch[n_sems[r]])
            if r + 1 < rows:
                red[("out", r)] = SlotReduce(at, *scratch[n_bufs[rows + r]], scratch[n_sems[rows + r]])
            gat[("in", r)] = SlotGather(at, normed.at[r], mlp_in.at[r], scratch[n_gsem[r]])
            if r + 1 < rows:
                gat[("att", r)] = SlotGather(at, att.at[r], g_att.at[r], scratch[n_gsem[r]])
            if r:
                gat[("ct", r)] = SlotGather(at, ct.at[r], ctf.at[r - 1], scratch[n_gsem[rows + r]])
        both = {**red, **gat}
        at.greet()
        down.start()

        def mine_of(r, zd):
            return own_terms.at[r - 1, zd]

        def own_load(r, zd):
            return pltpu.make_async_copy(src.at[r - 1, zd * 2 + at.c], mine_of(r, zd), own_sem.at[r, zd])

        def exchange(r, zd):
            return red[("mix", r)].exchange(zd, src.at[r - 1, zd * 2 + 1 - at.c])

        for job in row_loads:
            job.wait()
        gat[("in", 0)].begin()
        for r in range(1, rows):
            for i in range(L):
                zd = plan.block(z, i)
                exchange(r, zd).start()
                own_load(r, zd).start()
        for r in range(1, rows):
            gat[("ct", r)].begin()
        for job in loads:
            job.start()
        gain_sum[...] = jnp.zeros_like(gain_sum)

        def combine_mix(r, i):
            zd = plan.block(z, i)
            own_load(r, zd).wait()
            exchange(r, zd).wait()
            red[("mix", r)].combine(zd, mine_of(r, zd))

        def kinds_of(r):
            return (("sum", stage_g), ("out", stage_o)) if r + 1 < rows else (("sum", stage_g),)

        def last_store(i):
            zd = plan.block(z, i)
            return pltpu.make_async_copy(stage_o.at[i % 2], out_terms.at[pl.ds(2 * zd, 2)], last_sem.at[i % 2])

        def combine_terms(r, i):
            zd = plan.block(z, i)
            if r + 1 == rows:
                last_store(i).wait()
            for kind, stage in kinds_of(r):
                job = red[(kind, r)]
                job.exchange(zd, stage.at[i % 2, 1 - at.c]).wait()
                job.combine(zd, stage.at[i % 2, at.c])

        def x_load(r, i):
            blk = plan.block(z, i)
            return (
                pltpu.make_async_copy(mlp_in.at[r, pl.ds(2 * blk, 2)], xb.at[i % 2], x_sem.at[i % 2]),
                pltpu.make_async_copy(
                    (ctf.at[r - 1] if r else ct_row).at[pl.ds(2 * blk, 2)], cb.at[i % 2], c_sem.at[i % 2]
                ),
            )

        def act_store(r, i):
            blk = plan.block(z, i)
            at_row = pl.ds(pl.multiple_of(r * S + blk * 2 * T, 2 * T), 2 * T)
            return (
                pltpu.make_async_copy(hb.at[i % 2, pl.ds(0, 2 * T), :], hid_hbm.at[at_row, :], h_sem.at[i % 2]),
                pltpu.make_async_copy(gb.at[i % 2, pl.ds(0, 2 * T), :], ggu_hbm.at[at_row, :], g_sem.at[i % 2]),
            )

        def first_part(r, i):
            if i == 0:
                gat[("in", r)].finish()
                if r:
                    gat[("ct", r)].finish()
                for job in x_load(r, 0):
                    job.start()
                if r == 0:
                    down.finish()
                    for job in loads:
                        job.wait()
            for job in x_load(r, i):
                job.wait()
            if i + 1 < L:
                for job in x_load(r, i + 1):
                    job.start()
            if r * L + i >= 2:
                before = (r, i - 2) if i >= 2 else (r - 1, L + i - 2)
                for job in act_store(*before):
                    job.wait()
            k = i % 2

            @pl.loop(0, ff // tile)
            def _(j):
                cols = pl.ds(pl.multiple_of(j * tile, tile), tile)
                up_cols = pl.ds(pl.multiple_of(ff + j * tile, tile), tile)
                x = xb[k].reshape(2 * T, D)
                gate = jnp.dot(x, wgu[0:D, cols], preferred_element_type=F32)
                up = jnp.dot(x, wgu[0:D, up_cols], preferred_element_type=F32)
                back = jnp.dot(cb[k].reshape(2 * T, D), wd[0:D, cols], preferred_element_type=F32)
                sig = 1.0 / (1.0 + jnp.exp(-gate))
                silu = gate * sig
                hb[k, 0 : 2 * T, cols] = (silu * up).astype(BF16)
                gb[k, 0 : 2 * T, cols] = (back * up * (sig * (1.0 + gate * (1.0 - sig)))).astype(BF16)
                gb[k, 0 : 2 * T, up_cols] = (back * silu).astype(BF16)

            for job in act_store(r, i):
                job.start()

        def second_part(r, i):
            k = i % 2

            @pl.loop(0, D // wide)
            def _(j):
                cols = pl.ds(pl.multiple_of(j * wide, wide), wide)
                back = cols_dot(gb[k, 0 : 2 * T, :], wgu[cols, :]).astype(BF16)
                stage_g[k, 0, :, cols] = back[:T]
                stage_g[k, 1, :, cols] = back[T:]
                out = cols_dot(hb[k, 0 : 2 * T, :], wd[cols, :]).astype(BF16)
                stage_o[k, 0, :, cols] = out[:T]
                stage_o[k, 1, :, cols] = out[T:]

            zd = plan.block(z, i)
            if r + 1 == rows:
                last_store(i).start()
            for kind, stage in kinds_of(r):
                red[(kind, r)].exchange(zd, stage.at[k, 1 - at.c]).start()

        def finish_mix(r):
            def put(part, value):
                value = value + tok[r, part, :].astype(F32)
                mixed[r, part, :] = value
                if r + 1 == rows:
                    mixed_last[part, :] = value
                normed[r, part, :] = (value * inv_root_of(value) * gain[1:2, :]).astype(BF16)

            red[("mix", r)].final(put)
            red[("mix", r)].sent()
            gat[("in", r)].begin()

        def finish_sum(r):
            def put(part, value):
                back, gain_part = norm_back_part(mixed[r, part, :], gain[1:2, :], value)
                total = ct[r, part, :].astype(F32) + back
                g_mixed[r, part, :] = total
                if r + 1 < rows:
                    att[r, part, :] = total.astype(BF16)
                else:
                    att_last[part, :] = total.astype(BF16)
                gain_sum[1:2, :] += gain_part

            red[("sum", r)].final(put)
            red[("sum", r)].sent()
            if r + 1 < rows:
                gat[("att", r)].begin()

        def finish_out(r):
            def put(part, value):
                layer_out[r, part, :] = (mixed[r, part, :] + value).astype(BF16)

            red[("out", r)].final(put)
            red[("out", r)].sent()

        units = send_units(at, square, n)
        again = [
            pltpu.make_async_copy(ggu_hbm, wgu.at[pl.ds(0, rows * S), :], w_sem.at[0]),
            pltpu.make_async_copy(hid_hbm, wd.at[pl.ds(0, rows * S), :], w_sem.at[1]),
        ]

        def columns(k):
            cols = pl.ds(pl.multiple_of((units[k][0] * 2 + units[k][1]) * U, U), U)
            return [
                pltpu.make_async_copy(mlp_in.at[:, :, :, cols], xt.at[k % 2], t_sem.at[k % 2]),
                pltpu.make_async_copy(ct_row.at[:, :, cols], ct_t.at[k % 2, 0], t_sem.at[2 + k % 2]),
                pltpu.make_async_copy(
                    ctf.at[:, :, :, cols], ct_t.at[k % 2, pl.ds(1, rows - 1)], t_sem.at[4 + k % 2]
                ),
            ]

        def grad_store(k):
            b, half = units[k][:2]
            part = pl.ds(half * U, U)
            return [
                pltpu.make_async_copy(hb.at[k % 2, pl.ds(0, U), :], grad_d.at[b, part, :], h_sem.at[k % 2]),
                pltpu.make_async_copy(gb.at[k % 2, pl.ds(0, U), :], grad_gu.at[b, part, :], g_sem.at[k % 2]),
            ]

        def grad_sends(k):
            b, half, _, to = units[k]
            part = pl.ds(half * U, U)
            return [
                remote(src.at[b, part, :], dst.at[k], gsend.at[a, k], grecv.at[a, k], {"batch": to})
                for a, (src, dst) in enumerate(((grad_d, first_d), (grad_gu, first_gu)))
            ]

        def prepare_grads():
            for i in (L - 2, L - 1):
                for job in act_store(rows - 1, i):
                    job.wait()
            for job in again + columns(0):
                job.start()

        def grad(k):
            if k == 0:
                for job in again:
                    job.wait()
            for job in columns(k):
                job.wait()
            if k + 1 < 2 * n:
                for job in columns(k + 1):
                    job.start()
            ring = k % 2

            @pl.loop(0, 2 * ff // tile)
            def _(j):
                cols = pl.ds(pl.multiple_of(j * tile, tile), tile)
                x = xt[ring].reshape(rows * S, U)
                gb[ring, 0:U, cols] = rows_dot(x, wgu[0 : rows * S, cols]).astype(BF16)

            @pl.loop(0, ff // tile)
            def _(j):
                cols = pl.ds(pl.multiple_of(j * tile, tile), tile)
                x = ct_t[ring].reshape(rows * S, U)
                hb[ring, 0:U, cols] = rows_dot(x, wd[0 : rows * S, cols]).astype(BF16)

            for job in grad_store(k):
                job.start()

        def task(name):
            kind, r, i = name
            if kind == "first":
                first_part(r, i)
            elif kind in ("second", "both"):
                if kind == "both":
                    first_part(r, i)
                second_part(r, i)
                if (r, i) == (rows - 1, L - 1):
                    prepare_grads()
            else:
                grad(r)

        def after(s):
            if s == 4:
                down.forward()
            if s + 1 < (rows - 1) * L:
                combine_mix(1 + (s + 1) // L, (s + 1) % L)
            name = plan.tasks[s - 1][0] if s - 1 in plan.tasks else None
            if name and name[0] in ("second", "both"):
                combine_terms(*name[1:])
            if name and name[0] == "grad":
                for job in grad_store(name[1]):
                    job.wait()
                if square and name[1] < 2:
                    for job in grad_sends(name[1]):
                        job.start()

        def finish(j):
            {"mix": finish_mix, "sum": finish_sum, "out": finish_out}[j[0]](j[1])

        combine_mix(1, 0)
        run_plan(plan, at, both, task, after, finish)
        if square:
            for k in range(2):
                for job in grad_sends(k):
                    job.wait()
        for r in range(rows - 1):
            gat[("att", r)].finish()

    return pl.pallas_call(
        kernel,
        out_shape=(
            jax.ShapeDtypeStruct((rows - 1, H, T, D), BF16),
            jax.ShapeDtypeStruct((rows, H, T, D), BF16),
            jax.ShapeDtypeStruct((rows - 1, H, T, D), BF16),
            jax.ShapeDtypeStruct((rows * S, ff), BF16),
            jax.ShapeDtypeStruct((rows * S, 2 * ff), BF16),
            jax.ShapeDtypeStruct((n, 2 * U, 2 * ff), BF16),
            jax.ShapeDtypeStruct((n, 2 * U, ff), BF16),
            jax.ShapeDtypeStruct((2, U, 2 * ff), BF16),
            jax.ShapeDtypeStruct((2, U, ff), BF16),
            jax.ShapeDtypeStruct((H, T, D), BF16),
            jax.ShapeDtypeStruct((rows, T, D), F32),
            jax.ShapeDtypeStruct((rows - 1, T, D), BF16),
            jax.ShapeDtypeStruct((T, D), F32),
            jax.ShapeDtypeStruct((T, D), BF16),
            jax.ShapeDtypeStruct((8, D), F32),
        ),
        in_specs=[ANY, ANY, ANY, ANY, VMEM, VMEM, VMEM, ANY, ANY],
        out_specs=(ANY,) * 10 + (VMEM,) * 5,
        scratch_shapes=names.shapes,
        compiler_params=pltpu.CompilerParams(collective_id=2, has_side_effects=True, vmem_limit_bytes=VMEM_LIMIT),
        name="feed_forward",
    )(terms, ct_first, mixed_first, mid_first, tokens, cotangent, gains, w_gu, w_d)


class LateReduce:
    def __init__(self, at, src, first, parts, bufs, sems):
        self.at, self.src, self.first, self.parts = at, src, first, parts
        if at.square:
            self.mine, self.came = bufs
        self.load, self.send, self.recv = sems
        self.U = src.shape[1] // 2

    @staticmethod
    def bufs(n, U, K):
        return [pltpu.VMEM((2, U, K), BF16)] * 2 if n == 4 else []

    @staticmethod
    def sems(n):
        m = 4 if n == 4 else n
        return [DMA((4,)), DMA((m,)), DMA((m,))]

    def loads(self, j):
        at, U = self.at, self.U
        b = at.y * 2 + 1 - at.x if j else (1 - at.y) * 2 + at.x
        return [
            pltpu.make_async_copy(self.src.at[b, pl.ds(j * U, U), :], self.mine.at[j], self.load.at[2 * j]),
            pltpu.make_async_copy(self.first.at[j], self.came.at[j], self.load.at[2 * j + 1]),
        ]

    def pass_on(self, j):
        to = {"batch": self.at.xn if j else self.at.yn}
        dst = self.parts.at[1, pl.ds(j * self.U, self.U), :]
        return remote(self.mine.at[j], dst, self.send.at[j], self.recv.at[j], to)

    def rest(self, j):
        at, rows = self.at, pl.ds(j * self.U, self.U)
        b = (1 - at.y) * 2 + at.x if j else at.y * 2 + 1 - at.x
        to = {"batch": at.yn if j else at.xn}
        return remote(self.src.at[b, rows, :], self.parts.at[0, rows, :], self.send.at[2 + j], self.recv.at[2 + j], to)

    def direct(self, off):
        to = (self.at.b + off) % self.at.n
        return remote(self.src.at[to], self.parts.at[off - 1], self.send.at[off], self.recv.at[off], {"batch": to})

    def start(self):
        if self.at.square:
            for j in (0, 1):
                for job in self.loads(j):
                    job.start()
        else:
            for off in range(1, self.at.n):
                self.direct(off).start()

    def second_step(self):
        if not self.at.square:
            return
        for j in (0, 1):
            for job in self.loads(j):
                job.wait()

            def add(rows, j=j):
                self.mine[j, rows, :] = (self.mine[j, rows, :].astype(F32) + self.came[j, rows, :].astype(F32)).astype(BF16)

            chunk_loop(self.U, 16, add)
            self.pass_on(j).start()
        for j in (0, 1):
            self.rest(j).start()

    def finish(self):
        if self.at.square:
            for j in (0, 1):
                self.pass_on(j).wait()
                self.rest(j).wait()
        else:
            for off in range(1, self.at.n):
                self.direct(off).wait()


def send_units(at, square, n):
    if not square:
        return [(k // 2, k % 2, None, None) for k in range(2 * n)]
    return [
        ((1 - at.y) * 2 + 1 - at.x, 0, 1 - at.y, at.xn),
        ((1 - at.y) * 2 + 1 - at.x, 1, 3 - at.x, at.yn),
        (at.y * 2 + 1 - at.x, 0, at.y, at.xn),
        ((1 - at.y) * 2 + at.x, 1, 2 + at.x, at.yn),
        ((1 - at.y) * 2 + at.x, 0, None, None),
        (at.y * 2 + 1 - at.x, 1, None, None),
        (at.b, 0, None, None),
        (at.b, 1, None, None),
    ]


def BACK_RANK(last):
    return [("att", last), ("out", last)] + [("in", r) for r in range(last + 1)]


def attention_back(
    n,
    H,
    g_att,
    att_last,
    out_terms,
    mixed_last,
    attended,
    qkv,
    lse,
    attn_in,
    w_qkv,
    w_o,
    cosine,
    sine,
    starts,
    tokens,
    g_mixed,
    gains,
    gain_sum,
    g_gu,
    g_d,
    first_gu,
    first_d,
):
    rows, T, D = tokens.shape
    L = H // 2
    S = H * T
    R, ff = g_d.shape[1], g_d.shape[2]
    W = w_o.shape[1]
    heads = W // HEAD_DIM
    U = R // 2
    square = n == 4
    step = 2 * T
    wide = min(512, D)
    blocks = L
    last = rows - 1
    gather, out = ("att", last), ("out", last)
    rank = BACK_RANK(last)
    tasks = []
    for r in range(rows):
        tasks.append((("prob", r, 0), (gather,) if r == last else (), (), 0, 1))
        if r == 0:
            tasks.append((("heads", r, 0), (), (), 0, 1))
        else:
            tasks += [(("head", r, h), (), (), 0, 1) for h in range(heads)]
        tasks += [(("terms", r, i), (), (("in", r),), i, 1) for i in range(L)]
    tasks += [(("grad", k, 0), (), (), 0, 1) for k in range(n)]
    plan = Plan(L, rank, [j for j in rank if j != gather], {out: list(range(L))}, {}, {gather: 0}, tasks)
    P = 2 if square else n - 1
    names = Names()
    r_bufs = [names.add(SlotReduce.bufs(L, T, D)) for _ in range(rows)]
    r_sems = [names.add(SlotReduce.sems(L)) for _ in range(rows)]
    o_sems = names.add(SlotReduce.sems(L))
    l_sems = names.add(SlotGather.sems(L))
    m_bufs = [names.add(LateReduce.bufs(n, U, K)) for K in (ff, 2 * ff)]
    m_sems = [names.add(LateReduce.sems(n)) for _ in range(2)]
    if square:
        a_bufs = names.add([pltpu.VMEM((4, U, 4 * W), BF16), pltpu.VMEM((2, U, 4 * W), BF16)])
        a_sems = names.add([DMA((6,)), DMA((6,))])
    else:
        a_bufs = names.add([pltpu.VMEM((n, 2, U, 4 * W), BF16)])
        a_sems = names.add([DMA((n,)), DMA((n,))])
    s_at = names.add(
        [pltpu.VMEM((8, D), F32), pltpu.VMEM((n, 8, R), F32), pltpu.VMEM((H, 8, R), F32)]
        + [DMA((n,)), DMA((n,)), DMA((H,)), DMA((H,)), DMA]
    )
    rest = names.add(
        [
            pltpu.VMEM((2, 2, T, D), BF16),
            pltpu.VMEM((2, T, D), BF16),
            pltpu.VMEM((S, W), BF16),
            pltpu.VMEM((S, W), F32),
            pltpu.VMEM((S, W), F32),
            pltpu.VMEM((S, W), F32),
            pltpu.VMEM((rows * S, 3 * W), BF16),
            pltpu.VMEM((2, 2, T, D), BF16),
            pltpu.VMEM((2, rows * S, U), BF16),
            pltpu.VMEM((2, rows, H, T, U), BF16),
            pltpu.VMEM((2 * n, U, 4 * W), BF16),
            DMA((2,)),
            DMA((6,)),
            DMA((L,)),
            DMA,
            pltpu.SemaphoreType.REGULAR,
        ]
    )

    def kernel(
        ga_first,
        att_own,
        oterms,
        mix_last,
        att,
        qkv,
        ls,
        x_hbm,
        wq,
        wo,
        cos,
        sin,
        st,
        tok,
        gmix,
        gain,
        gain_in,
        ggu,
        gd,
        fgu,
        fd,
        grad_in,
        out_q,
        out_k,
        out_v,
        out_o,
        layer_last,
        ga_last,
        parts_d,
        parts_gu,
        gain_out,
        *scratch,
    ):
        at = Place(n, H)
        z = at.z
        small, over_batch, over_head, bsend, brecv, hsend, hrecv, local = scratch[s_at]
        gab, land, gat, gq, gk, gv, gqkv, stage, xt, gt, units_buf, ga_sem, t_sem, own_sem, mix_sem, free = scratch[rest]
        sums = {("in", r): SlotReduce(at, *scratch[r_bufs[r]], scratch[r_sems[r]]) for r in range(rows)}
        sums[out] = SlotReduce(at, *scratch[r_bufs[last]], scratch[o_sems])
        late = SlotGather(at, att_own, ga_last, scratch[l_sems])
        asend, arecv = scratch[a_sems]
        units = send_units(at, square, n)
        take_mix = pltpu.make_async_copy(gmix, grad_in, mix_sem)
        take_mix.start()

        def rows_of(r):
            return ga_last if r == last else ga_first.at[r]

        def ga_load(g):
            return pltpu.make_async_copy(
                rows_of(g // blocks).at[pl.ds(g % blocks * 2, 2)], gab.at[g % 2], ga_sem.at[g % 2]
            )

        def own_load(i):
            zd = plan.block(z, i)
            return pltpu.make_async_copy(oterms.at[zd * 2 + at.c], land.at[i % 2], own_sem.at[i])

        def out_exchange(i):
            zd = plan.block(z, i)
            return sums[out].exchange(zd, oterms.at[zd * 2 + 1 - at.c])

        ga_load(0).start()
        ga_load(1).start()
        own_load(0).start()
        own_load(1).start()
        at.greet(all_heads=True)
        late.begin()
        for i in range(L):
            out_exchange(i).start()

        def combine_out(i):
            zd = plan.block(z, i)
            own_load(i).wait()
            out_exchange(i).wait()
            sums[out].combine(zd, land.at[i % 2])
            if i + 2 < L:
                own_load(i + 2).start()

        mlp = [
            LateReduce(at, src, first, parts, scratch[m_bufs[i]], scratch[m_sems[i]])
            for i, (src, first, parts) in enumerate(((gd, fd, parts_d), (ggu, fgu, parts_gu)))
        ]
        for job in mlp:
            job.start()
        small[...] = gain_in[...]
        for job in mlp:
            job.second_step()

        def prob(r):
            gq[...] = jnp.zeros_like(gq)
            gk[...] = jnp.zeros_like(gk)
            gv[...] = jnp.zeros_like(gv)
            if r == last:
                late.finish()
                ga_load(r * blocks).start()
                ga_load(r * blocks + 1).start()
            for b in range(blocks):
                g = r * blocks + b
                ga_load(g).wait()
                gat[b * step : (b + 1) * step, :] = jnp.dot(
                    gab[g % 2].reshape(step, D), wo[...], preferred_element_type=F32
                ).astype(BF16)
                if b + 2 < blocks or (r + 1 < last and g + 2 < rows * blocks):
                    ga_load(g + 2).start()

        def head(r, h):
            attend_back(qkv.at[r], st.at[r], ls.at[r], gat, gq, gk, gv, h, W)

        def terms(r, i):
            zd = plan.block(z, i)
            k = i % 2
            if r == last and i == 0:
                pl.semaphore_wait(free, 1 + jnp.minimum(z, 1) + jnp.minimum(L - 1 - z, 1))
            part = pl.ds(pl.multiple_of(zd * 2 * T, 2 * T), 2 * T)
            c, s = cos[r, part, :], -sin[r, part, :]
            keep = pl.ds(pl.multiple_of(r * S + zd * 2 * T, 2 * T), 2 * T)
            gqkv[keep, 0:W] = rotate(gq[part, :], c, s).astype(BF16)
            gqkv[keep, W : 2 * W] = rotate(gk[part, :], c, s).astype(BF16)
            gqkv[keep, 2 * W : 3 * W] = gv[part, :].astype(BF16)

            @pl.loop(0, D // wide)
            def _(j):
                cols = pl.ds(pl.multiple_of(j * wide, wide), wide)
                back = cols_dot(gqkv[keep, :], wq[cols, :]).astype(BF16)
                stage[k, 0, :, cols] = back[:T]
                stage[k, 1, :, cols] = back[T:]

            sums[("in", r)].exchange(zd, stage.at[k, 1 - at.c]).start()

        def combine_terms(r, i):
            zd = plan.block(z, i)
            job = sums[("in", r)]
            job.exchange(zd, stage.at[i % 2, 1 - at.c]).wait()
            job.combine(zd, stage.at[i % 2, at.c])

        def columns(k):
            cols = pl.ds(pl.multiple_of((units[k][0] * 2 + units[k][1]) * U, U), U)
            return [pltpu.make_async_copy(x_hbm.at[:, cols], xt.at[k % 2], t_sem.at[k % 2])] + [
                pltpu.make_async_copy(rows_of(r).at[:, :, cols], gt.at[k % 2, r], t_sem.at[2 + k % 2])
                for r in range(rows)
            ]

        def columns_wait(k):
            pltpu.make_async_copy(xt.at[k % 2], xt.at[k % 2], t_sem.at[k % 2]).wait()
            pltpu.make_async_copy(gt.at[k % 2], gt.at[k % 2], t_sem.at[2 + k % 2]).wait()

        def grad(k):
            if k == 0:
                for job in columns(0):
                    job.start()
            columns_wait(k)
            if k + 1 < 2 * n:
                for job in columns(k + 1):
                    job.start()
            units_buf[k, :, 0 : 3 * W] = rows_dot(xt[k % 2], gqkv[...]).astype(BF16)
            units_buf[k, :, 3 * W : 4 * W] = rows_dot(gt[k % 2].reshape(rows * S, U), att[...].reshape(rows * S, W)).astype(BF16)
            if units[k][3] is not None:
                unit_send(k).start()

        if square:
            a_first, a_second = scratch[a_bufs]

            def unit_send(k):
                _, _, slot, to = units[k]
                return remote(units_buf.at[k], a_first.at[slot], asend.at[k], arecv.at[slot], {"batch": to})

            def unit_pass(j):
                to = at.xn if j else at.yn
                return remote(units_buf.at[4 + j], a_second.at[j], asend.at[4 + j], arecv.at[4 + j], {"batch": to})

            def unit_second():
                for j, k, slot in ((0, 0, 1 - at.y), (1, 1, 3 - at.x)):
                    unit_send(k).wait_recv()

                    def add(part, j=j, slot=slot):
                        units_buf[4 + j, part, :] = (
                            units_buf[4 + j, part, :].astype(F32) + a_first[slot, part, :].astype(F32)
                        ).astype(BF16)

                    chunk_loop(U, 16, add)
                    unit_pass(j).start()

            def unit_final(put):
                for j, k, slot in ((0, 2, at.y), (1, 3, 2 + at.x)):
                    unit_send(k).wait_recv()
                    unit_pass(j).wait_recv()

                    @pl.loop(0, U // 16)
                    def _(i, j=j, slot=slot):
                        r = pl.multiple_of(i * 16, 16)
                        part = pl.ds(r, 16)
                        put(
                            pl.ds(r + j * U, 16),
                            units_buf[6 + j, part, :].astype(F32)
                            + a_first[slot, part, :].astype(F32)
                            + a_second[j, part, :].astype(F32),
                        )

                for k in range(4):
                    unit_send(k).wait_send()
                for j in (0, 1):
                    unit_pass(j).wait_send()

        else:
            (a_slots,) = scratch[a_bufs]

            def unit_direct(off):
                to = (at.b + off) % n
                return remote(
                    units_buf.at[pl.ds(2 * to, 2)], a_slots.at[off], asend.at[off], arecv.at[off], {"batch": to}
                )

            def unit_second():
                for off in range(1, n):
                    unit_direct(off).start()

            def unit_final(put):
                for off in range(1, n):
                    unit_direct(off).wait()
                for j in (0, 1):

                    @pl.loop(0, U // 16)
                    def _(i, j=j):
                        r = pl.multiple_of(i * 16, 16)
                        part = pl.ds(r, 16)
                        total = units_buf[2 * at.b + j, part, :].astype(F32)
                        for off in range(1, n):
                            total = total + a_slots[off, j, part, :].astype(F32)
                        put(pl.ds(r + j * U, 16), total)

        def finish(j):
            r = j[1]
            if j == out:

                def put_layer(part, value):
                    layer_last[part, :] = (mix_last[part, :] + value).astype(BF16)

                sums[j].final(put_layer)
                sums[j].sent()
                pl.semaphore_signal(free, inc=1, device_id={"head": at.sib}, device_id_type=MESH)

                @pl.when(z > 0)
                def _():
                    pl.semaphore_signal(free, inc=1, device_id={"head": at.down}, device_id_type=MESH)

                @pl.when(z < L - 1)
                def _():
                    pl.semaphore_signal(free, inc=1, device_id={"head": at.up}, device_id_type=MESH)

                return

            def put(part, value):
                back, gain_part = norm_back_part(tok[r, part, :].astype(F32), gain[0:1, :], value)
                grad_in[r, part, :] += back
                small[0:1, :] += gain_part

            sums[j].final(put)
            sums[j].sent()

        def task(name):
            kind, r, i = name
            if kind == "prob":
                prob(r)
                if r == 0:
                    take_mix.wait()
            elif kind == "heads":
                pl.loop(0, heads)(lambda h: head(r, h))
            elif kind == "head":
                head(r, i)
            elif kind == "terms":
                terms(r, i)
            else:
                grad(2 * r)
                grad(2 * r + 1)

        grads_at = min(s for s, task in plan.tasks.items() if task[0][0] == "grad")

        def after(s):
            name = plan.tasks[s - 1][0] if s - 1 in plan.tasks else None
            if s + 1 < L:
                combine_out(s + 1)
            if name and name[0] == "terms":
                combine_terms(*name[1:])
            if s == grads_at + n - 1:
                unit_second()

        combine_out(0)
        run_plan(plan, at, {**sums, gather: late}, task, after, finish)

        def slice_of(b):
            return small.at[:, pl.ds(pl.multiple_of(b * R, R), R)]

        def batch_job(off):
            to = (at.b + off) % n
            return remote(slice_of(to), over_batch.at[off], bsend.at[off], brecv.at[off], {"batch": to})

        for off in range(1, n):
            batch_job(off).start()
        mine = pltpu.make_async_copy(slice_of(at.b), over_batch.at[0], local)
        mine.start()
        mine.wait()
        total = over_batch[0]
        for off in range(1, n):
            batch_job(off).wait_recv()
            total = total + over_batch[off]
        over_head[at.h] = total

        def head_job(off, block):
            to = (at.h + off) % H
            return remote(over_head.at[block], over_head.at[block], hsend.at[off], hrecv.at[off], {"head": to})

        for off in range(1, H):
            head_job(off, at.h).start()

        def put_units(part, value):
            out_q[part, :] = value[:, :W]
            out_k[part, :] = value[:, W : 2 * W]
            out_v[part, :] = value[:, 2 * W : 3 * W]
            out_o[part, :] = value[:, 3 * W :]

        unit_final(put_units)
        for off in range(1, H):
            head_job(off, (at.h + H - off) % H).wait_recv()
        total = over_head[0]
        for h in range(1, H):
            total = total + over_head[h]
        gain_out[...] = total
        for off in range(1, n):
            batch_job(off).wait_send()
        for off in range(1, H):
            head_job(off, at.h).wait_send()
        for job in mlp:
            job.finish()

    weight = jax.ShapeDtypeStruct((R, W), F32)
    return pl.pallas_call(
        kernel,
        out_shape=(
            jax.ShapeDtypeStruct((rows, T, D), F32),
            weight,
            weight,
            weight,
            weight,
            jax.ShapeDtypeStruct((T, D), BF16),
            jax.ShapeDtypeStruct((H, T, D), BF16),
            jax.ShapeDtypeStruct((P, R, ff), BF16),
            jax.ShapeDtypeStruct((P, R, 2 * ff), BF16),
            jax.ShapeDtypeStruct((8, R), F32),
        ),
        in_specs=[ANY, VMEM, ANY, VMEM] + [VMEM] * 3 + [ANY] + [VMEM] * 6 + [ANY, VMEM, VMEM] + [ANY] * 4,
        out_specs=(VMEM,) * 6 + (ANY,) * 3 + (VMEM,),
        scratch_shapes=names.shapes,
        compiler_params=pltpu.CompilerParams(collective_id=4, has_side_effects=True, vmem_limit_bytes=BACK_LIMIT),
        name="attention_back",
    )(
        g_att,
        att_last,
        out_terms,
        mixed_last,
        attended,
        qkv,
        lse,
        attn_in,
        w_qkv,
        w_o,
        cosine,
        sine,
        starts,
        tokens,
        g_mixed,
        gains,
        gain_sum,
        g_gu,
        g_d,
        first_gu,
        first_d,
    )


def rows_dot(left, right):
    return lax.dot_general(left, right, (((0,), (0,)), ((), ())), preferred_element_type=F32)


def cols_dot(left, right):
    return lax.dot_general(left, right, (((1,), (1,)), ((), ())), preferred_element_type=F32)


QUERIES = 256


def rotate(values, cosine, sine):
    half_dim = HEAD_DIM // 2
    parts = []
    for g in range(values.shape[1] // 128):
        part = values[:, g * 128 : (g + 1) * 128]
        lane = lax.broadcasted_iota(jnp.int32, part.shape, 1)
        swapped = jnp.where(
            lane % HEAD_DIM < half_dim, pltpu.roll(part, 128 - half_dim, 1), pltpu.roll(part, half_dim, 1)
        )
        parts.append(part * cosine + swapped * sine)
    return jnp.concatenate(parts, axis=1) if len(parts) > 1 else parts[0]


def only_head(values, h):
    lane = lax.broadcasted_iota(jnp.int32, values.shape, 1)
    return jnp.where(lane // HEAD_DIM == h, values, jnp.zeros_like(values))


def masked_scores(keys, query, starts, first):
    scores = cols_dot(keys, query)
    key_index = lax.broadcasted_iota(jnp.int32, scores.shape, 0)
    query_index = lax.broadcasted_iota(jnp.int32, scores.shape, 1) + first
    return jnp.where((key_index >= starts) & (key_index <= query_index), scores, masked_value)


def attend(qkv, starts, lse, attended, h, W):
    S = qkv.shape[0]
    scale = HEAD_DIM**-0.5
    block = min(QUERIES, S)
    for i in range(S // block):
        rows = pl.ds(i * block, block)
        width = (i + 1) * block
        query = only_head(qkv[rows, 0:W], h) * jnp.asarray(scale, BF16)
        scores = masked_scores(qkv[0:width, W : 2 * W], query, starts[:, rows], i * block)
        top = jnp.max(scores, axis=0, keepdims=True)
        weights = jnp.exp(scores - top)
        total = jnp.sum(weights, axis=0, keepdims=True)
        lse[pl.ds(h, 1), rows] = top + jnp.log(total)
        probs = (weights * (1.0 / total)).astype(BF16)
        out = rows_dot(probs, qkv[0:width, 2 * W : 3 * W]).astype(BF16)
        lane = lax.broadcasted_iota(jnp.int32, out.shape, 1)
        attended[rows, :] = jnp.where(lane // HEAD_DIM == h, out, attended[rows, :])


def attend_back(qkv, starts, lse, grad, g_query, g_key, g_value, h, W):
    S = qkv.shape[0]
    scale = HEAD_DIM**-0.5
    block = min(QUERIES, S)
    for i in range(S // block):
        rows = pl.ds(i * block, block)
        width = (i + 1) * block
        query = only_head(qkv[rows, 0:W], h) * jnp.asarray(scale, BF16)
        keys = qkv[0:width, W : 2 * W]
        scores = masked_scores(keys, query, starts[:, rows], i * block)
        probs = jnp.exp(scores - lse[pl.ds(h, 1), rows])
        back = only_head(grad[rows, :], h)
        g_prob = cols_dot(qkv[0:width, 2 * W : 3 * W], back)
        delta = jnp.sum(probs * g_prob, axis=0, keepdims=True)
        g_score = (probs * (g_prob - delta)).astype(BF16)
        g_value[0:width, :] += jnp.dot(probs.astype(BF16), back, preferred_element_type=F32)
        g_key[0:width, :] += jnp.dot(g_score, query, preferred_element_type=F32)
        g_query[rows, :] += only_head(rows_dot(g_score, keys) * scale, h)


def hand_out(layer_first, layer_last, arrays, grad_d, grad_gu, parts_d, parts_gu):
    _, R, ff = grad_d.shape
    P = parts_d.shape[0]
    lead, T, D = layer_first.shape
    count = len(arrays)

    def kernel(*refs):
        first_in, last_in = refs[:2]
        plain = refs[2 : 2 + count]
        gd, ggu, pd, pgu = refs[2 + count : 6 + count]
        outs = refs[6 + count : 10 + 2 * count]
        held = refs[10 + 2 * count : 10 + 3 * count]
        layer, own_d, own_gu, more_d, more_gu, sum_d, sum_g, sum_u, sem, out_sem = refs[10 + 3 * count :]
        b = lax.axis_index("batch")
        take = [
            pltpu.make_async_copy(gd.at[b], own_d, sem.at[0]),
            pltpu.make_async_copy(pd, more_d, sem.at[1]),
            pltpu.make_async_copy(ggu.at[b], own_gu, sem.at[2]),
            pltpu.make_async_copy(pgu, more_gu, sem.at[3]),
            pltpu.make_async_copy(first_in, layer.at[pl.ds(0, lead)], sem.at[4]),
            pltpu.make_async_copy(last_in, layer.at[lead], sem.at[5]),
        ] + [pltpu.make_async_copy(plain[i], held[i], sem.at[6 + i]) for i in range(count)]
        sources = [layer, *held, sum_g, sum_u, sum_d]
        give = [pltpu.make_async_copy(src, dst, out_sem.at[i]) for i, (src, dst) in enumerate(zip(sources, outs))]
        for job in take:
            job.start()

        def total(own, more, rows):
            value = own[rows, :].astype(F32)
            for p in range(P):
                value = value + more[p, rows, :].astype(F32)
            return value

        take[0].wait()
        take[1].wait()

        def down(rows):
            sum_d[rows, :] = total(own_d, more_d, rows)

        chunk_loop(R, 16, down)
        give[3 + count].start()
        take[2].wait()
        take[3].wait()

        def gate_up(rows):
            value = total(own_gu, more_gu, rows)
            sum_g[rows, :] = value[:, :ff]
            sum_u[rows, :] = value[:, ff:]

        chunk_loop(R, 16, gate_up)
        give[1 + count].start()
        give[2 + count].start()
        take[4].wait()
        take[5].wait()
        give[0].start()
        for i in range(count):
            take[6 + i].wait()
            give[1 + i].start()
        for job in give:
            job.wait()

    wide = jax.ShapeDtypeStruct((R, ff), F32)
    return pl.pallas_call(
        kernel,
        out_shape=(
            jax.ShapeDtypeStruct((lead + 1, T, D), BF16),
            *(jax.ShapeDtypeStruct(a.shape, a.dtype) for a in arrays),
            wide,
            wide,
            wide,
        ),
        in_specs=[ANY] * (6 + count),
        out_specs=(ANY,) * (4 + count),
        scratch_shapes=[pltpu.VMEM(a.shape, a.dtype) for a in arrays]
        + [
            pltpu.VMEM((lead + 1, T, D), BF16),
            pltpu.VMEM((R, ff), BF16),
            pltpu.VMEM((R, 2 * ff), BF16),
            pltpu.VMEM((P, R, ff), BF16),
            pltpu.VMEM((P, R, 2 * ff), BF16),
            pltpu.VMEM((R, ff), F32),
            pltpu.VMEM((R, ff), F32),
            pltpu.VMEM((R, ff), F32),
            DMA((6 + count,)),
            DMA((4 + count,)),
        ],
        compiler_params=pltpu.CompilerParams(vmem_limit_bytes=VMEM_LIMIT),
        name="hand_out",
    )(layer_first, layer_last, *arrays, grad_d, grad_gu, parts_d, parts_gu)


def per_device(
    n,
    H,
    tokens,
    segment_ids,
    position_ids,
    w_query,
    w_key,
    w_value,
    w_output,
    w_gate,
    w_up,
    w_down,
    attn_gain,
    mlp_gain,
    cotangent,
):
    rows, T, D = tokens.shape
    S = T * H
    R, hw = w_query.shape
    ff = w_gate.shape[1]
    shard_gains = jnp.concatenate(
        [attn_gain.astype(F32)[None], mlp_gain.astype(F32)[None], jnp.zeros((6, R), F32)], axis=0
    )
    half_dim = HEAD_DIM // 2
    frequencies = jnp.asarray(
        np.tile(rope_base ** (-(np.arange(half_dim) * 2.0) / HEAD_DIM), 4).astype(np.float32)[None]
    )
    (
        attn_in,
        ct_first,
        w_qkv,
        w_o,
        w_gu,
        terms,
        gains,
        qkv,
        lse,
        attended,
        mixed_first,
        mid_first,
        cosine,
        sine,
        starts,
    ) = attention_in(
        n,
        H,
        tokens,
        cotangent,
        shard_gains,
        (w_query, w_key, w_value, w_output, w_gate, w_up),
        position_ids,
        frequencies,
    )
    w_qkv = w_qkv.reshape(D, 3 * hw)
    w_o = w_o.reshape(D, hw)
    w_gu = w_gu.reshape(D, 2 * ff)
    (
        _,
        _,
        g_att,
        _,
        _,
        grad_gu,
        grad_d,
        first_gu,
        first_d,
        out_terms,
        g_mixed,
        layer_first,
        mixed_last,
        att_last,
        gain_sum,
    ) = feed_forward(n, H, terms, ct_first, mixed_first, mid_first, tokens, cotangent, gains, w_gu, w_down)
    grad_input, grad_q, grad_k, grad_v, grad_o, layer_last, _, parts_d, parts_gu, gain_grads = attention_back(
        n,
        H,
        g_att,
        att_last,
        out_terms,
        mixed_last,
        attended,
        qkv,
        lse,
        attn_in.reshape(rows * S, D),
        w_qkv,
        w_o,
        cosine,
        sine,
        starts,
        tokens,
        g_mixed,
        gains,
        gain_sum,
        grad_gu,
        grad_d,
        first_gu,
        first_d,
    )
    results = hand_out(
        layer_first, layer_last, (grad_input, grad_q, grad_k, grad_v, grad_o), grad_d, grad_gu, parts_d, parts_gu
    )
    return (*results, gain_grads[0], gain_grads[1])


def solution(mesh):
    row = P("batch", "head", None)
    ids = P("batch", None)
    weight = P("batch", "head")
    gain = P("batch")
    return jax.shard_map(
        functools.partial(per_device, mesh.shape["batch"], mesh.shape["head"]),
        mesh=mesh,
        in_specs=(row, ids, ids) + (weight,) * 7 + (gain, gain, row),
        out_specs=(row, row) + (weight,) * 7 + (gain, gain),
        check_vma=False,
    )
```
